32 devices in a mesh: heads: 4 (over y, x), tok: 8 (over z, core).
Axes of the slice: x: 2, y: 2, z: 4, core: 2. Of those that a mesh axis runs over, the one named last changes fastest.
Arguments:
- queries: bfloat16 [8, 8, 8, 1024], P('tok', None, None, 'heads'), may hold values from -12 to 12
- key_rows: bfloat16 [8, 8, 8, 1024], P('tok', None, None, 'heads'), may hold values from -6 to 6
- value_rows: bfloat16 [8, 8, 8, 1024], P('tok', None, None, 'heads'), may hold values from -6 to 6
- residual: bfloat16 [8, 8, 8, 1024], P('heads', 'tok'), may hold values from -3 to 3
- w_out: bfloat16 [1024, 1024], P('heads'), may hold values from -0.375 to 0.375
- w_neck: bfloat16 [1024, 256], replicated, may hold values from -0.1875 to 0.1875
- w_first: bfloat16 [3, 3, 3, 256, 256], replicated, may hold values from -0.109375 to 0.109375
- w_second: bfloat16 [3, 3, 3, 256, 256], replicated, may hold values from -0.109375 to 0.109375
- w_class: bfloat16 [256], replicated, may hold values from -0.5 to 0.5
- labels: int32 [8, 8, 8], P('heads', None, 'tok'), may hold values from 0 to 1, as said below
Outputs:
- encoded: bfloat16 [8, 8, 8, 1024], P('heads', 'tok')
- dice_loss: float32 [], replicated
- grad_encoded: bfloat16 [8, 8, 8, 1024], P('heads', 'tok')
The draws below stay inside these ranges and needn't reach their ends.
Inputs may be any that keep to these rules, and one draw needn't show every extreme that they name: `labels`: 1 marks a fault cell.
All inputs are finite; a program needn't handle non-finite values.
Results may differ from the reference program's by a relative error of at most 0.025.
Values may be sent and summed in bfloat16 or wider, within the bound.
No kernel may reach another device: no remote copies, remote signals or barrier semaphores. Data moves between devices by JAX's collectives and lax.ppermute only.
A program may use at most 128 MiB of HBM per device.

```python
import jax
import jax.numpy as jnp
from jax import lax

D = 1024
HEADS = 16
HD = 64
C = 256
NC = 8
NT = 8
NI = 8
TOKENS = 512


def query_key_pair(key):
    base = jax.random.fold_in(key, 4242)
    key_query, key_keys = jax.random.split(base, 2)
    width = HEADS * HD
    query_draw = jnp.clip(2.5 * jax.random.normal(key_query, (TOKENS, width), jnp.float32), -12.0, 12.0)
    keys_draw = jnp.clip(jax.random.normal(key_keys, (TOKENS, width), jnp.float32), -6.0, 6.0)
    return (query_draw.reshape(NT, NC, NI, width), keys_draw.reshape(NT, NC, NI, width))


def draw_queries(key, part):
    return query_key_pair(key)[0].astype(jnp.bfloat16)


def draw_key_rows(key, part):
    return query_key_pair(key)[1].astype(jnp.bfloat16)


def draw_labels(key, part):
    cross_pos = jnp.arange(NC, dtype=jnp.int32)[:, None, None]
    inline_pos = jnp.arange(NI, dtype=jnp.int32)[None, None, :]
    span_inline = max(NI - 1, 1)
    span_cross = max(NC - 1, 1)
    threshold = 60 * (span_inline + 2 * inline_pos) * (span_cross + 2 * cross_pos) // (span_inline * span_cross)
    uniform_ints = jax.random.randint(jax.random.fold_in(key, 777), (NC, NT, NI), 0, 1000, dtype=jnp.int32)
    return (uniform_ints < threshold).astype(jnp.int32)


def steps_of(rng, shape, pieces, smallest, top_value):
    def one(dim, parts):
        draws = jax.random.uniform(jax.random.fold_in(jax.random.fold_in(rng, 6), dim), (parts,), jnp.float32, smallest / len(pieces), top_value / len(pieces))
        return jnp.repeat(jnp.exp(draws), shape[dim] // parts).reshape((-1,) + (1,) * (len(shape) - dim - 1))

    factor_of = one(*pieces[0])
    for cut in pieces[1:]:
        factor_of = factor_of * one(*cut)
    return factor_of


def gaussian(own_key, shape, scale, bound, shards=(), held_as=jnp.bfloat16):
    result = jax.random.normal(own_key, shape, jnp.float32) * scale
    if len(shards) > 0:
        result = steps_of(own_key, shape, shards, -0.22, 0.18) * result
    return jnp.clip(result, min=-bound, max=bound).astype(held_as)


def setup_inputs(seed: int = 0) -> dict:
    arg_keys = jax.random.split(jax.random.key(seed), 11)
    return {
        "queries": draw_queries(jax.random.fold_in(arg_keys[10], 71), 0),
        "key_rows": draw_key_rows(jax.random.fold_in(arg_keys[10], 71), 0),
        "value_rows": gaussian(arg_keys[2], (NT, NC, NI, HEADS * HD), 1.0, 6.0, ((0, 8), (3, 4))),
        "residual": gaussian(arg_keys[3], (NC, NT, NI, D), 0.5, 3.0, ((0, 4), (1, 8))),
        "w_out": gaussian(arg_keys[4], (HEADS * HD, D), (HEADS * HD // 4) ** -0.5, 0.375, ((0, 4),)),
        "w_neck": gaussian(arg_keys[5], (D, C), D ** -0.5, 0.1875),
        "w_first": gaussian(arg_keys[6], (3, 3, 3, C, C), (27 * C // 2) ** -0.5, 0.109375),
        "w_second": gaussian(arg_keys[7], (3, 3, 3, C, C), (27 * C // 2) ** -0.5, 0.109375),
        "w_class": gaussian(arg_keys[8], (C,), (C // 2) ** -0.5, 0.5),
        "labels": draw_labels(jax.random.fold_in(arg_keys[10], 71), 0),
    }


OFFSETS = [(along_c, along_t, along_x) for along_c in range(3) for along_t in range(3) for along_x in range(3)]
LOSS_SCALE = 64.0


def silu_slope(volume):
    sigma = jax.nn.sigmoid(volume)
    return sigma * (1.0 + volume * (1.0 - sigma))


def conv_apply(volume, weights, flipped):
    padded = jnp.pad(volume, ((1, 1), (1, 1), (1, 1), (0, 0)))
    extent = volume.shape
    outputs = jnp.zeros(extent[:3] + (weights.shape[3],), jnp.float32)
    for (along_c, along_t, along_x) in OFFSETS:
        if flipped:
            anchor = (2 - along_c, 2 - along_t, 2 - along_x)
            matrix = jnp.transpose(weights[along_c, along_t, along_x])
        else:
            anchor = (along_c, along_t, along_x)
            matrix = weights[along_c, along_t, along_x]
        window = padded[anchor[0]:anchor[0] + extent[0], anchor[1]:anchor[1] + extent[1], anchor[2]:anchor[2] + extent[2]]
        product = jnp.dot(window.reshape(-1, extent[3]), matrix, preferred_element_type=jnp.float32)
        outputs = outputs + product.reshape(outputs.shape)
    return outputs


def attend_block(query_block, keys_wide, values_wide):
    scores = jnp.einsum('qhd,khd->hqk', query_block.astype(jnp.float32), keys_wide) * (HD ** -0.5)
    row_peak = jnp.max(scores, axis=-1, keepdims=True)
    raw_weights = jnp.exp(scores - row_peak)
    totals = jnp.sum(raw_weights, axis=-1)
    mixing = raw_weights.astype(jnp.bfloat16)
    mixed = jnp.einsum('hqk,khd->qhd', mixing.astype(jnp.float32), values_wide)
    return (mixed / jnp.transpose(totals)[:, :, None]).astype(jnp.bfloat16)


def reference(queries, key_rows, value_rows, residual, w_out, w_neck, w_first, w_second, w_class, labels):
    width = HEADS * HD
    keys_wide = key_rows.reshape(TOKENS, HEADS, HD).astype(jnp.float32)
    values_wide = value_rows.reshape(TOKENS, HEADS, HD).astype(jnp.float32)
    block_rows = 256 if TOKENS % 256 == 0 else TOKENS
    query_blocks = queries.reshape(TOKENS // block_rows, block_rows, HEADS, HD)
    attended = lax.map(lambda query_block: attend_block(query_block, keys_wide, values_wide), query_blocks)
    attended = attended.reshape(NT, NC, NI, width)
    attention_out = jnp.einsum('tzxe,ed->ztxd', attended.astype(jnp.float32), w_out.astype(jnp.float32))
    encoded = (residual.astype(jnp.float32) + attention_out).astype(jnp.bfloat16)
    neck_feats = jnp.einsum('ztxd,dc->ztxc', encoded.astype(jnp.float32), w_neck.astype(jnp.float32)).astype(jnp.bfloat16)
    hidden_one = conv_apply(neck_feats, w_first, False)
    active_one = jax.nn.silu(hidden_one).astype(jnp.bfloat16)
    hidden_two = conv_apply(active_one, w_second, False)
    active_two = jax.nn.silu(hidden_two).astype(jnp.bfloat16)
    logits = jnp.einsum('ztxc,c->ztx', active_two.astype(jnp.float32), w_class.astype(jnp.float32))
    probability = jax.nn.sigmoid(logits)
    fault_mask = labels.astype(jnp.float32)
    intersection = jnp.sum(probability * fault_mask)
    dice_denominator = jnp.sum(probability) + jnp.sum(fault_mask)
    dice_loss = 1.0 - 2.0 * intersection / dice_denominator
    grad_logits = LOSS_SCALE * TOKENS * (-2.0) * (fault_mask * dice_denominator - intersection) / (dice_denominator * dice_denominator) * probability * (1.0 - probability)
    grad_hidden_two = (grad_logits[..., None] * w_class.astype(jnp.float32) * silu_slope(hidden_two)).astype(jnp.bfloat16)
    grad_active_one = conv_apply(grad_hidden_two, w_second, True)
    grad_hidden_one = (grad_active_one * silu_slope(hidden_one)).astype(jnp.bfloat16)
    grad_neck = conv_apply(grad_hidden_one, w_first, True).astype(jnp.bfloat16)
    grad_encoded = jnp.einsum('ztxc,dc->ztxd', grad_neck.astype(jnp.float32), w_neck.astype(jnp.float32)).astype(jnp.bfloat16)
    return (encoded, dice_loss, grad_encoded)
```

```python
import functools

import jax
import jax.numpy as jnp
from jax import lax
from jax.experimental import pallas as pl
from jax.experimental.pallas import tpu as pltpu
from jax.sharding import PartitionSpec as P

HD = 64
F32 = jnp.float32
BF16 = jnp.bfloat16


OFFSETS = [
    (along_c, along_t, along_x)
    for along_c in range(3)
    for along_t in range(3)
    for along_x in range(3)
]
LOSS_SCALE = 64.0
NEG_LARGE = -1e30


def padded_2(value, sides, width):
    for axis, dim in sides:
        size, length = (lax.axis_size(axis), value.shape[dim])
        up = [(i, (i + 1) % size) for i in range(size - 1)]
        down = [(j, i) for i, j in up]
        last = lax.slice_in_dim(value, length - width, length, axis=dim)
        first = lax.slice_in_dim(value, 0, width, axis=dim)
        before = lax.ppermute(last, axis, up)
        after = lax.ppermute(first, axis, down)
        value = jnp.concatenate([before, value, after], axis=dim)
    return value


def silu_slope(volume):
    sigma = jax.nn.sigmoid(volume)
    return sigma * (1.0 + volume * (1.0 - sigma))


def with_rims(volume):
    padded = padded_2(volume, (("heads", 0), ("tok", 2)), 1)
    return jnp.pad(padded, ((0, 0), (1, 1), (0, 0), (0, 0)))


def conv_apply(volume, weights, flipped):
    extent = volume.shape[:3]
    padded = with_rims(volume)
    pieces = []
    for along_c, along_t, along_x in OFFSETS:
        if flipped:
            anchor = (2 - along_c, 2 - along_t, 2 - along_x)
        else:
            anchor = (along_c, along_t, along_x)
        pieces.append(
            padded[
                anchor[0] : anchor[0] + extent[0],
                anchor[1] : anchor[1] + extent[1],
                anchor[2] : anchor[2] + extent[2],
            ]
        )
    stacked = jnp.stack(pieces, axis=3)
    columns = stacked.reshape(extent[0] * extent[1] * extent[2], 27, volume.shape[3])
    kernel = weights.reshape(27, weights.shape[3], weights.shape[4])
    if flipped:
        contraction = (((1, 2), (0, 2)), ((), ()))
    else:
        contraction = (((1, 2), (0, 1)), ((), ()))
    return lax.dot_general(columns, kernel, contraction, preferred_element_type=jnp.float32)


def online_step(carried, query_block, key_block, value_block, scale):
    row_peak, totals, weighted_sum = carried
    scores = (
        jnp.einsum("qhd,khd->qhk", query_block, key_block, preferred_element_type=jnp.float32)
        * scale
    )
    new_peak = jnp.maximum(row_peak, jnp.max(scores, axis=-1))
    factor = jnp.exp(row_peak - new_peak)
    raw_weights = jnp.exp(scores - new_peak[:, :, None])
    totals = totals * factor + jnp.sum(raw_weights, axis=-1)
    weighted_sum = weighted_sum * factor[:, :, None] + jnp.einsum(
        "qhk,khd->qhd",
        raw_weights.astype(jnp.bfloat16),
        value_block,
        preferred_element_type=jnp.float32,
    )
    return (new_peak, totals, weighted_sum)


def on_tiles(
    queries, key_rows, value_rows, residual, w_out, w_neck, w_first, w_second, w_class, labels
):
    width_here = queries.shape[-1]
    heads_here = width_here // HD
    scale = HD ** (-0.5)
    local_queries = queries.reshape(-1, heads_here, HD)
    query_total = local_queries.shape[0]
    start_state = (
        jnp.full((query_total, heads_here), NEG_LARGE, jnp.float32),
        jnp.zeros((query_total, heads_here), jnp.float32),
        jnp.zeros((query_total, heads_here, HD), jnp.float32),
    )

    def fold_keys(carried, key_piece):
        key_flat = key_piece[0].reshape(-1, heads_here, HD)
        value_flat = key_piece[1].reshape(-1, heads_here, HD)
        key_total = key_flat.shape[0]
        if key_total > 512 and key_total % 512 == 0:
            key_blocks = key_flat.reshape(key_total // 512, 512, heads_here, HD)
            value_blocks = value_flat.reshape(key_total // 512, 512, heads_here, HD)

            def scan_step(inner, paired):
                return (online_step(inner, local_queries, paired[0], paired[1], scale), None)

            return lax.scan(scan_step, carried, (key_blocks, value_blocks))[0]
        return online_step(carried, local_queries, key_flat, value_flat, scale)

    row_peak, totals, weighted_sum = fold_keys(
        start_state,
        (
            lax.all_gather(key_rows, "tok", axis=0, tiled=True),
            lax.all_gather(value_rows, "tok", axis=0, tiled=True),
        ),
    )
    attended = (weighted_sum / totals[:, :, None]).astype(jnp.bfloat16)
    attended_grid = attended.reshape(queries.shape)
    owned = lax.all_to_all(attended_grid, "heads", split_axis=1, concat_axis=3, tiled=True)
    attention_out = jnp.einsum(
        "tzxe,ed->ztxd",
        owned,
        lax.all_gather(w_out, "heads", axis=0, tiled=True),
        preferred_element_type=jnp.float32,
    )
    encoded = (residual.astype(jnp.float32) + attention_out).astype(jnp.bfloat16)
    tiled = lax.all_to_all(encoded, "tok", split_axis=2, concat_axis=1, tiled=True)
    neck_feats = jnp.einsum(
        "ztxd,dc->ztxc", tiled, w_neck, preferred_element_type=jnp.float32
    ).astype(jnp.bfloat16)
    extent = neck_feats.shape[:3]
    channels = w_neck.shape[1]
    cell_count = extent[0] * extent[1] * extent[2]
    hidden_one = conv_apply(neck_feats, w_first, False)
    active_one = jax.nn.silu(hidden_one).astype(jnp.bfloat16)
    hidden_two = conv_apply(active_one.reshape(extent + (channels,)), w_second, False)
    active_two = jax.nn.silu(hidden_two).astype(jnp.bfloat16)
    logits = jnp.dot(active_two, w_class, preferred_element_type=jnp.float32)
    probability = jax.nn.sigmoid(logits)
    fault_mask = labels.reshape(cell_count).astype(jnp.float32)
    intersection, total_prob, total_fault = lax.psum(
        (jnp.sum(probability * fault_mask), jnp.sum(probability), jnp.sum(fault_mask)),
        ("heads", "tok"),
    )
    dice_denominator = total_prob + total_fault
    dice_loss = 1.0 - 2.0 * intersection / dice_denominator
    cells_all = float(cell_count * lax.axis_size("heads") * lax.axis_size("tok"))
    grad_logits = (
        LOSS_SCALE
        * cells_all
        * -2.0
        * (fault_mask * dice_denominator - intersection)
        / (dice_denominator * dice_denominator)
        * probability
        * (1.0 - probability)
    )
    grad_hidden_two = (
        grad_logits[:, None] * w_class.astype(jnp.float32)[None, :] * silu_slope(hidden_two)
    ).astype(jnp.bfloat16)
    grad_active_one = conv_apply(grad_hidden_two.reshape(extent + (channels,)), w_second, True)
    grad_hidden_one = (grad_active_one * silu_slope(hidden_one)).astype(jnp.bfloat16)
    grad_neck = (
        conv_apply(grad_hidden_one.reshape(extent + (channels,)), w_first, True)
        .astype(jnp.bfloat16)
        .reshape(extent + (channels,))
    )
    grad_tiles = jnp.einsum(
        "ztxc,dc->ztxd", grad_neck, w_neck, preferred_element_type=jnp.float32
    ).astype(jnp.bfloat16)
    grad_encoded = lax.all_to_all(grad_tiles, "tok", split_axis=1, concat_axis=2, tiled=True)
    return (encoded, dice_loss, grad_encoded)


def dot(a, b):
    return jnp.dot(a, b, preferred_element_type=F32)


def dot_t(a, b):
    return lax.dot_general(a, b, (((1,), (1,)), ((), ())), preferred_element_type=F32)


def sigma_of(v):
    return 1.0 / (1.0 + jnp.exp(-v))


def slope_of(v):
    s = sigma_of(v)
    return s * (1.0 + v * (1.0 - s))


def iota(shape, dim):
    return lax.broadcasted_iota(jnp.int32, shape, dim)


def along_inline(value, step, inline):
    if step == 0:
        return value
    rows = value.shape[0]
    x = iota(value.shape, 0) % inline
    edge = inline - 1 if step > 0 else 0
    return jnp.where(x == edge, 0.0, pltpu.roll(value, (-step) % rows, axis=0))


def along_rows(value, step):
    if step == 0:
        return value
    zeros = jnp.zeros((abs(step), value.shape[1]), value.dtype)
    if step > 0:
        return jnp.concatenate([value[step:], zeros], axis=0)
    return jnp.concatenate([zeros, value[:step]], axis=0)


def pack_kernel(place, q_ref, k_ref, v_ref, r_ref, neck_ref, lab_ref, out_ref):
    rows = q_ref.shape[1] * q_ref.shape[2]
    width = q_ref.shape[3]
    for i, ref in enumerate((q_ref, k_ref, v_ref)):
        flat = ref[...].astype(F32).reshape(rows, width).astype(BF16)
        out_ref[i * rows : (i + 1) * rows, :] = flat
    own = r_ref.shape[0] * r_ref.shape[2]
    residual = r_ref[...].astype(F32).reshape(own, r_ref.shape[3]).astype(BF16)
    out_ref[3 * rows : 3 * rows + own, :] = dot(residual, neck_ref[...]).astype(BF16)
    count = lab_ref.shape[0] * lab_ref.shape[1]
    labels = lab_ref[...].astype(F32).reshape(count, 1)
    out_ref[3 * rows + own :, :] = jnp.where(
        iota((count, width), 1) == place[3], labels, 0.0
    ).astype(BF16)


def attention_kernel(zs, rows, own, *refs):
    place = refs[0]
    ours, theirs = refs[1 : 1 + zs], refs[1 + zs : 1 + 2 * zs]
    out_w, neck_w = refs[1 + 2 * zs : 3 + 2 * zs]
    part_ref = refs[3 + 2 * zs]
    enc_refs = refs[4 + 2 * zs : -4]
    qq, kk, vv, part = refs[-4:]
    z, core, h = place[0], place[1], place[2]
    width = qq.shape[1]
    queries_n, keys_n = qq.shape[0], kk.shape[0]
    labels = jnp.zeros((ours[0].shape[0] - 3 * rows - own, width), F32)
    for d in range(zs):
        qq[d * rows : (d + 1) * rows, :] = ours[d][0:rows, :]
        for ref, side in ((ours[d], core), (theirs[d], 1 - core)):
            at = pl.multiple_of((2 * (z ^ d) + side) * rows, rows)
            kk[pl.ds(at, rows), :] = ref[rows : 2 * rows, :]
            vv[pl.ds(at, rows), :] = ref[2 * rows : 3 * rows, :]
            labels = labels + ref[3 * rows + own :, :].astype(F32)
    heads_here = width // HD
    scale = HD ** (-0.5)
    query = qq[...]
    keys, values = kk[...], vv[...]
    lane_head = iota((queries_n, width), 1) // HD
    attended = jnp.zeros((queries_n, width), F32)
    for head in range(heads_here):
        mine = lane_head == head
        scores = dot_t(jnp.where(mine, query, jnp.zeros_like(query)), keys) * scale
        raw = jnp.exp(scores - jnp.max(scores, axis=1, keepdims=True))
        total = jnp.sum(raw, axis=1, keepdims=True)
        mixed = dot(raw.astype(BF16), values)
        attended = jnp.where(mine, mixed / total, attended)
    product = dot(attended.astype(BF16), out_w[...])
    part[...] = dot(product.astype(BF16), neck_w[...])
    for d in range(zs):
        at = pl.multiple_of(d * rows + h * own, own)
        part[pl.ds(at, own), :] += ours[d][3 * rows : 3 * rows + own, :].astype(F32)
    part_ref[0:queries_n, :] = part[...].astype(BF16)
    part_ref[queries_n:, :] = labels.astype(BF16)
    first = product[0:rows, :]
    blocks = [first[i * own : (i + 1) * own, :] for i in range(rows // own)]
    for d, ref in enumerate(enc_refs):
        picked = blocks[0]
        for i in range(1, len(blocks)):
            picked = jnp.where((h ^ d) == i, blocks[i], picked)
        ref[...] = picked.astype(BF16)


def decoder_kernel(sizes, place, ours, theirs, first_w, second_w, class_w, neck_w, loss_ref, grad_ref, *scratch):
    nc, nt, ni, own_c, zs = sizes
    grid, cols, slope1, grad2, cols3, w1, w2, sems = scratch
    channels = grid.shape[2]
    slab = nt * ni
    rows = nc * ni
    cells = nc * slab
    z, core, h, tslab = place[0], place[1], place[2], place[4]
    taps = 9
    copies = []
    for i, (src, dst) in enumerate(((first_w, w1), (second_w, w2))):
        for a in range(3):
            copies.append(pltpu.make_async_copy(src.at[a], dst.at[a], sems.at[3 * i + a]))
            copies[-1].start()

    for d in range(zs):
        for ref, side in ((ours, core), (theirs, 1 - core)):
            block = ref[d * rows : (d + 1) * rows, :].astype(F32)
            at = pl.multiple_of((2 * (z ^ d) + side) * ni, ni)
            for c in range(nc):
                grid[c, pl.ds(at, ni), :] = block[c * ni : (c + 1) * ni, :]

    slope1[...] = jnp.zeros_like(slope1)
    grad2[...] = jnp.zeros_like(grad2)
    edge = jnp.zeros((slab, taps * channels), BF16)
    cols[0:slab, :] = edge
    cols[(nc + 1) * slab :, :] = edge

    def spread(value, c):
        for e in range(3):
            moved = along_inline(value, e - 1, ni)
            for b in range(3):
                lane = (b * 3 + e) * channels
                cols[(c + 1) * slab : (c + 2) * slab, lane : lane + channels] = along_rows(
                    moved, (b - 1) * ni
                ).astype(BF16)

    def conv(weights, base):
        total = None
        for a in range(3):
            if base is not None:
                copies[base + a].wait()
            matrix = weights[a].reshape(taps * channels, channels)
            term = dot(cols[a * slab : a * slab + cells, :], matrix)
            total = term if total is None else total + term
        return total

    for c in range(nc):
        spread(grid[c], c)
    hidden_one = conv(w1, 0)
    for c in range(nc):
        v = hidden_one[c * slab : (c + 1) * slab, :]
        s = sigma_of(v)
        slope1[c + 1, ni : ni + slab, :] = s * (1.0 + v * (1.0 - s))
        spread((v * s).astype(BF16).astype(F32), c)
    hidden_two = conv(w2, 3)
    sigma_two = sigma_of(hidden_two)
    active_two = (hidden_two * sigma_two).astype(BF16)
    class_row = class_w[...].astype(F32)
    logits = dot_t(active_two, jnp.broadcast_to(class_row, (128, channels)).astype(BF16))
    probability = sigma_of(logits)
    lab_rows = ours.shape[0] - rows * zs
    lab = ours[rows * zs :, 0:128].astype(F32).reshape(own_c, nt, 1, 128)
    spread_lab = jnp.broadcast_to(lab[None], (nc // own_c, own_c, nt, ni, 128)).reshape(cells, 128)
    row = iota((cells, 128), 0)
    wanted = (row // (slab * own_c)) * nt + row % ni
    picked = jnp.where(iota((cells, 128), 1) == wanted, spread_lab, 0.0).astype(BF16)
    mask = dot(picked, jnp.ones((128, 128), BF16))
    intersection = jnp.sum(probability * mask, axis=0, keepdims=True)
    total_prob = jnp.sum(probability, axis=0, keepdims=True)
    total_fault = jnp.sum(mask, axis=0, keepdims=True)
    denominator = total_prob + total_fault
    loss_ref[...] = 1.0 - 2.0 * intersection / denominator
    grad_logits = (
        LOSS_SCALE
        * float(cells)
        * -2.0
        * (mask * denominator - intersection)
        / (denominator * denominator)
        * probability
        * (1.0 - probability)
    )
    wide = jnp.concatenate([grad_logits] * (channels // 128), axis=1)
    slope_two = sigma_two * (1.0 + hidden_two * (1.0 - sigma_two))
    g2 = wide * class_row * slope_two
    for c in range(nc):
        grad2[c + 2, 2 * ni : 2 * ni + slab, :] = g2[c * slab : (c + 1) * slab, :]

    band = 4 * ni
    c0 = h * own_c
    t0 = pl.multiple_of(tslab * ni, ni)
    for i in range(own_c + 4):
        region = grad2[c0 + i, pl.ds(t0, band + 2 * ni), :]
        for e in range(3):
            moved = along_inline(region, 1 - e, ni)
            for b in range(3):
                lane = (b * 3 + e) * channels
                cols3[i * band : (i + 1) * band, lane : lane + channels] = moved[
                    (2 - b) * ni : (2 - b) * ni + band, :
                ].astype(BF16)
    out3 = (own_c + 2) * band
    total = jnp.zeros((out3, channels), F32)
    for a in range(3):
        for b in range(3):
            for e in range(3):
                lane = (b * 3 + e) * channels
                piece = cols3[(2 - a) * band : (2 - a) * band + out3, lane : lane + channels]
                total = total + dot_t(piece, w2[a, b, e])
    slopes = [slope1[c0 + i, pl.ds(t0, band), :] for i in range(own_c + 2)]
    g1 = (total * jnp.concatenate(slopes, axis=0)).astype(BF16).astype(F32)
    shifted = [along_inline(g1, 1 - e, ni) for e in range(3)]
    total = jnp.zeros((own_c * ni, channels), F32)
    for a in range(3):
        for b in range(3):
            for e in range(3):
                cells_in = [
                    shifted[e][(i + 2 - a) * band + (2 - b) * ni : (i + 2 - a) * band + (3 - b) * ni, :]
                    for i in range(own_c)
                ]
                piece = jnp.concatenate(cells_in, axis=0).astype(BF16)
                total = total + dot_t(piece, w1[a, b, e])
    grad = dot_t(total.astype(BF16), neck_w[...])
    grad_ref[...] = grad.reshape(grad_ref.shape).astype(BF16)


def vmem():
    return pl.BlockSpec(memory_space=pltpu.VMEM)


def smem():
    return pl.BlockSpec(memory_space=pltpu.SMEM)


def whole_grid(
    queries, key_rows, value_rows, residual, w_out, w_neck, w_first, w_second, w_class, labels
):
    heads_n, tok_n = lax.axis_size("heads"), lax.axis_size("tok")
    zs = tok_n // 2
    _, nc, ni, width = queries.shape
    own_c = residual.shape[0]
    nt = labels.shape[1]
    channels = w_neck.shape[1]
    rows, own, lab = nc * ni, own_c * ni, own_c * nt
    h, t = lax.axis_index("heads"), lax.axis_index("tok")
    place = jnp.stack([t // 2, t % 2, h, h * tok_n + t, t]).astype(jnp.int32)

    def swap_tok(value, bits):
        return lax.ppermute(value, "tok", [(i, i ^ bits) for i in range(tok_n)])

    def swap_heads(value, bits):
        return lax.ppermute(value, "heads", [(i, i ^ bits) for i in range(heads_n)])

    packed = pl.pallas_call(
        pack_kernel,
        out_shape=jax.ShapeDtypeStruct((3 * rows + own + lab, width), BF16),
        in_specs=[smem()] + [vmem()] * 6,
        out_specs=vmem(),
    )(place, queries, key_rows, value_rows, residual, w_neck, labels)
    ours = [packed] + [swap_tok(packed, 2 * d) for d in range(1, zs)]
    theirs = [swap_tok(value, 1) for value in ours]
    enc_shape = jax.ShapeDtypeStruct((own, residual.shape[3]), BF16)
    queries_n, keys_n = rows * zs, rows * tok_n
    out = pl.pallas_call(
        functools.partial(attention_kernel, zs, rows, own),
        out_shape=[jax.ShapeDtypeStruct((queries_n + lab, channels), BF16)] + [enc_shape] * heads_n,
        in_specs=[smem()] + [vmem()] * (2 * zs + 2),
        out_specs=[vmem()] * (1 + heads_n),
        scratch_shapes=[
            pltpu.VMEM((queries_n, width), BF16),
            pltpu.VMEM((keys_n, width), BF16),
            pltpu.VMEM((keys_n, width), BF16),
            pltpu.VMEM((queries_n, channels), F32),
        ],
        compiler_params=pltpu.CompilerParams(vmem_limit_bytes=32 * 2**20),
    )(place, *ours, *theirs, w_out, w_neck)
    parts = [out[0]] + [swap_heads(out[0], d) for d in range(1, heads_n)]
    pieces = [out[1]] + [swap_heads(out[1 + d], d) for d in range(1, heads_n)]

    def pairwise(values):
        values = [v.astype(F32) for v in values]
        while len(values) > 1:
            values = [values[i] + values[i + 1] for i in range(0, len(values), 2)]
        return values[0]

    half = pairwise(parts).astype(BF16)
    other = swap_tok(half, 1)
    encoded = (residual.astype(F32) + pairwise(pieces).reshape(residual.shape)).astype(BF16)

    slab = nt * ni
    loss, grad = pl.pallas_call(
        functools.partial(decoder_kernel, (nc, nt, ni, own_c, zs)),
        out_shape=[
            jax.ShapeDtypeStruct((1, 128), F32),
            jax.ShapeDtypeStruct(residual.shape, BF16),
        ],
        in_specs=[smem(), vmem(), vmem()]
        + [pl.BlockSpec(memory_space=pl.ANY)] * 2
        + [vmem(), vmem()],
        out_specs=[vmem(), vmem()],
        scratch_shapes=[
            pltpu.VMEM((nc, slab, channels), F32),
            pltpu.VMEM(((nc + 2) * slab, 9 * channels), BF16),
            pltpu.VMEM((nc + 2, (nt + 4) * ni, channels), F32),
            pltpu.VMEM((nc + 4, (nt + 6) * ni, channels), F32),
            pltpu.VMEM(((own_c + 4) * 4 * ni, 9 * channels), BF16),
            pltpu.VMEM(w_first.shape, BF16),
            pltpu.VMEM(w_second.shape, BF16),
            pltpu.SemaphoreType.DMA((6,)),
        ],
        compiler_params=pltpu.CompilerParams(vmem_limit_bytes=40 * 2**20),
    )(place, half, other, w_first, w_second, w_class.reshape(1, channels), w_neck)
    return (encoded, loss[0, 0], grad)


def power_of_two(n):
    return n > 0 and n & (n - 1) == 0


def fits_whole(queries, residual, w_neck, labels):
    heads_n, tok_n = lax.axis_size("heads"), lax.axis_size("tok")
    slabs, nc, ni, width = queries.shape
    nt = labels.shape[1]
    return (
        slabs == 1
        and labels.shape[2] == 1
        and ni == 8
        and nt == tok_n
        and tok_n >= 4
        and power_of_two(tok_n)
        and power_of_two(heads_n)
        and heads_n * tok_n <= 128
        and nc * nt * ni <= 1024
        and width % 128 == 0
        and w_neck.shape[1] == width
        and (residual.shape[0] * ni) % 16 == 0
        and (residual.shape[0] * nt) % 16 == 0
    )


def on_device(*arguments):
    queries, residual, w_neck, labels = (arguments[i] for i in (0, 3, 5, 9))
    if fits_whole(queries, residual, w_neck, labels):
        return whole_grid(*arguments)
    return on_tiles(*arguments)


def solution(mesh):
    placed = (
        P("tok", None, None, "heads"),
        P("tok", None, None, "heads"),
        P("tok", None, None, "heads"),
        P("heads", "tok", None, None),
        P("heads", None),
        P(),
        P(),
        P(),
        P(),
        P("heads", None, "tok"),
    )
    return jax.shard_map(
        on_device,
        mesh=mesh,
        in_specs=placed,
        out_specs=(P("heads", "tok", None, None), P(), P("heads", "tok", None, None)),
        check_vma=False,
    )
```

```python
import functools

import jax
import jax.numpy as jnp
from jax import lax
from jax.experimental import pallas as pl
from jax.experimental.pallas import tpu as pltpu
from jax.sharding import PartitionSpec as P

HD = 64
F32 = jnp.float32
BF16 = jnp.bfloat16
LABEL_ROWS = 16


OFFSETS = [
    (along_c, along_t, along_x)
    for along_c in range(3)
    for along_t in range(3)
    for along_x in range(3)
]
LOSS_SCALE = 64.0
NEG_LARGE = -1e30


def padded_2(value, sides, width):
    for axis, dim in sides:
        size, length = (lax.axis_size(axis), value.shape[dim])
        up = [(i, (i + 1) % size) for i in range(size - 1)]
        down = [(j, i) for i, j in up]
        last = lax.slice_in_dim(value, length - width, length, axis=dim)
        first = lax.slice_in_dim(value, 0, width, axis=dim)
        before = lax.ppermute(last, axis, up)
        after = lax.ppermute(first, axis, down)
        value = jnp.concatenate([before, value, after], axis=dim)
    return value


def silu_slope(volume):
    sigma = jax.nn.sigmoid(volume)
    return sigma * (1.0 + volume * (1.0 - sigma))


def with_rims(volume):
    padded = padded_2(volume, (("heads", 0), ("tok", 2)), 1)
    return jnp.pad(padded, ((0, 0), (1, 1), (0, 0), (0, 0)))


def conv_apply(volume, weights, flipped):
    extent = volume.shape[:3]
    padded = with_rims(volume)
    pieces = []
    for along_c, along_t, along_x in OFFSETS:
        if flipped:
            anchor = (2 - along_c, 2 - along_t, 2 - along_x)
        else:
            anchor = (along_c, along_t, along_x)
        pieces.append(
            padded[
                anchor[0] : anchor[0] + extent[0],
                anchor[1] : anchor[1] + extent[1],
                anchor[2] : anchor[2] + extent[2],
            ]
        )
    stacked = jnp.stack(pieces, axis=3)
    columns = stacked.reshape(extent[0] * extent[1] * extent[2], 27, volume.shape[3])
    kernel = weights.reshape(27, weights.shape[3], weights.shape[4])
    if flipped:
        contraction = (((1, 2), (0, 2)), ((), ()))
    else:
        contraction = (((1, 2), (0, 1)), ((), ()))
    return lax.dot_general(columns, kernel, contraction, preferred_element_type=jnp.float32)


def online_step(carried, query_block, key_block, value_block, scale):
    row_peak, totals, weighted_sum = carried
    scores = (
        jnp.einsum("qhd,khd->qhk", query_block, key_block, preferred_element_type=jnp.float32)
        * scale
    )
    new_peak = jnp.maximum(row_peak, jnp.max(scores, axis=-1))
    factor = jnp.exp(row_peak - new_peak)
    raw_weights = jnp.exp(scores - new_peak[:, :, None])
    totals = totals * factor + jnp.sum(raw_weights, axis=-1)
    weighted_sum = weighted_sum * factor[:, :, None] + jnp.einsum(
        "qhk,khd->qhd",
        raw_weights.astype(jnp.bfloat16),
        value_block,
        preferred_element_type=jnp.float32,
    )
    return (new_peak, totals, weighted_sum)


def on_tiles(
    queries, key_rows, value_rows, residual, w_out, w_neck, w_first, w_second, w_class, labels
):
    width_here = queries.shape[-1]
    heads_here = width_here // HD
    scale = HD ** (-0.5)
    local_queries = queries.reshape(-1, heads_here, HD)
    query_total = local_queries.shape[0]
    start_state = (
        jnp.full((query_total, heads_here), NEG_LARGE, jnp.float32),
        jnp.zeros((query_total, heads_here), jnp.float32),
        jnp.zeros((query_total, heads_here, HD), jnp.float32),
    )

    def fold_keys(carried, key_piece):
        key_flat = key_piece[0].reshape(-1, heads_here, HD)
        value_flat = key_piece[1].reshape(-1, heads_here, HD)
        key_total = key_flat.shape[0]
        if key_total > 512 and key_total % 512 == 0:
            key_blocks = key_flat.reshape(key_total // 512, 512, heads_here, HD)
            value_blocks = value_flat.reshape(key_total // 512, 512, heads_here, HD)

            def scan_step(inner, paired):
                return (online_step(inner, local_queries, paired[0], paired[1], scale), None)

            return lax.scan(scan_step, carried, (key_blocks, value_blocks))[0]
        return online_step(carried, local_queries, key_flat, value_flat, scale)

    row_peak, totals, weighted_sum = fold_keys(
        start_state,
        (
            lax.all_gather(key_rows, "tok", axis=0, tiled=True),
            lax.all_gather(value_rows, "tok", axis=0, tiled=True),
        ),
    )
    attended = (weighted_sum / totals[:, :, None]).astype(jnp.bfloat16)
    attended_grid = attended.reshape(queries.shape)
    owned = lax.all_to_all(attended_grid, "heads", split_axis=1, concat_axis=3, tiled=True)
    attention_out = jnp.einsum(
        "tzxe,ed->ztxd",
        owned,
        lax.all_gather(w_out, "heads", axis=0, tiled=True),
        preferred_element_type=jnp.float32,
    )
    encoded = (residual.astype(jnp.float32) + attention_out).astype(jnp.bfloat16)
    tiled = lax.all_to_all(encoded, "tok", split_axis=2, concat_axis=1, tiled=True)
    neck_feats = jnp.einsum(
        "ztxd,dc->ztxc", tiled, w_neck, preferred_element_type=jnp.float32
    ).astype(jnp.bfloat16)
    extent = neck_feats.shape[:3]
    channels = w_neck.shape[1]
    cell_count = extent[0] * extent[1] * extent[2]
    hidden_one = conv_apply(neck_feats, w_first, False)
    active_one = jax.nn.silu(hidden_one).astype(jnp.bfloat16)
    hidden_two = conv_apply(active_one.reshape(extent + (channels,)), w_second, False)
    active_two = jax.nn.silu(hidden_two).astype(jnp.bfloat16)
    logits = jnp.dot(active_two, w_class, preferred_element_type=jnp.float32)
    probability = jax.nn.sigmoid(logits)
    fault_mask = labels.reshape(cell_count).astype(jnp.float32)
    intersection, total_prob, total_fault = lax.psum(
        (jnp.sum(probability * fault_mask), jnp.sum(probability), jnp.sum(fault_mask)),
        ("heads", "tok"),
    )
    dice_denominator = total_prob + total_fault
    dice_loss = 1.0 - 2.0 * intersection / dice_denominator
    cells_all = float(cell_count * lax.axis_size("heads") * lax.axis_size("tok"))
    grad_logits = (
        LOSS_SCALE
        * cells_all
        * -2.0
        * (fault_mask * dice_denominator - intersection)
        / (dice_denominator * dice_denominator)
        * probability
        * (1.0 - probability)
    )
    grad_hidden_two = (
        grad_logits[:, None] * w_class.astype(jnp.float32)[None, :] * silu_slope(hidden_two)
    ).astype(jnp.bfloat16)
    grad_active_one = conv_apply(grad_hidden_two.reshape(extent + (channels,)), w_second, True)
    grad_hidden_one = (grad_active_one * silu_slope(hidden_one)).astype(jnp.bfloat16)
    grad_neck = (
        conv_apply(grad_hidden_one.reshape(extent + (channels,)), w_first, True)
        .astype(jnp.bfloat16)
        .reshape(extent + (channels,))
    )
    grad_tiles = jnp.einsum(
        "ztxc,dc->ztxd", grad_neck, w_neck, preferred_element_type=jnp.float32
    ).astype(jnp.bfloat16)
    grad_encoded = lax.all_to_all(grad_tiles, "tok", split_axis=1, concat_axis=2, tiled=True)
    return (encoded, dice_loss, grad_encoded)


def dot(a, b):
    return jnp.dot(a, b, preferred_element_type=F32)


def dot_t(a, b):
    return lax.dot_general(a, b, (((1,), (1,)), ((), ())), preferred_element_type=F32)


def sigma_of(v):
    return 1.0 / (1.0 + jnp.exp(-v))


def slope_of(v):
    s = sigma_of(v)
    return s * (1.0 + v * (1.0 - s))


def iota(shape, dim):
    return lax.broadcasted_iota(jnp.int32, shape, dim)


def along_inline(value, step, inline):
    if step == 0:
        return value
    rows = value.shape[0]
    x = iota(value.shape, 0) % inline
    edge = inline - 1 if step > 0 else 0
    return jnp.where(x == edge, 0.0, pltpu.roll(value, (-step) % rows, axis=0))


def along_rows(value, step):
    if step == 0:
        return value
    zeros = jnp.zeros((abs(step), value.shape[1]), value.dtype)
    if step > 0:
        return jnp.concatenate([value[step:], zeros], axis=0)
    return jnp.concatenate([zeros, value[:step]], axis=0)


def place_of(tok_n):
    h, t = lax.axis_index("heads"), lax.axis_index("tok")
    return h, t // 2, t % 2, t


def pack_kernel(tok_n, q_ref, k_ref, v_ref, r_ref, neck_ref, lab_ref, out_ref):
    h, _, _, t = place_of(tok_n)
    rows = q_ref.shape[1] * q_ref.shape[2]
    width = q_ref.shape[3]
    for i, ref in enumerate((q_ref, k_ref, v_ref)):
        flat = ref[...].astype(F32).reshape(rows, width).astype(BF16)
        out_ref[i * rows : (i + 1) * rows, :] = flat
    own = r_ref.shape[0] * r_ref.shape[2]
    residual = r_ref[...].astype(F32).reshape(own, r_ref.shape[3]).astype(BF16)
    out_ref[3 * rows : 3 * rows + own, :] = dot(residual, neck_ref[...]).astype(BF16)
    own_c, _, nt = lab_ref.shape
    spread = jnp.zeros((LABEL_ROWS, width), F32)
    for c in range(own_c):
        row = jnp.broadcast_to(lab_ref[c].astype(F32), (LABEL_ROWS, nt)).astype(BF16)
        at = (h * own_c + c) * nt + iota((nt, width), 0)
        spread = spread + dot(row, (iota((nt, width), 1) == at).astype(F32).astype(BF16))
    out_ref[3 * rows + own :, :] = jnp.where(
        iota((LABEL_ROWS, width), 0) == t, spread, 0.0
    ).astype(BF16)


def weights_kernel(first_ref, second_ref, out_ref, neck_ref, packed_ref, *refs):
    first_in, second_in, first_t, second_t, joint, again, out_w, neck_w, sems = refs
    small = [
        pltpu.make_async_copy(out_ref, out_w, sems.at[6]),
        pltpu.make_async_copy(neck_ref, neck_w, sems.at[7]),
    ]
    for copy in small:
        copy.start()
    copies = []
    for i, (src, dst) in enumerate(((first_ref, first_in), (second_ref, second_in))):
        for a in range(3):
            copies.append(pltpu.make_async_copy(src.at[a], dst.at[a], sems.at[3 * i + a]))
            copies[-1].start()
    again[...] = packed_ref[...]
    for copy in small:
        copy.wait()
    joint[...] = dot(out_w[...], neck_w[...]).astype(BF16)
    for i, (src, dst) in enumerate(((first_in, first_t), (second_in, second_t))):
        for a in range(3):
            copies[3 * i + a].wait()
            for b in range(3):
                for e in range(3):
                    dst[a, b, e] = src[a, b, e].T


def attention_kernel(tok_n, zs, rows, own, *refs):
    ours, theirs = refs[:zs], refs[zs : 2 * zs]
    out_w, joint_w = refs[2 * zs : 2 + 2 * zs]
    part_refs = refs[2 + 2 * zs : -4]
    qq, kk, vv, part = refs[-4:]
    h, z, core, _ = place_of(tok_n)
    width = qq.shape[1]
    queries_n = qq.shape[0]
    labels = jnp.zeros((LABEL_ROWS, width), F32)
    for d in range(zs):
        qq[d * rows : (d + 1) * rows, :] = ours[d][0:rows, :]
        for ref, side in ((ours[d], core), (theirs[d], 1 - core)):
            at = pl.multiple_of((2 * (z ^ d) + side) * rows, rows)
            kk[pl.ds(at, rows), :] = ref[rows : 2 * rows, :]
            vv[pl.ds(at, rows), :] = ref[2 * rows : 3 * rows, :]
            labels = labels + ref[3 * rows + own :, :].astype(F32)
    heads_here = width // HD
    scale = HD ** (-0.5)
    query = qq[...]
    keys, values = kk[...], vv[...]
    lane_head = iota((queries_n, width), 1) // HD
    attended = jnp.zeros((queries_n, width), F32)
    for head in range(heads_here):
        mine = lane_head == head
        scores = dot_t(jnp.where(mine, query, jnp.zeros_like(query)), keys) * scale
        raw = jnp.exp(scores - jnp.max(scores, axis=1, keepdims=True))
        total = jnp.sum(raw, axis=1, keepdims=True)
        mixed = dot(raw.astype(BF16), values)
        attended = jnp.where(mine, mixed / total, attended)
    attended = attended.astype(BF16)
    part[...] = dot(attended, joint_w[...])
    for d in range(zs):
        at = pl.multiple_of(d * rows + h * own, own)
        part[pl.ds(at, own), :] += ours[d][3 * rows : 3 * rows + own, :].astype(F32)
    partial = part[...].astype(BF16)
    labels = labels.astype(BF16)
    first = dot(attended[0:rows, :], out_w[...])
    blocks = [first[i * own : (i + 1) * own, :] for i in range(rows // own)]
    for d, ref in enumerate(part_refs):
        ref[0:queries_n, :] = partial
        ref[queries_n : queries_n + LABEL_ROWS, :] = labels
        picked = blocks[0]
        for i in range(1, len(blocks)):
            picked = jnp.where((h ^ d) == i, blocks[i], picked)
        for i in range(picked.shape[1] // width):
            at = queries_n + LABEL_ROWS + i * own
            ref[at : at + own, :] = picked[:, i * width : (i + 1) * width].astype(BF16)


def decoder_kernel(sizes, *refs):
    nc, nt, ni, own_c, zs, tok_n, parts_n = sizes
    ours, theirs, r_ref, w1, w2, w1_t, w2_t, class_w, neck_w = refs[:9]
    parts = refs[9 : 9 + parts_n]
    encoded_ref, loss_ref, grad_ref, grid, cols, slope1, grad2, cols3 = refs[9 + parts_n :]
    channels = grid.shape[2]
    slab = nt * ni
    rows = nc * ni
    cells = nc * slab
    h, z, core, tslab = place_of(tok_n)
    taps = 9
    for d in range(zs):
        for ref, side in ((ours, core), (theirs, 1 - core)):
            block = ref[d * rows : (d + 1) * rows, :].astype(F32)
            at = pl.multiple_of((2 * (z ^ d) + side) * ni, ni)
            for c in range(nc):
                grid[c, pl.ds(at, ni), :] = block[c * ni : (c + 1) * ni, :]

    slope1[...] = jnp.zeros_like(slope1)
    grad2[...] = jnp.zeros_like(grad2)
    edge = jnp.zeros((slab, taps * channels), BF16)
    cols[0:slab, :] = edge
    cols[(nc + 1) * slab :, :] = edge

    def spread(value, c):
        for e in range(3):
            moved = along_inline(value, e - 1, ni)
            for b in range(3):
                lane = (b * 3 + e) * channels
                cols[(c + 1) * slab : (c + 2) * slab, lane : lane + channels] = along_rows(
                    moved, (b - 1) * ni
                ).astype(BF16)

    def conv(weights):
        total = None
        for a in range(3):
            matrix = weights[a].reshape(taps * channels, channels)
            term = dot(cols[a * slab : a * slab + cells, :], matrix)
            total = term if total is None else total + term
        return total

    for c in range(nc):
        spread(grid[c], c)
    hidden_one = conv(w1)
    for c in range(nc):
        v = hidden_one[c * slab : (c + 1) * slab, :]
        s = sigma_of(v)
        slope1[c + 1, ni : ni + slab, :] = s * (1.0 + v * (1.0 - s))
        spread((v * s).astype(BF16).astype(F32), c)
    hidden_two = conv(w2)
    sigma_two = sigma_of(hidden_two)
    active_two = (hidden_two * sigma_two).astype(BF16)
    class_row = class_w[...].astype(F32).reshape(1, channels)
    logits = dot_t(active_two, jnp.broadcast_to(class_row, (128, channels)).astype(BF16))
    probability = sigma_of(logits)
    lab = ours[rows * zs : rows * zs + ni, 0:128].astype(F32)
    spread_lab = jnp.broadcast_to(lab[None], (cells // ni, ni, 128)).reshape(cells, 128)
    wanted = iota((cells, 128), 0) // ni
    picked = jnp.where(iota((cells, 128), 1) == wanted, spread_lab, 0.0).astype(BF16)
    mask = dot(picked, jnp.ones((128, 128), BF16))
    intersection = jnp.sum(probability * mask, axis=0, keepdims=True)
    total_prob = jnp.sum(probability, axis=0, keepdims=True)
    total_fault = jnp.sum(mask, axis=0, keepdims=True)
    denominator = total_prob + total_fault
    loss_ref[...] = 1.0 - 2.0 * intersection / denominator
    grad_logits = (
        LOSS_SCALE
        * float(cells)
        * -2.0
        * (mask * denominator - intersection)
        / (denominator * denominator)
        * probability
        * (1.0 - probability)
    )
    wide = jnp.concatenate([grad_logits] * (channels // 128), axis=1)
    slope_two = sigma_two * (1.0 + hidden_two * (1.0 - sigma_two))
    g2 = wide * class_row * slope_two
    for c in range(nc):
        grad2[c + 2, 2 * ni : 2 * ni + slab, :] = g2[c * slab : (c + 1) * slab, :]

    band = 4 * ni
    c0 = h * own_c
    t0 = pl.multiple_of(tslab * ni, ni)
    for i in range(own_c + 4):
        region = grad2[c0 + i, pl.ds(t0, band + 2 * ni), :]
        for e in range(3):
            moved = along_inline(region, 1 - e, ni)
            for b in range(3):
                lane = (b * 3 + e) * channels
                cols3[i * band : (i + 1) * band, lane : lane + channels] = moved[
                    (2 - b) * ni : (2 - b) * ni + band, :
                ].astype(BF16)
    out3 = (own_c + 2) * band
    total = jnp.zeros((out3, channels), F32)
    for a in range(3):
        for b in range(3):
            for e in range(3):
                lane = (b * 3 + e) * channels
                piece = cols3[(2 - a) * band : (2 - a) * band + out3, lane : lane + channels]
                total = total + dot(piece, w2_t[a, b, e])
    slopes = [slope1[c0 + i, pl.ds(t0, band), :] for i in range(own_c + 2)]
    g1 = (total * jnp.concatenate(slopes, axis=0)).astype(BF16).astype(F32)
    shifted = [along_inline(g1, 1 - e, ni) for e in range(3)]
    total = jnp.zeros((own_c * ni, channels), F32)
    for a in range(3):
        for b in range(3):
            for e in range(3):
                cells_in = [
                    shifted[e][(i + 2 - a) * band + (2 - b) * ni : (i + 2 - a) * band + (3 - b) * ni, :]
                    for i in range(own_c)
                ]
                piece = jnp.concatenate(cells_in, axis=0).astype(BF16)
                total = total + dot(piece, w1_t[a, b, e])
    grad = dot_t(total.astype(BF16), neck_w[...])
    grad_ref[...] = grad.reshape(grad_ref.shape).astype(BF16)

    own = own_c * ni
    width = parts[0].shape[1]
    base = rows * zs + LABEL_ROWS
    for i in range(r_ref.shape[3] // width):
        terms = [ref[base + i * own : base + (i + 1) * own, :].astype(F32) for ref in parts]
        total = pairwise(terms).reshape(own_c, 1, ni, width)
        lanes = slice(i * width, (i + 1) * width)
        encoded_ref[:, :, :, lanes] = (r_ref[:, :, :, lanes].astype(F32) + total).astype(BF16)


def pairwise(values):
    while len(values) > 1:
        values = [values[i] + values[i + 1] for i in range(0, len(values), 2)]
    return values[0]


def vmem():
    return pl.BlockSpec(memory_space=pltpu.VMEM)


def hbm():
    return pl.BlockSpec(memory_space=pltpu.HBM)


def whole_grid(
    queries, key_rows, value_rows, residual, w_out, w_neck, w_first, w_second, w_class, labels
):
    heads_n, tok_n = lax.axis_size("heads"), lax.axis_size("tok")
    zs = tok_n // 2
    _, nc, ni, width = queries.shape
    own_c = residual.shape[0]
    nt = labels.shape[1]
    channels = w_neck.shape[1]
    rows, own = nc * ni, own_c * ni

    def swap_tok(value, bits):
        return lax.ppermute(value, "tok", [(i, i ^ bits) for i in range(tok_n)])

    def swap_heads(value, bits):
        return lax.ppermute(value, "heads", [(i, i ^ bits) for i in range(heads_n)])

    packed = pl.pallas_call(
        functools.partial(pack_kernel, tok_n),
        out_shape=pltpu.VMEM((3 * rows + own + LABEL_ROWS, width), BF16),
        in_specs=[vmem()] * 6,
        out_specs=vmem(),
    )(queries, key_rows, value_rows, residual, w_neck, labels.transpose(0, 2, 1))
    ours = [packed] + [swap_tok(packed, 2 * d) for d in range(1, zs)]
    kept = [pltpu.with_memory_space_constraint(w, pltpu.HBM) for w in (w_first, w_second, w_out, w_neck)]
    first_in, second_in, first_t, second_t, joint, again, out_w, neck_w = pl.pallas_call(
        weights_kernel,
        out_shape=[pltpu.VMEM(w_first.shape, BF16)] * 4
        + [
            pltpu.VMEM((width, channels), BF16),
            pltpu.VMEM(packed.shape, BF16),
            pltpu.VMEM(w_out.shape, BF16),
            pltpu.VMEM(w_neck.shape, BF16),
        ],
        in_specs=[hbm()] * 4 + [vmem()],
        out_specs=[vmem()] * 8,
        scratch_shapes=[pltpu.SemaphoreType.DMA((8,))],
        compiler_params=pltpu.CompilerParams(vmem_limit_bytes=24 * 2**20),
        cost_estimate=pl.CostEstimate(flops=0, bytes_accessed=28 * 2**20, transcendentals=0),
    )(*kept, packed)
    theirs = [swap_tok(value, 1) for value in [again] + ours[1:]]
    queries_n, keys_n = rows * zs, rows * tok_n
    enc_rows = own * residual.shape[3] // width
    part_shape = pltpu.VMEM((queries_n + LABEL_ROWS + enc_rows, channels), BF16)
    sent = pl.pallas_call(
        functools.partial(attention_kernel, tok_n, zs, rows, own),
        out_shape=[part_shape] * heads_n,
        in_specs=[vmem()] * (2 * zs + 2),
        out_specs=[vmem()] * heads_n,
        scratch_shapes=[
            pltpu.VMEM((queries_n, width), BF16),
            pltpu.VMEM((keys_n, width), BF16),
            pltpu.VMEM((keys_n, width), BF16),
            pltpu.VMEM((queries_n, channels), F32),
        ],
        compiler_params=pltpu.CompilerParams(vmem_limit_bytes=16 * 2**20),
    )(*ours, *theirs, out_w, joint)
    parts = [sent[0]] + [swap_heads(sent[d], d) for d in range(1, heads_n)]
    used = queries_n + LABEL_ROWS
    half = pairwise([part[:used].astype(F32) for part in parts]).astype(BF16)
    other = swap_tok(half, 1)
    slab = nt * ni
    return tuple(
        pl.pallas_call(
            functools.partial(decoder_kernel, (nc, nt, ni, own_c, zs, tok_n, heads_n)),
            out_shape=[
                jax.ShapeDtypeStruct(residual.shape, BF16),
                jax.ShapeDtypeStruct((1, 128), F32),
                jax.ShapeDtypeStruct(residual.shape, BF16),
            ],
            in_specs=[vmem()] * (9 + heads_n),
            out_specs=[vmem()] * 3,
            scratch_shapes=[
                pltpu.VMEM((nc, slab, channels), F32),
                pltpu.VMEM(((nc + 2) * slab, 9 * channels), BF16),
                pltpu.VMEM((nc + 2, (nt + 4) * ni, channels), F32),
                pltpu.VMEM((nc + 4, (nt + 6) * ni, channels), F32),
                pltpu.VMEM(((own_c + 4) * 4 * ni, 9 * channels), BF16),
            ],
            compiler_params=pltpu.CompilerParams(vmem_limit_bytes=36 * 2**20),
        )(half, other, residual, first_in, second_in, first_t, second_t, w_class, neck_w, *parts)
    )


def power_of_two(n):
    return n > 0 and n & (n - 1) == 0


def fits_whole(queries, residual, w_neck, labels):
    heads_n, tok_n = lax.axis_size("heads"), lax.axis_size("tok")
    slabs, nc, ni, width = queries.shape
    nt = labels.shape[1]
    return (
        slabs == 1
        and nc * nt <= 128
        and labels.shape[2] == 1
        and ni == 8
        and nt == tok_n
        and tok_n >= 4
        and power_of_two(tok_n)
        and power_of_two(heads_n)
        and residual.shape[0] * heads_n == nc
        and nc * nt * ni <= 1024
        and width % 128 == 0
        and w_neck.shape[1] == width
        and (residual.shape[0] * ni) % 16 == 0
    )


def on_device(*arguments):
    queries, residual, w_neck, labels = (arguments[i] for i in (0, 3, 5, 9))
    if fits_whole(queries, residual, w_neck, labels):
        encoded, loss, grad = whole_grid(*arguments)
        return (encoded, loss[0, 0], grad)
    return on_tiles(*arguments)


def solution(mesh):
    placed = (
        P("tok", None, None, "heads"),
        P("tok", None, None, "heads"),
        P("tok", None, None, "heads"),
        P("heads", "tok", None, None),
        P("heads", None),
        P(),
        P(),
        P(),
        P(),
        P("heads", None, "tok"),
    )
    return jax.shard_map(
        on_device,
        mesh=mesh,
        in_specs=placed,
        out_specs=(P("heads", "tok", None, None), P(), P("heads", "tok", None, None)),
        check_vma=False,
    )
```

```python
import functools

import jax
import jax.numpy as jnp
from jax import lax
from jax.experimental import pallas as pl
from jax.experimental.pallas import tpu as pltpu
from jax.sharding import PartitionSpec as P

HD = 64
F32 = jnp.float32
BF16 = jnp.bfloat16
LABEL_ROWS = 16
TILE = 128


OFFSETS = [
    (along_c, along_t, along_x)
    for along_c in range(3)
    for along_t in range(3)
    for along_x in range(3)
]
LOSS_SCALE = 64.0
NEG_LARGE = -1e30


def padded_2(value, sides, width):
    for axis, dim in sides:
        size, length = (lax.axis_size(axis), value.shape[dim])
        up = [(i, (i + 1) % size) for i in range(size - 1)]
        down = [(j, i) for i, j in up]
        last = lax.slice_in_dim(value, length - width, length, axis=dim)
        first = lax.slice_in_dim(value, 0, width, axis=dim)
        before = lax.ppermute(last, axis, up)
        after = lax.ppermute(first, axis, down)
        value = jnp.concatenate([before, value, after], axis=dim)
    return value


def silu_slope(volume):
    sigma = jax.nn.sigmoid(volume)
    return sigma * (1.0 + volume * (1.0 - sigma))


def with_rims(volume):
    padded = padded_2(volume, (("heads", 0), ("tok", 2)), 1)
    return jnp.pad(padded, ((0, 0), (1, 1), (0, 0), (0, 0)))


def conv_apply(volume, weights, flipped):
    extent = volume.shape[:3]
    padded = with_rims(volume)
    pieces = []
    for along_c, along_t, along_x in OFFSETS:
        if flipped:
            anchor = (2 - along_c, 2 - along_t, 2 - along_x)
        else:
            anchor = (along_c, along_t, along_x)
        pieces.append(
            padded[
                anchor[0] : anchor[0] + extent[0],
                anchor[1] : anchor[1] + extent[1],
                anchor[2] : anchor[2] + extent[2],
            ]
        )
    stacked = jnp.stack(pieces, axis=3)
    columns = stacked.reshape(extent[0] * extent[1] * extent[2], 27, volume.shape[3])
    kernel = weights.reshape(27, weights.shape[3], weights.shape[4])
    if flipped:
        contraction = (((1, 2), (0, 2)), ((), ()))
    else:
        contraction = (((1, 2), (0, 1)), ((), ()))
    return lax.dot_general(columns, kernel, contraction, preferred_element_type=jnp.float32)


def online_step(carried, query_block, key_block, value_block, scale):
    row_peak, totals, weighted_sum = carried
    scores = (
        jnp.einsum("qhd,khd->qhk", query_block, key_block, preferred_element_type=jnp.float32)
        * scale
    )
    new_peak = jnp.maximum(row_peak, jnp.max(scores, axis=-1))
    factor = jnp.exp(row_peak - new_peak)
    raw_weights = jnp.exp(scores - new_peak[:, :, None])
    totals = totals * factor + jnp.sum(raw_weights, axis=-1)
    weighted_sum = weighted_sum * factor[:, :, None] + jnp.einsum(
        "qhk,khd->qhd",
        raw_weights.astype(jnp.bfloat16),
        value_block,
        preferred_element_type=jnp.float32,
    )
    return (new_peak, totals, weighted_sum)


def on_tiles(
    queries, key_rows, value_rows, residual, w_out, w_neck, w_first, w_second, w_class, labels
):
    width_here = queries.shape[-1]
    heads_here = width_here // HD
    scale = HD ** (-0.5)
    local_queries = queries.reshape(-1, heads_here, HD)
    query_total = local_queries.shape[0]
    start_state = (
        jnp.full((query_total, heads_here), NEG_LARGE, jnp.float32),
        jnp.zeros((query_total, heads_here), jnp.float32),
        jnp.zeros((query_total, heads_here, HD), jnp.float32),
    )

    def fold_keys(carried, key_piece):
        key_flat = key_piece[0].reshape(-1, heads_here, HD)
        value_flat = key_piece[1].reshape(-1, heads_here, HD)
        key_total = key_flat.shape[0]
        if key_total > 512 and key_total % 512 == 0:
            key_blocks = key_flat.reshape(key_total // 512, 512, heads_here, HD)
            value_blocks = value_flat.reshape(key_total // 512, 512, heads_here, HD)

            def scan_step(inner, paired):
                return (online_step(inner, local_queries, paired[0], paired[1], scale), None)

            return lax.scan(scan_step, carried, (key_blocks, value_blocks))[0]
        return online_step(carried, local_queries, key_flat, value_flat, scale)

    row_peak, totals, weighted_sum = fold_keys(
        start_state,
        (
            lax.all_gather(key_rows, "tok", axis=0, tiled=True),
            lax.all_gather(value_rows, "tok", axis=0, tiled=True),
        ),
    )
    attended = (weighted_sum / totals[:, :, None]).astype(jnp.bfloat16)
    attended_grid = attended.reshape(queries.shape)
    owned = lax.all_to_all(attended_grid, "heads", split_axis=1, concat_axis=3, tiled=True)
    attention_out = jnp.einsum(
        "tzxe,ed->ztxd",
        owned,
        lax.all_gather(w_out, "heads", axis=0, tiled=True),
        preferred_element_type=jnp.float32,
    )
    encoded = (residual.astype(jnp.float32) + attention_out).astype(jnp.bfloat16)
    tiled = lax.all_to_all(encoded, "tok", split_axis=2, concat_axis=1, tiled=True)
    neck_feats = jnp.einsum(
        "ztxd,dc->ztxc", tiled, w_neck, preferred_element_type=jnp.float32
    ).astype(jnp.bfloat16)
    extent = neck_feats.shape[:3]
    channels = w_neck.shape[1]
    cell_count = extent[0] * extent[1] * extent[2]
    hidden_one = conv_apply(neck_feats, w_first, False)
    active_one = jax.nn.silu(hidden_one).astype(jnp.bfloat16)
    hidden_two = conv_apply(active_one.reshape(extent + (channels,)), w_second, False)
    active_two = jax.nn.silu(hidden_two).astype(jnp.bfloat16)
    logits = jnp.dot(active_two, w_class, preferred_element_type=jnp.float32)
    probability = jax.nn.sigmoid(logits)
    fault_mask = labels.reshape(cell_count).astype(jnp.float32)
    intersection, total_prob, total_fault = lax.psum(
        (jnp.sum(probability * fault_mask), jnp.sum(probability), jnp.sum(fault_mask)),
        ("heads", "tok"),
    )
    dice_denominator = total_prob + total_fault
    dice_loss = 1.0 - 2.0 * intersection / dice_denominator
    cells_all = float(cell_count * lax.axis_size("heads") * lax.axis_size("tok"))
    grad_logits = (
        LOSS_SCALE
        * cells_all
        * -2.0
        * (fault_mask * dice_denominator - intersection)
        / (dice_denominator * dice_denominator)
        * probability
        * (1.0 - probability)
    )
    grad_hidden_two = (
        grad_logits[:, None] * w_class.astype(jnp.float32)[None, :] * silu_slope(hidden_two)
    ).astype(jnp.bfloat16)
    grad_active_one = conv_apply(grad_hidden_two.reshape(extent + (channels,)), w_second, True)
    grad_hidden_one = (grad_active_one * silu_slope(hidden_one)).astype(jnp.bfloat16)
    grad_neck = (
        conv_apply(grad_hidden_one.reshape(extent + (channels,)), w_first, True)
        .astype(jnp.bfloat16)
        .reshape(extent + (channels,))
    )
    grad_tiles = jnp.einsum(
        "ztxc,dc->ztxd", grad_neck, w_neck, preferred_element_type=jnp.float32
    ).astype(jnp.bfloat16)
    grad_encoded = lax.all_to_all(grad_tiles, "tok", split_axis=1, concat_axis=2, tiled=True)
    return (encoded, dice_loss, grad_encoded)


def dot(a, b):
    return jnp.dot(a, b, preferred_element_type=F32)


def dot_t(a, b):
    return lax.dot_general(a, b, (((1,), (1,)), ((), ())), preferred_element_type=F32)


def sigma_of(v):
    return 1.0 / (1.0 + jnp.exp(-v))


def slope_of(v):
    s = sigma_of(v)
    return s * (1.0 + v * (1.0 - s))


def iota(shape, dim):
    return lax.broadcasted_iota(jnp.int32, shape, dim)


def along_inline(value, step, inline):
    if step == 0:
        return value
    rows = value.shape[0]
    x = iota(value.shape, 0) % inline
    edge = inline - 1 if step > 0 else 0
    return jnp.where(x == edge, 0.0, pltpu.roll(value, (-step) % rows, axis=0))


def along_rows(value, step):
    if step == 0:
        return value
    zeros = jnp.zeros((abs(step), value.shape[1]), value.dtype)
    if step > 0:
        return jnp.concatenate([value[step:], zeros], axis=0)
    return jnp.concatenate([zeros, value[:step]], axis=0)


def place_of(tok_n):
    h, t = lax.axis_index("heads"), lax.axis_index("tok")
    return h, t // 2, t % 2, t


def pack_kernel(tok_n, q_ref, k_ref, v_ref, r_ref, neck_ref, lab_ref, out_ref):
    h, _, _, t = place_of(tok_n)
    rows = q_ref.shape[1] * q_ref.shape[2]
    width = q_ref.shape[3]
    for i, ref in enumerate((q_ref, k_ref, v_ref)):
        flat = ref[...].astype(F32).reshape(rows, width).astype(BF16)
        out_ref[i * rows : (i + 1) * rows, :] = flat
    own = r_ref.shape[0] * r_ref.shape[2]
    residual = r_ref[...].astype(F32).reshape(own, r_ref.shape[3]).astype(BF16)
    out_ref[3 * rows : 3 * rows + own, :] = dot(residual, neck_ref[...]).astype(BF16)
    own_c, _, nt = lab_ref.shape
    spread = jnp.zeros((LABEL_ROWS, width), F32)
    for c in range(own_c):
        row = jnp.broadcast_to(lab_ref[c].astype(F32), (LABEL_ROWS, nt)).astype(BF16)
        at = (h * own_c + c) * nt + iota((nt, width), 0)
        spread = spread + dot(row, (iota((nt, width), 1) == at).astype(F32).astype(BF16))
    out_ref[3 * rows + own :, :] = jnp.where(
        iota((LABEL_ROWS, width), 0) == t, spread, 0.0
    ).astype(BF16)


def weights_kernel(first_ref, second_ref, out_ref, neck_ref, packed_ref, *refs):
    first_in, second_in, first_t, second_t, joint, again, out_w, neck_w, sems = refs
    small = [
        pltpu.make_async_copy(out_ref, out_w, sems.at[6]),
        pltpu.make_async_copy(neck_ref, neck_w, sems.at[7]),
    ]
    for copy in small:
        copy.start()
    copies = []
    for i, (src, dst) in enumerate(((first_ref, first_in), (second_ref, second_in))):
        for a in range(3):
            copies.append(pltpu.make_async_copy(src.at[a], dst.at[a], sems.at[3 * i + a]))
            copies[-1].start()
    again[...] = packed_ref[...]
    for copy in small:
        copy.wait()
    joint[...] = dot(out_w[...], neck_w[...]).astype(BF16)
    for i, (src, dst) in enumerate(((first_in, first_t), (second_in, second_t))):
        for a in range(3):
            copies[3 * i + a].wait()
            for b in range(3):
                for e in range(3):
                    dst[a, b, e] = src[a, b, e].T


def attention_kernel(tok_n, zs, rows, own, *refs):
    ours, theirs = refs[:zs], refs[zs : 2 * zs]
    out_w, joint_w = refs[2 * zs : 2 + 2 * zs]
    part_refs = refs[2 + 2 * zs : -4]
    qq, kk, vv, part = refs[-4:]
    h, z, core, _ = place_of(tok_n)
    width = qq.shape[1]
    queries_n = qq.shape[0]
    labels = jnp.zeros((LABEL_ROWS, width), F32)
    for d in range(zs):
        qq[d * rows : (d + 1) * rows, :] = ours[d][0:rows, :]
        for ref, side in ((ours[d], core), (theirs[d], 1 - core)):
            at = pl.multiple_of((2 * (z ^ d) + side) * rows, rows)
            kk[pl.ds(at, rows), :] = ref[rows : 2 * rows, :]
            vv[pl.ds(at, rows), :] = ref[2 * rows : 3 * rows, :]
            labels = labels + ref[3 * rows + own :, :].astype(F32)
    heads_here = width // HD
    scale = HD ** (-0.5)
    query = qq[...]
    keys, values = kk[...], vv[...]
    lane_head = iota((queries_n, width), 1) // HD
    attended = jnp.zeros((queries_n, width), F32)
    for head in range(heads_here):
        mine = lane_head == head
        scores = dot_t(jnp.where(mine, query, jnp.zeros_like(query)), keys) * scale
        raw = jnp.exp(scores - jnp.max(scores, axis=1, keepdims=True))
        total = jnp.sum(raw, axis=1, keepdims=True)
        mixed = dot(raw.astype(BF16), values)
        attended = jnp.where(mine, mixed / total, attended)
    attended = attended.astype(BF16)
    part[...] = dot(attended, joint_w[...])
    for d in range(zs):
        at = pl.multiple_of(d * rows + h * own, own)
        part[pl.ds(at, own), :] += ours[d][3 * rows : 3 * rows + own, :].astype(F32)
    partial = part[...].astype(BF16)
    labels = labels.astype(BF16)
    first = dot(attended[0:rows, :], out_w[...])
    blocks = [first[i * own : (i + 1) * own, :] for i in range(rows // own)]
    for d, ref in enumerate(part_refs):
        ref[0:queries_n, :] = partial
        ref[queries_n : queries_n + LABEL_ROWS, :] = labels
        picked = blocks[0]
        for i in range(1, len(blocks)):
            picked = jnp.where((h ^ d) == i, blocks[i], picked)
        for i in range(picked.shape[1] // width):
            at = queries_n + LABEL_ROWS + i * own
            ref[at : at + own, :] = picked[:, i * width : (i + 1) * width].astype(BF16)


def decoder_kernel(sizes, *refs):
    nc, nt, ni, own_c, zs, tok_n, parts_n = sizes
    ours, theirs, r_ref, w1, w2, w1_t, w2_t, class_w, neck_w = refs[:9]
    parts = refs[9 : 9 + parts_n]
    encoded_ref, loss_ref, grad_ref, grid, cols, slope1, grad2, cols3, hid1, hid2 = refs[9 + parts_n :]
    channels = grid.shape[2]
    slab = nt * ni
    rows = nc * ni
    cells = nc * slab
    h, z, core, tslab = place_of(tok_n)
    taps = 9
    for d in range(zs):
        for ref, side in ((ours, core), (theirs, 1 - core)):
            block = ref[d * rows : (d + 1) * rows, :].astype(F32)
            at = pl.multiple_of((2 * (z ^ d) + side) * ni, ni)
            for c in range(nc):
                grid[c, pl.ds(at, ni), :] = block[c * ni : (c + 1) * ni, :]

    slope1[...] = jnp.zeros_like(slope1)
    grad2[...] = jnp.zeros_like(grad2)
    edge = jnp.zeros((slab, taps * channels), BF16)
    cols[0:slab, :] = edge
    cols[(nc + 1) * slab :, :] = edge

    def spread(value, c):
        for e in range(3):
            moved = along_inline(value, e - 1, ni)
            for b in range(3):
                lane = (b * 3 + e) * channels
                cols[(c + 1) * slab : (c + 2) * slab, lane : lane + channels] = along_rows(
                    moved, (b - 1) * ni
                ).astype(BF16)

    def conv(weights, out):
        for m in range(0, cells, TILE):
            total = None
            for a in range(3):
                matrix = weights[a].reshape(taps * channels, channels)
                term = dot(cols[a * slab + m : a * slab + m + TILE, :], matrix)
                total = term if total is None else total + term
            out[m : m + TILE, :] = total

    for c in range(nc):
        spread(grid[c], c)
    conv(w1, hid1)
    for c in range(nc):
        v = hid1[c * slab : (c + 1) * slab, :]
        s = sigma_of(v)
        slope1[c + 1, ni : ni + slab, :] = s * (1.0 + v * (1.0 - s))
        spread((v * s).astype(BF16).astype(F32), c)
    conv(w2, hid2)
    hidden_two = hid2[...]
    sigma_two = sigma_of(hidden_two)
    active_two = (hidden_two * sigma_two).astype(BF16)
    class_row = class_w[...].astype(F32).reshape(1, channels)
    logits = dot_t(active_two, jnp.broadcast_to(class_row, (128, channels)).astype(BF16))
    probability = sigma_of(logits)
    lab = ours[rows * zs : rows * zs + ni, 0:128].astype(F32)
    spread_lab = jnp.broadcast_to(lab[None], (cells // ni, ni, 128)).reshape(cells, 128)
    wanted = iota((cells, 128), 0) // ni
    picked = jnp.where(iota((cells, 128), 1) == wanted, spread_lab, 0.0).astype(BF16)
    mask = dot(picked, jnp.ones((128, 128), BF16))
    intersection = jnp.sum(probability * mask, axis=0, keepdims=True)
    total_prob = jnp.sum(probability, axis=0, keepdims=True)
    total_fault = jnp.sum(mask, axis=0, keepdims=True)
    denominator = total_prob + total_fault
    loss_ref[...] = 1.0 - 2.0 * intersection / denominator
    grad_logits = (
        LOSS_SCALE
        * float(cells)
        * -2.0
        * (mask * denominator - intersection)
        / (denominator * denominator)
        * probability
        * (1.0 - probability)
    )
    wide = jnp.concatenate([grad_logits] * (channels // 128), axis=1)
    slope_two = sigma_two * (1.0 + hidden_two * (1.0 - sigma_two))
    g2 = wide * class_row * slope_two
    for c in range(nc):
        grad2[c + 2, 2 * ni : 2 * ni + slab, :] = g2[c * slab : (c + 1) * slab, :]

    band = 4 * ni
    c0 = h * own_c
    t0 = pl.multiple_of(tslab * ni, ni)
    for i in range(own_c + 4):
        region = grad2[c0 + i, pl.ds(t0, band + 2 * ni), :]
        for e in range(3):
            moved = along_inline(region, 1 - e, ni)
            for b in range(3):
                lane = (b * 3 + e) * channels
                cols3[i * band : (i + 1) * band, lane : lane + channels] = moved[
                    (2 - b) * ni : (2 - b) * ni + band, :
                ].astype(BF16)
    out3 = (own_c + 2) * band
    total = jnp.zeros((out3, channels), F32)
    for a in range(3):
        for b in range(3):
            for e in range(3):
                lane = (b * 3 + e) * channels
                piece = cols3[(2 - a) * band : (2 - a) * band + out3, lane : lane + channels]
                total = total + dot(piece, w2_t[a, b, e])
    slopes = [slope1[c0 + i, pl.ds(t0, band), :] for i in range(own_c + 2)]
    g1 = (total * jnp.concatenate(slopes, axis=0)).astype(BF16).astype(F32)
    shifted = [along_inline(g1, 1 - e, ni) for e in range(3)]
    total = jnp.zeros((own_c * ni, channels), F32)
    for a in range(3):
        pieces = []
        for b in range(3):
            for e in range(3):
                cells_in = [
                    shifted[e][(i + 2 - a) * band + (2 - b) * ni : (i + 2 - a) * band + (3 - b) * ni, :]
                    for i in range(own_c)
                ]
                pieces.append(jnp.concatenate(cells_in, axis=0).astype(BF16))
        matrix = w1_t[a].reshape(taps * channels, channels)
        total = total + dot(jnp.concatenate(pieces, axis=1), matrix)
    grad = dot_t(total.astype(BF16), neck_w[...])
    grad_ref[...] = grad.reshape(grad_ref.shape).astype(BF16)

    own = own_c * ni
    width = parts[0].shape[1]
    base = rows * zs + LABEL_ROWS
    for i in range(r_ref.shape[3] // width):
        terms = [ref[base + i * own : base + (i + 1) * own, :].astype(F32) for ref in parts]
        total = pairwise(terms).reshape(own_c, 1, ni, width)
        lanes = slice(i * width, (i + 1) * width)
        encoded_ref[:, :, :, lanes] = (r_ref[:, :, :, lanes].astype(F32) + total).astype(BF16)


def pairwise(values):
    while len(values) > 1:
        values = [values[i] + values[i + 1] for i in range(0, len(values), 2)]
    return values[0]


def vmem():
    return pl.BlockSpec(memory_space=pltpu.VMEM)


def hbm():
    return pl.BlockSpec(memory_space=pltpu.HBM)


def whole_grid(
    queries, key_rows, value_rows, residual, w_out, w_neck, w_first, w_second, w_class, labels
):
    heads_n, tok_n = lax.axis_size("heads"), lax.axis_size("tok")
    zs = tok_n // 2
    _, nc, ni, width = queries.shape
    own_c = residual.shape[0]
    nt = labels.shape[1]
    channels = w_neck.shape[1]
    rows, own = nc * ni, own_c * ni

    def swap_tok(value, bits):
        return lax.ppermute(value, "tok", [(i, i ^ bits) for i in range(tok_n)])

    def swap_heads(value, bits):
        return lax.ppermute(value, "heads", [(i, i ^ bits) for i in range(heads_n)])

    packed = pl.pallas_call(
        functools.partial(pack_kernel, tok_n),
        out_shape=pltpu.VMEM((3 * rows + own + LABEL_ROWS, width), BF16),
        in_specs=[vmem()] * 6,
        out_specs=vmem(),
    )(queries, key_rows, value_rows, residual, w_neck, labels.transpose(0, 2, 1))
    ours = [packed] + [swap_tok(packed, 2 * d) for d in range(1, zs)]
    kept = [pltpu.with_memory_space_constraint(w, pltpu.HBM) for w in (w_first, w_second, w_out, w_neck)]
    first_in, second_in, first_t, second_t, joint, again, out_w, neck_w = pl.pallas_call(
        weights_kernel,
        out_shape=[pltpu.VMEM(w_first.shape, BF16)] * 4
        + [
            pltpu.VMEM((width, channels), BF16),
            pltpu.VMEM(packed.shape, BF16),
            pltpu.VMEM(w_out.shape, BF16),
            pltpu.VMEM(w_neck.shape, BF16),
        ],
        in_specs=[hbm()] * 4 + [vmem()],
        out_specs=[vmem()] * 8,
        scratch_shapes=[pltpu.SemaphoreType.DMA((8,))],
        compiler_params=pltpu.CompilerParams(vmem_limit_bytes=24 * 2**20),
        cost_estimate=pl.CostEstimate(flops=0, bytes_accessed=28 * 2**20, transcendentals=0),
    )(*kept, packed)
    theirs = [swap_tok(value, 1) for value in [again] + ours[1:]]
    queries_n, keys_n = rows * zs, rows * tok_n
    enc_rows = own * residual.shape[3] // width
    part_shape = pltpu.VMEM((queries_n + LABEL_ROWS + enc_rows, channels), BF16)
    sent = pl.pallas_call(
        functools.partial(attention_kernel, tok_n, zs, rows, own),
        out_shape=[part_shape] * heads_n,
        in_specs=[vmem()] * (2 * zs + 2),
        out_specs=[vmem()] * heads_n,
        scratch_shapes=[
            pltpu.VMEM((queries_n, width), BF16),
            pltpu.VMEM((keys_n, width), BF16),
            pltpu.VMEM((keys_n, width), BF16),
            pltpu.VMEM((queries_n, channels), F32),
        ],
        compiler_params=pltpu.CompilerParams(vmem_limit_bytes=16 * 2**20),
    )(*ours, *theirs, out_w, joint)
    parts = [sent[0]] + [swap_heads(sent[d], d) for d in range(1, heads_n)]
    used = queries_n + LABEL_ROWS
    half = pairwise([part[:used].astype(F32) for part in parts]).astype(BF16)
    other = swap_tok(half, 1)
    slab = nt * ni
    return tuple(
        pl.pallas_call(
            functools.partial(decoder_kernel, (nc, nt, ni, own_c, zs, tok_n, heads_n)),
            out_shape=[
                jax.ShapeDtypeStruct(residual.shape, BF16),
                jax.ShapeDtypeStruct((1, 128), F32),
                jax.ShapeDtypeStruct(residual.shape, BF16),
            ],
            in_specs=[vmem()] * (9 + heads_n),
            out_specs=[vmem()] * 3,
            scratch_shapes=[
                pltpu.VMEM((nc, slab, channels), F32),
                pltpu.VMEM(((nc + 2) * slab, 9 * channels), BF16),
                pltpu.VMEM((nc + 2, (nt + 4) * ni, channels), F32),
                pltpu.VMEM((nc + 4, (nt + 6) * ni, channels), F32),
                pltpu.VMEM(((own_c + 4) * 4 * ni, 9 * channels), BF16),
                pltpu.VMEM((nc * slab, channels), F32),
                pltpu.VMEM((nc * slab, channels), F32),
            ],
            compiler_params=pltpu.CompilerParams(vmem_limit_bytes=36 * 2**20),
        )(half, other, residual, first_in, second_in, first_t, second_t, w_class, neck_w, *parts)
    )


def power_of_two(n):
    return n > 0 and n & (n - 1) == 0


def fits_whole(queries, residual, w_neck, labels):
    heads_n, tok_n = lax.axis_size("heads"), lax.axis_size("tok")
    slabs, nc, ni, width = queries.shape
    nt = labels.shape[1]
    return (
        slabs == 1
        and nc * nt <= 128
        and labels.shape[2] == 1
        and ni == 8
        and nt == tok_n
        and tok_n >= 4
        and power_of_two(tok_n)
        and power_of_two(heads_n)
        and residual.shape[0] * heads_n == nc
        and nc * nt * ni <= 1024
        and (nc * nt * ni) % TILE == 0
        and width % 128 == 0
        and w_neck.shape[1] == width
        and (residual.shape[0] * ni) % 16 == 0
    )


def on_device(*arguments):
    queries, residual, w_neck, labels = (arguments[i] for i in (0, 3, 5, 9))
    if fits_whole(queries, residual, w_neck, labels):
        encoded, loss, grad = whole_grid(*arguments)
        return (encoded, loss[0, 0], grad)
    return on_tiles(*arguments)


def solution(mesh):
    placed = (
        P("tok", None, None, "heads"),
        P("tok", None, None, "heads"),
        P("tok", None, None, "heads"),
        P("heads", "tok", None, None),
        P("heads", None),
        P(),
        P(),
        P(),
        P(),
        P("heads", None, "tok"),
    )
    return jax.shard_map(
        on_device,
        mesh=mesh,
        in_specs=placed,
        out_specs=(P("heads", "tok", None, None), P(), P("heads", "tok", None, None)),
        check_vma=False,
    )
```

```python
import functools

import jax
import jax.numpy as jnp
from jax import lax
from jax.experimental import pallas as pl
from jax.experimental.pallas import tpu as pltpu
from jax.sharding import PartitionSpec as P

HD = 64
F32 = jnp.float32
BF16 = jnp.bfloat16
LABEL_ROWS = 16
TILE = 128


OFFSETS = [
    (along_c, along_t, along_x)
    for along_c in range(3)
    for along_t in range(3)
    for along_x in range(3)
]
LOSS_SCALE = 64.0
NEG_LARGE = -1e30


def padded_2(value, sides, width):
    for axis, dim in sides:
        size, length = (lax.axis_size(axis), value.shape[dim])
        up = [(i, (i + 1) % size) for i in range(size - 1)]
        down = [(j, i) for i, j in up]
        last = lax.slice_in_dim(value, length - width, length, axis=dim)
        first = lax.slice_in_dim(value, 0, width, axis=dim)
        before = lax.ppermute(last, axis, up)
        after = lax.ppermute(first, axis, down)
        value = jnp.concatenate([before, value, after], axis=dim)
    return value


def silu_slope(volume):
    sigma = jax.nn.sigmoid(volume)
    return sigma * (1.0 + volume * (1.0 - sigma))


def with_rims(volume):
    padded = padded_2(volume, (("heads", 0), ("tok", 2)), 1)
    return jnp.pad(padded, ((0, 0), (1, 1), (0, 0), (0, 0)))


def conv_apply(volume, weights, flipped):
    extent = volume.shape[:3]
    padded = with_rims(volume)
    pieces = []
    for along_c, along_t, along_x in OFFSETS:
        if flipped:
            anchor = (2 - along_c, 2 - along_t, 2 - along_x)
        else:
            anchor = (along_c, along_t, along_x)
        pieces.append(
            padded[
                anchor[0] : anchor[0] + extent[0],
                anchor[1] : anchor[1] + extent[1],
                anchor[2] : anchor[2] + extent[2],
            ]
        )
    stacked = jnp.stack(pieces, axis=3)
    columns = stacked.reshape(extent[0] * extent[1] * extent[2], 27, volume.shape[3])
    kernel = weights.reshape(27, weights.shape[3], weights.shape[4])
    if flipped:
        contraction = (((1, 2), (0, 2)), ((), ()))
    else:
        contraction = (((1, 2), (0, 1)), ((), ()))
    return lax.dot_general(columns, kernel, contraction, preferred_element_type=jnp.float32)


def online_step(carried, query_block, key_block, value_block, scale):
    row_peak, totals, weighted_sum = carried
    scores = (
        jnp.einsum("qhd,khd->qhk", query_block, key_block, preferred_element_type=jnp.float32)
        * scale
    )
    new_peak = jnp.maximum(row_peak, jnp.max(scores, axis=-1))
    factor = jnp.exp(row_peak - new_peak)
    raw_weights = jnp.exp(scores - new_peak[:, :, None])
    totals = totals * factor + jnp.sum(raw_weights, axis=-1)
    weighted_sum = weighted_sum * factor[:, :, None] + jnp.einsum(
        "qhk,khd->qhd",
        raw_weights.astype(jnp.bfloat16),
        value_block,
        preferred_element_type=jnp.float32,
    )
    return (new_peak, totals, weighted_sum)


def on_tiles(
    queries, key_rows, value_rows, residual, w_out, w_neck, w_first, w_second, w_class, labels
):
    width_here = queries.shape[-1]
    heads_here = width_here // HD
    scale = HD ** (-0.5)
    local_queries = queries.reshape(-1, heads_here, HD)
    query_total = local_queries.shape[0]
    start_state = (
        jnp.full((query_total, heads_here), NEG_LARGE, jnp.float32),
        jnp.zeros((query_total, heads_here), jnp.float32),
        jnp.zeros((query_total, heads_here, HD), jnp.float32),
    )

    def fold_keys(carried, key_piece):
        key_flat = key_piece[0].reshape(-1, heads_here, HD)
        value_flat = key_piece[1].reshape(-1, heads_here, HD)
        key_total = key_flat.shape[0]
        if key_total > 512 and key_total % 512 == 0:
            key_blocks = key_flat.reshape(key_total // 512, 512, heads_here, HD)
            value_blocks = value_flat.reshape(key_total // 512, 512, heads_here, HD)

            def scan_step(inner, paired):
                return (online_step(inner, local_queries, paired[0], paired[1], scale), None)

            return lax.scan(scan_step, carried, (key_blocks, value_blocks))[0]
        return online_step(carried, local_queries, key_flat, value_flat, scale)

    row_peak, totals, weighted_sum = fold_keys(
        start_state,
        (
            lax.all_gather(key_rows, "tok", axis=0, tiled=True),
            lax.all_gather(value_rows, "tok", axis=0, tiled=True),
        ),
    )
    attended = (weighted_sum / totals[:, :, None]).astype(jnp.bfloat16)
    attended_grid = attended.reshape(queries.shape)
    owned = lax.all_to_all(attended_grid, "heads", split_axis=1, concat_axis=3, tiled=True)
    attention_out = jnp.einsum(
        "tzxe,ed->ztxd",
        owned,
        lax.all_gather(w_out, "heads", axis=0, tiled=True),
        preferred_element_type=jnp.float32,
    )
    encoded = (residual.astype(jnp.float32) + attention_out).astype(jnp.bfloat16)
    tiled = lax.all_to_all(encoded, "tok", split_axis=2, concat_axis=1, tiled=True)
    neck_feats = jnp.einsum(
        "ztxd,dc->ztxc", tiled, w_neck, preferred_element_type=jnp.float32
    ).astype(jnp.bfloat16)
    extent = neck_feats.shape[:3]
    channels = w_neck.shape[1]
    cell_count = extent[0] * extent[1] * extent[2]
    hidden_one = conv_apply(neck_feats, w_first, False)
    active_one = jax.nn.silu(hidden_one).astype(jnp.bfloat16)
    hidden_two = conv_apply(active_one.reshape(extent + (channels,)), w_second, False)
    active_two = jax.nn.silu(hidden_two).astype(jnp.bfloat16)
    logits = jnp.dot(active_two, w_class, preferred_element_type=jnp.float32)
    probability = jax.nn.sigmoid(logits)
    fault_mask = labels.reshape(cell_count).astype(jnp.float32)
    intersection, total_prob, total_fault = lax.psum(
        (jnp.sum(probability * fault_mask), jnp.sum(probability), jnp.sum(fault_mask)),
        ("heads", "tok"),
    )
    dice_denominator = total_prob + total_fault
    dice_loss = 1.0 - 2.0 * intersection / dice_denominator
    cells_all = float(cell_count * lax.axis_size("heads") * lax.axis_size("tok"))
    grad_logits = (
        LOSS_SCALE
        * cells_all
        * -2.0
        * (fault_mask * dice_denominator - intersection)
        / (dice_denominator * dice_denominator)
        * probability
        * (1.0 - probability)
    )
    grad_hidden_two = (
        grad_logits[:, None] * w_class.astype(jnp.float32)[None, :] * silu_slope(hidden_two)
    ).astype(jnp.bfloat16)
    grad_active_one = conv_apply(grad_hidden_two.reshape(extent + (channels,)), w_second, True)
    grad_hidden_one = (grad_active_one * silu_slope(hidden_one)).astype(jnp.bfloat16)
    grad_neck = (
        conv_apply(grad_hidden_one.reshape(extent + (channels,)), w_first, True)
        .astype(jnp.bfloat16)
        .reshape(extent + (channels,))
    )
    grad_tiles = jnp.einsum(
        "ztxc,dc->ztxd", grad_neck, w_neck, preferred_element_type=jnp.float32
    ).astype(jnp.bfloat16)
    grad_encoded = lax.all_to_all(grad_tiles, "tok", split_axis=1, concat_axis=2, tiled=True)
    return (encoded, dice_loss, grad_encoded)


def dot(a, b):
    return jnp.dot(a, b, preferred_element_type=F32)


def dot_t(a, b):
    return lax.dot_general(a, b, (((1,), (1,)), ((), ())), preferred_element_type=F32)


def sigma_of(v):
    return 1.0 / (1.0 + jnp.exp(-v))


def slope_of(v):
    s = sigma_of(v)
    return s * (1.0 + v * (1.0 - s))


def iota(shape, dim):
    return lax.broadcasted_iota(jnp.int32, shape, dim)


def along_inline(value, step, inline):
    if step == 0:
        return value
    rows = value.shape[0]
    x = iota(value.shape, 0) % inline
    edge = inline - 1 if step > 0 else 0
    return jnp.where(x == edge, 0.0, pltpu.roll(value, (-step) % rows, axis=0))


def along_rows(value, step):
    if step == 0:
        return value
    zeros = jnp.zeros((abs(step), value.shape[1]), value.dtype)
    if step > 0:
        return jnp.concatenate([value[step:], zeros], axis=0)
    return jnp.concatenate([zeros, value[:step]], axis=0)


def place_of(tok_n):
    h, t = lax.axis_index("heads"), lax.axis_index("tok")
    return h, t // 2, t % 2, t


def pack_kernel(tok_n, q_ref, k_ref, v_ref, r_ref, neck_ref, lab_ref, out_ref):
    h, _, _, t = place_of(tok_n)
    rows = q_ref.shape[1] * q_ref.shape[2]
    width = q_ref.shape[3]
    for i, ref in enumerate((q_ref, k_ref, v_ref)):
        flat = ref[...].astype(F32).reshape(rows, width).astype(BF16)
        out_ref[i * rows : (i + 1) * rows, :] = flat
    own = r_ref.shape[0] * r_ref.shape[2]
    residual = r_ref[...].astype(F32).reshape(own, r_ref.shape[3]).astype(BF16)
    out_ref[3 * rows : 3 * rows + own, :] = dot(residual, neck_ref[...]).astype(BF16)
    own_c, _, nt = lab_ref.shape
    spread = jnp.zeros((LABEL_ROWS, width), F32)
    for c in range(own_c):
        row = jnp.broadcast_to(lab_ref[c].astype(F32), (LABEL_ROWS, nt)).astype(BF16)
        at = (h * own_c + c) * nt + iota((nt, width), 0)
        spread = spread + dot(row, (iota((nt, width), 1) == at).astype(F32).astype(BF16))
    out_ref[3 * rows + own :, :] = jnp.where(
        iota((LABEL_ROWS, width), 0) == t, spread, 0.0
    ).astype(BF16)


def weights_kernel(first_ref, second_ref, out_ref, neck_ref, packed_ref, *refs):
    first_in, second_in, first_t, second_t, joint, again, out_w, neck_w, sems = refs
    small = [
        pltpu.make_async_copy(out_ref, out_w, sems.at[6]),
        pltpu.make_async_copy(neck_ref, neck_w, sems.at[7]),
    ]
    for copy in small:
        copy.start()
    copies = []
    for i, (src, dst) in enumerate(((first_ref, first_in), (second_ref, second_in))):
        for a in range(3):
            copies.append(pltpu.make_async_copy(src.at[a], dst.at[a], sems.at[3 * i + a]))
            copies[-1].start()
    again[...] = packed_ref[...]
    for copy in small:
        copy.wait()
    joint[...] = dot(out_w[...], neck_w[...]).astype(BF16)
    for i, (src, dst) in enumerate(((first_in, first_t), (second_in, second_t))):
        for a in range(3):
            copies[3 * i + a].wait()
            for b in range(3):
                for e in range(3):
                    dst[a, b, e] = src[a, b, e].T


def far_first(zs):
    return [0, 1] + list(range(zs - 1, 1, -1))


def attention_kernel(tok_n, zs, rows, own, *refs):
    order = far_first(zs)
    ours = [refs[order.index(d)] for d in range(zs)]
    theirs = [refs[zs + order.index(d)] for d in range(zs)]
    out_w, joint_w = refs[2 * zs : 2 + 2 * zs]
    part_refs = refs[2 + 2 * zs : -4]
    qq, kk, vv, part = refs[-4:]
    h, z, core, _ = place_of(tok_n)
    width = qq.shape[1]
    queries_n = qq.shape[0]
    labels = jnp.zeros((LABEL_ROWS, width), F32)
    for d in range(zs):
        qq[d * rows : (d + 1) * rows, :] = ours[d][0:rows, :]
        for ref, side in ((ours[d], core), (theirs[d], 1 - core)):
            at = pl.multiple_of((2 * (z ^ d) + side) * rows, rows)
            kk[pl.ds(at, rows), :] = ref[rows : 2 * rows, :]
            vv[pl.ds(at, rows), :] = ref[2 * rows : 3 * rows, :]
            labels = labels + ref[3 * rows + own :, :].astype(F32)
    heads_here = width // HD
    scale = HD ** (-0.5)
    query = qq[...]
    keys, values = kk[...], vv[...]
    lane_head = iota((queries_n, width), 1) // HD
    attended = jnp.zeros((queries_n, width), F32)
    for head in range(heads_here):
        mine = lane_head == head
        scores = dot_t(jnp.where(mine, query, jnp.zeros_like(query)), keys) * scale
        raw = jnp.exp(scores - jnp.max(scores, axis=1, keepdims=True))
        total = jnp.sum(raw, axis=1, keepdims=True)
        mixed = dot(raw.astype(BF16), values)
        attended = jnp.where(mine, mixed / total, attended)
    attended = attended.astype(BF16)
    part[...] = dot(attended, joint_w[...])
    for d in range(zs):
        at = pl.multiple_of(d * rows + h * own, own)
        part[pl.ds(at, own), :] += ours[d][3 * rows : 3 * rows + own, :].astype(F32)
    partial = part[...].astype(BF16)
    labels = labels.astype(BF16)
    first = dot(attended[0:rows, :], out_w[...])
    blocks = [first[i * own : (i + 1) * own, :] for i in range(rows // own)]
    for d, ref in enumerate(part_refs):
        ref[0:queries_n, :] = partial
        ref[queries_n : queries_n + LABEL_ROWS, :] = labels
        picked = blocks[0]
        for i in range(1, len(blocks)):
            picked = jnp.where((h ^ d) == i, blocks[i], picked)
        for i in range(picked.shape[1] // width):
            at = queries_n + LABEL_ROWS + i * own
            ref[at : at + own, :] = picked[:, i * width : (i + 1) * width].astype(BF16)


def decoder_kernel(sizes, *refs):
    nc, nt, ni, own_c, zs, tok_n, parts_n = sizes
    ours, theirs, r_ref, w1, w2, w1_t, w2_t, class_w, neck_w = refs[:9]
    parts = refs[9 : 9 + parts_n]
    encoded_ref, loss_ref, grad_ref, grid, cols, slope1, grad2, cols3, hid1, hid2 = refs[9 + parts_n :]
    channels = grid.shape[2]
    slab = nt * ni
    rows = nc * ni
    cells = nc * slab
    h, z, core, tslab = place_of(tok_n)
    taps = 9
    for d in range(zs):
        for ref, side in ((ours, core), (theirs, 1 - core)):
            block = ref[d * rows : (d + 1) * rows, :].astype(F32)
            at = pl.multiple_of((2 * (z ^ d) + side) * ni, ni)
            for c in range(nc):
                grid[c, pl.ds(at, ni), :] = block[c * ni : (c + 1) * ni, :]

    slope1[...] = jnp.zeros_like(slope1)
    grad2[...] = jnp.zeros_like(grad2)
    edge = jnp.zeros((slab, taps * channels), BF16)
    cols[0:slab, :] = edge
    cols[(nc + 1) * slab :, :] = edge

    def spread(value, c):
        for e in range(3):
            moved = along_inline(value, e - 1, ni)
            for b in range(3):
                lane = (b * 3 + e) * channels
                cols[(c + 1) * slab : (c + 2) * slab, lane : lane + channels] = along_rows(
                    moved, (b - 1) * ni
                ).astype(BF16)

    def conv(weights, out):
        for m in range(0, cells, TILE):
            total = None
            for a in range(3):
                matrix = weights[a].reshape(taps * channels, channels)
                term = dot(cols[a * slab + m : a * slab + m + TILE, :], matrix)
                total = term if total is None else total + term
            out[m : m + TILE, :] = total

    for c in range(nc):
        spread(grid[c], c)
    conv(w1, hid1)
    for c in range(nc):
        v = hid1[c * slab : (c + 1) * slab, :]
        s = sigma_of(v)
        slope1[c + 1, ni : ni + slab, :] = s * (1.0 + v * (1.0 - s))
        spread((v * s).astype(BF16).astype(F32), c)
    conv(w2, hid2)
    hidden_two = hid2[...]
    sigma_two = sigma_of(hidden_two)
    active_two = (hidden_two * sigma_two).astype(BF16)
    class_row = class_w[...].astype(F32).reshape(1, channels)
    logits = dot_t(active_two, jnp.broadcast_to(class_row, (128, channels)).astype(BF16))
    probability = sigma_of(logits)
    lab = ours[rows * zs : rows * zs + ni, 0:128].astype(F32)
    spread_lab = jnp.broadcast_to(lab[None], (cells // ni, ni, 128)).reshape(cells, 128)
    wanted = iota((cells, 128), 0) // ni
    picked = jnp.where(iota((cells, 128), 1) == wanted, spread_lab, 0.0).astype(BF16)
    mask = dot(picked, jnp.ones((128, 128), BF16))
    intersection = jnp.sum(probability * mask, axis=0, keepdims=True)
    total_prob = jnp.sum(probability, axis=0, keepdims=True)
    total_fault = jnp.sum(mask, axis=0, keepdims=True)
    denominator = total_prob + total_fault
    loss_ref[...] = 1.0 - 2.0 * intersection / denominator
    grad_logits = (
        LOSS_SCALE
        * float(cells)
        * -2.0
        * (mask * denominator - intersection)
        / (denominator * denominator)
        * probability
        * (1.0 - probability)
    )
    wide = jnp.concatenate([grad_logits] * (channels // 128), axis=1)
    slope_two = sigma_two * (1.0 + hidden_two * (1.0 - sigma_two))
    g2 = wide * class_row * slope_two
    for c in range(nc):
        grad2[c + 2, 2 * ni : 2 * ni + slab, :] = g2[c * slab : (c + 1) * slab, :]

    band = 4 * ni
    c0 = h * own_c
    t0 = pl.multiple_of(tslab * ni, ni)
    for i in range(own_c + 4):
        region = grad2[c0 + i, pl.ds(t0, band + 2 * ni), :]
        for e in range(3):
            moved = along_inline(region, 1 - e, ni)
            for b in range(3):
                lane = (b * 3 + e) * channels
                cols3[i * band : (i + 1) * band, lane : lane + channels] = moved[
                    (2 - b) * ni : (2 - b) * ni + band, :
                ].astype(BF16)
    out3 = (own_c + 2) * band
    total = jnp.zeros((out3, channels), F32)
    for a in range(3):
        for b in range(3):
            for e in range(3):
                lane = (b * 3 + e) * channels
                piece = cols3[(2 - a) * band : (2 - a) * band + out3, lane : lane + channels]
                total = total + dot(piece, w2_t[a, b, e])
    slopes = [slope1[c0 + i, pl.ds(t0, band), :] for i in range(own_c + 2)]
    g1 = (total * jnp.concatenate(slopes, axis=0)).astype(BF16).astype(F32)
    shifted = [along_inline(g1, 1 - e, ni) for e in range(3)]
    total = jnp.zeros((own_c * ni, channels), F32)
    for a in range(3):
        pieces = []
        for b in range(3):
            for e in range(3):
                cells_in = [
                    shifted[e][(i + 2 - a) * band + (2 - b) * ni : (i + 2 - a) * band + (3 - b) * ni, :]
                    for i in range(own_c)
                ]
                pieces.append(jnp.concatenate(cells_in, axis=0).astype(BF16))
        matrix = w1_t[a].reshape(taps * channels, channels)
        total = total + dot(jnp.concatenate(pieces, axis=1), matrix)
    grad = dot_t(total.astype(BF16), neck_w[...])
    grad_ref[...] = grad.reshape(grad_ref.shape).astype(BF16)

    own = own_c * ni
    width = parts[0].shape[1]
    base = rows * zs + LABEL_ROWS
    for i in range(r_ref.shape[3] // width):
        terms = [ref[base + i * own : base + (i + 1) * own, :].astype(F32) for ref in parts]
        total = pairwise(terms).reshape(own_c, 1, ni, width)
        lanes = slice(i * width, (i + 1) * width)
        encoded_ref[:, :, :, lanes] = (r_ref[:, :, :, lanes].astype(F32) + total).astype(BF16)


def pairwise(values):
    while len(values) > 1:
        values = [values[i] + values[i + 1] for i in range(0, len(values), 2)]
    return values[0]


def vmem():
    return pl.BlockSpec(memory_space=pltpu.VMEM)


def hbm():
    return pl.BlockSpec(memory_space=pltpu.HBM)


def whole_grid(
    queries, key_rows, value_rows, residual, w_out, w_neck, w_first, w_second, w_class, labels
):
    heads_n, tok_n = lax.axis_size("heads"), lax.axis_size("tok")
    zs = tok_n // 2
    _, nc, ni, width = queries.shape
    own_c = residual.shape[0]
    nt = labels.shape[1]
    channels = w_neck.shape[1]
    rows, own = nc * ni, own_c * ni

    def swap_tok(value, bits):
        return lax.ppermute(value, "tok", [(i, i ^ bits) for i in range(tok_n)])

    def swap_heads(value, bits):
        return lax.ppermute(value, "heads", [(i, i ^ bits) for i in range(heads_n)])

    packed = pl.pallas_call(
        functools.partial(pack_kernel, tok_n),
        out_shape=pltpu.VMEM((3 * rows + own + LABEL_ROWS, width), BF16),
        in_specs=[vmem()] * 6,
        out_specs=vmem(),
    )(queries, key_rows, value_rows, residual, w_neck, labels.transpose(0, 2, 1))
    ours = [packed] + [swap_tok(packed, 2 * d) for d in range(1, zs)]
    kept = [pltpu.with_memory_space_constraint(w, pltpu.HBM) for w in (w_first, w_second, w_out, w_neck)]
    first_in, second_in, first_t, second_t, joint, again, out_w, neck_w = pl.pallas_call(
        weights_kernel,
        out_shape=[pltpu.VMEM(w_first.shape, BF16)] * 4
        + [
            pltpu.VMEM((width, channels), BF16),
            pltpu.VMEM(packed.shape, BF16),
            pltpu.VMEM(w_out.shape, BF16),
            pltpu.VMEM(w_neck.shape, BF16),
        ],
        in_specs=[hbm()] * 4 + [vmem()],
        out_specs=[vmem()] * 8,
        scratch_shapes=[pltpu.SemaphoreType.DMA((8,))],
        compiler_params=pltpu.CompilerParams(vmem_limit_bytes=24 * 2**20),
        cost_estimate=pl.CostEstimate(flops=0, bytes_accessed=28 * 2**20, transcendentals=0),
    )(*kept, packed)
    theirs = [swap_tok(value, 1) for value in [again] + ours[1:]]
    order = far_first(zs)
    queries_n, keys_n = rows * zs, rows * tok_n
    enc_rows = own * residual.shape[3] // width
    part_shape = pltpu.VMEM((queries_n + LABEL_ROWS + enc_rows, channels), BF16)
    sent = pl.pallas_call(
        functools.partial(attention_kernel, tok_n, zs, rows, own),
        out_shape=[part_shape] * heads_n,
        in_specs=[vmem()] * (2 * zs + 2),
        out_specs=[vmem()] * heads_n,
        scratch_shapes=[
            pltpu.VMEM((queries_n, width), BF16),
            pltpu.VMEM((keys_n, width), BF16),
            pltpu.VMEM((keys_n, width), BF16),
            pltpu.VMEM((queries_n, channels), F32),
        ],
        compiler_params=pltpu.CompilerParams(vmem_limit_bytes=16 * 2**20),
    )(*[ours[d] for d in order], *[theirs[d] for d in order], out_w, joint)
    parts = [swap_heads(sent[d], d) for d in range(heads_n - 1, 0, -1)] + [sent[0]]
    used = queries_n + LABEL_ROWS
    half = pairwise([part[:used].astype(F32) for part in parts]).astype(BF16)
    other = swap_tok(half, 1)
    slab = nt * ni
    return tuple(
        pl.pallas_call(
            functools.partial(decoder_kernel, (nc, nt, ni, own_c, zs, tok_n, heads_n)),
            out_shape=[
                jax.ShapeDtypeStruct(residual.shape, BF16),
                jax.ShapeDtypeStruct((1, 128), F32),
                jax.ShapeDtypeStruct(residual.shape, BF16),
            ],
            in_specs=[vmem()] * (9 + heads_n),
            out_specs=[vmem()] * 3,
            scratch_shapes=[
                pltpu.VMEM((nc, slab, channels), F32),
                pltpu.VMEM(((nc + 2) * slab, 9 * channels), BF16),
                pltpu.VMEM((nc + 2, (nt + 4) * ni, channels), F32),
                pltpu.VMEM((nc + 4, (nt + 6) * ni, channels), F32),
                pltpu.VMEM(((own_c + 4) * 4 * ni, 9 * channels), BF16),
                pltpu.VMEM((nc * slab, channels), F32),
                pltpu.VMEM((nc * slab, channels), F32),
            ],
            compiler_params=pltpu.CompilerParams(vmem_limit_bytes=36 * 2**20),
        )(half, other, residual, first_in, second_in, first_t, second_t, w_class, neck_w, *parts)
    )


def power_of_two(n):
    return n > 0 and n & (n - 1) == 0


def fits_whole(queries, residual, w_neck, labels):
    heads_n, tok_n = lax.axis_size("heads"), lax.axis_size("tok")
    slabs, nc, ni, width = queries.shape
    nt = labels.shape[1]
    return (
        slabs == 1
        and nc * nt <= 128
        and labels.shape[2] == 1
        and ni == 8
        and nt == tok_n
        and tok_n >= 4
        and power_of_two(tok_n)
        and power_of_two(heads_n)
        and residual.shape[0] * heads_n == nc
        and nc * nt * ni <= 1024
        and (nc * nt * ni) % TILE == 0
        and width % 128 == 0
        and w_neck.shape[1] == width
        and (residual.shape[0] * ni) % 16 == 0
    )


def on_device(*arguments):
    queries, residual, w_neck, labels = (arguments[i] for i in (0, 3, 5, 9))
    if fits_whole(queries, residual, w_neck, labels):
        encoded, loss, grad = whole_grid(*arguments)
        return (encoded, loss[0, 0], grad)
    return on_tiles(*arguments)


def solution(mesh):
    placed = (
        P("tok", None, None, "heads"),
        P("tok", None, None, "heads"),
        P("tok", None, None, "heads"),
        P("heads", "tok", None, None),
        P("heads", None),
        P(),
        P(),
        P(),
        P(),
        P("heads", None, "tok"),
    )
    return jax.shard_map(
        on_device,
        mesh=mesh,
        in_specs=placed,
        out_specs=(P("heads", "tok", None, None), P(), P("heads", "tok", None, None)),
        check_vma=False,
    )
```

```python
import functools

import jax
import jax.numpy as jnp
from jax import lax
from jax.experimental import pallas as pl
from jax.experimental.pallas import tpu as pltpu
from jax.sharding import PartitionSpec as P

HD = 64
F32 = jnp.float32
BF16 = jnp.bfloat16
LABEL_ROWS = 16
TILE = 256


OFFSETS = [
    (along_c, along_t, along_x)
    for along_c in range(3)
    for along_t in range(3)
    for along_x in range(3)
]
LOSS_SCALE = 64.0
NEG_LARGE = -1e30


def padded_2(value, sides, width):
    for axis, dim in sides:
        size, length = (lax.axis_size(axis), value.shape[dim])
        up = [(i, (i + 1) % size) for i in range(size - 1)]
        down = [(j, i) for i, j in up]
        last = lax.slice_in_dim(value, length - width, length, axis=dim)
        first = lax.slice_in_dim(value, 0, width, axis=dim)
        before = lax.ppermute(last, axis, up)
        after = lax.ppermute(first, axis, down)
        value = jnp.concatenate([before, value, after], axis=dim)
    return value


def silu_slope(volume):
    sigma = jax.nn.sigmoid(volume)
    return sigma * (1.0 + volume * (1.0 - sigma))


def with_rims(volume):
    padded = padded_2(volume, (("heads", 0), ("tok", 2)), 1)
    return jnp.pad(padded, ((0, 0), (1, 1), (0, 0), (0, 0)))


def conv_apply(volume, weights, flipped):
    extent = volume.shape[:3]
    padded = with_rims(volume)
    pieces = []
    for along_c, along_t, along_x in OFFSETS:
        if flipped:
            anchor = (2 - along_c, 2 - along_t, 2 - along_x)
        else:
            anchor = (along_c, along_t, along_x)
        pieces.append(
            padded[
                anchor[0] : anchor[0] + extent[0],
                anchor[1] : anchor[1] + extent[1],
                anchor[2] : anchor[2] + extent[2],
            ]
        )
    stacked = jnp.stack(pieces, axis=3)
    columns = stacked.reshape(extent[0] * extent[1] * extent[2], 27, volume.shape[3])
    kernel = weights.reshape(27, weights.shape[3], weights.shape[4])
    if flipped:
        contraction = (((1, 2), (0, 2)), ((), ()))
    else:
        contraction = (((1, 2), (0, 1)), ((), ()))
    return lax.dot_general(columns, kernel, contraction, preferred_element_type=jnp.float32)


def online_step(carried, query_block, key_block, value_block, scale):
    row_peak, totals, weighted_sum = carried
    scores = (
        jnp.einsum("qhd,khd->qhk", query_block, key_block, preferred_element_type=jnp.float32)
        * scale
    )
    new_peak = jnp.maximum(row_peak, jnp.max(scores, axis=-1))
    factor = jnp.exp(row_peak - new_peak)
    raw_weights = jnp.exp(scores - new_peak[:, :, None])
    totals = totals * factor + jnp.sum(raw_weights, axis=-1)
    weighted_sum = weighted_sum * factor[:, :, None] + jnp.einsum(
        "qhk,khd->qhd",
        raw_weights.astype(jnp.bfloat16),
        value_block,
        preferred_element_type=jnp.float32,
    )
    return (new_peak, totals, weighted_sum)


def on_tiles(
    queries, key_rows, value_rows, residual, w_out, w_neck, w_first, w_second, w_class, labels
):
    width_here = queries.shape[-1]
    heads_here = width_here // HD
    scale = HD ** (-0.5)
    local_queries = queries.reshape(-1, heads_here, HD)
    query_total = local_queries.shape[0]
    start_state = (
        jnp.full((query_total, heads_here), NEG_LARGE, jnp.float32),
        jnp.zeros((query_total, heads_here), jnp.float32),
        jnp.zeros((query_total, heads_here, HD), jnp.float32),
    )

    def fold_keys(carried, key_piece):
        key_flat = key_piece[0].reshape(-1, heads_here, HD)
        value_flat = key_piece[1].reshape(-1, heads_here, HD)
        key_total = key_flat.shape[0]
        if key_total > 512 and key_total % 512 == 0:
            key_blocks = key_flat.reshape(key_total // 512, 512, heads_here, HD)
            value_blocks = value_flat.reshape(key_total // 512, 512, heads_here, HD)

            def scan_step(inner, paired):
                return (online_step(inner, local_queries, paired[0], paired[1], scale), None)

            return lax.scan(scan_step, carried, (key_blocks, value_blocks))[0]
        return online_step(carried, local_queries, key_flat, value_flat, scale)

    row_peak, totals, weighted_sum = fold_keys(
        start_state,
        (
            lax.all_gather(key_rows, "tok", axis=0, tiled=True),
            lax.all_gather(value_rows, "tok", axis=0, tiled=True),
        ),
    )
    attended = (weighted_sum / totals[:, :, None]).astype(jnp.bfloat16)
    attended_grid = attended.reshape(queries.shape)
    owned = lax.all_to_all(attended_grid, "heads", split_axis=1, concat_axis=3, tiled=True)
    attention_out = jnp.einsum(
        "tzxe,ed->ztxd",
        owned,
        lax.all_gather(w_out, "heads", axis=0, tiled=True),
        preferred_element_type=jnp.float32,
    )
    encoded = (residual.astype(jnp.float32) + attention_out).astype(jnp.bfloat16)
    tiled = lax.all_to_all(encoded, "tok", split_axis=2, concat_axis=1, tiled=True)
    neck_feats = jnp.einsum(
        "ztxd,dc->ztxc", tiled, w_neck, preferred_element_type=jnp.float32
    ).astype(jnp.bfloat16)
    extent = neck_feats.shape[:3]
    channels = w_neck.shape[1]
    cell_count = extent[0] * extent[1] * extent[2]
    hidden_one = conv_apply(neck_feats, w_first, False)
    active_one = jax.nn.silu(hidden_one).astype(jnp.bfloat16)
    hidden_two = conv_apply(active_one.reshape(extent + (channels,)), w_second, False)
    active_two = jax.nn.silu(hidden_two).astype(jnp.bfloat16)
    logits = jnp.dot(active_two, w_class, preferred_element_type=jnp.float32)
    probability = jax.nn.sigmoid(logits)
    fault_mask = labels.reshape(cell_count).astype(jnp.float32)
    intersection, total_prob, total_fault = lax.psum(
        (jnp.sum(probability * fault_mask), jnp.sum(probability), jnp.sum(fault_mask)),
        ("heads", "tok"),
    )
    dice_denominator = total_prob + total_fault
    dice_loss = 1.0 - 2.0 * intersection / dice_denominator
    cells_all = float(cell_count * lax.axis_size("heads") * lax.axis_size("tok"))
    grad_logits = (
        LOSS_SCALE
        * cells_all
        * -2.0
        * (fault_mask * dice_denominator - intersection)
        / (dice_denominator * dice_denominator)
        * probability
        * (1.0 - probability)
    )
    grad_hidden_two = (
        grad_logits[:, None] * w_class.astype(jnp.float32)[None, :] * silu_slope(hidden_two)
    ).astype(jnp.bfloat16)
    grad_active_one = conv_apply(grad_hidden_two.reshape(extent + (channels,)), w_second, True)
    grad_hidden_one = (grad_active_one * silu_slope(hidden_one)).astype(jnp.bfloat16)
    grad_neck = (
        conv_apply(grad_hidden_one.reshape(extent + (channels,)), w_first, True)
        .astype(jnp.bfloat16)
        .reshape(extent + (channels,))
    )
    grad_tiles = jnp.einsum(
        "ztxc,dc->ztxd", grad_neck, w_neck, preferred_element_type=jnp.float32
    ).astype(jnp.bfloat16)
    grad_encoded = lax.all_to_all(grad_tiles, "tok", split_axis=1, concat_axis=2, tiled=True)
    return (encoded, dice_loss, grad_encoded)


def dot(a, b):
    return jnp.dot(a, b, preferred_element_type=F32)


def dot_t(a, b):
    return lax.dot_general(a, b, (((1,), (1,)), ((), ())), preferred_element_type=F32)


def sigma_of(v):
    return 1.0 / (1.0 + jnp.exp(-v))


def slope_of(v):
    s = sigma_of(v)
    return s * (1.0 + v * (1.0 - s))


def iota(shape, dim):
    return lax.broadcasted_iota(jnp.int32, shape, dim)


def along_inline(value, step, inline):
    if step == 0:
        return value
    rows = value.shape[0]
    x = iota(value.shape, 0) % inline
    edge = inline - 1 if step > 0 else 0
    return jnp.where(x == edge, 0.0, pltpu.roll(value, (-step) % rows, axis=0))


def along_rows(value, step):
    if step == 0:
        return value
    zeros = jnp.zeros((abs(step), value.shape[1]), value.dtype)
    if step > 0:
        return jnp.concatenate([value[step:], zeros], axis=0)
    return jnp.concatenate([zeros, value[:step]], axis=0)


def place_of(tok_n):
    h, t = lax.axis_index("heads"), lax.axis_index("tok")
    return h, t // 2, t % 2, t


def pack_kernel(tok_n, q_ref, k_ref, v_ref, r_ref, neck_ref, lab_ref, out_ref):
    h, _, _, t = place_of(tok_n)
    rows = q_ref.shape[1] * q_ref.shape[2]
    width = q_ref.shape[3]
    for i, ref in enumerate((q_ref, k_ref, v_ref)):
        flat = ref[...].astype(F32).reshape(rows, width).astype(BF16)
        out_ref[i * rows : (i + 1) * rows, :] = flat
    own = r_ref.shape[0] * r_ref.shape[2]
    residual = r_ref[...].astype(F32).reshape(own, r_ref.shape[3]).astype(BF16)
    out_ref[3 * rows : 3 * rows + own, :] = dot(residual, neck_ref[...]).astype(BF16)
    own_c, _, nt = lab_ref.shape
    spread = jnp.zeros((LABEL_ROWS, width), F32)
    for c in range(own_c):
        row = jnp.broadcast_to(lab_ref[c].astype(F32), (LABEL_ROWS, nt)).astype(BF16)
        at = (h * own_c + c) * nt + iota((nt, width), 0)
        spread = spread + dot(row, (iota((nt, width), 1) == at).astype(F32).astype(BF16))
    out_ref[3 * rows + own :, :] = jnp.where(
        iota((LABEL_ROWS, width), 0) == t, spread, 0.0
    ).astype(BF16)


def weights_kernel(first_ref, second_ref, out_ref, neck_ref, packed_ref, *refs):
    first_in, second_in, first_t, second_t, joint, again, out_w, neck_w = refs[:8]
    first_mid, second_mid, sems = refs[8:]
    small = [
        pltpu.make_async_copy(out_ref, out_w, sems.at[6]),
        pltpu.make_async_copy(neck_ref, neck_w, sems.at[7]),
    ]
    for copy in small:
        copy.start()
    sets = (
        (first_ref, first_in, first_mid, first_t),
        (second_ref, second_in, second_mid, second_t),
    )
    copies = []
    for i, (src, dst, mid, _) in enumerate(sets):
        for a, place in enumerate((dst.at[0], mid, dst.at[3])):
            copies.append(pltpu.make_async_copy(src.at[a], place, sems.at[3 * i + a]))
            copies[-1].start()
    again[...] = packed_ref[...]
    for copy in small:
        copy.wait()
    joint[...] = dot(out_w[...], neck_w[...]).astype(BF16)
    for i, (_, dst, mid, flipped) in enumerate(sets):
        for a in range(3):
            copies[3 * i + a].wait()
        for b in range(3):
            for e in range(3):
                taps = (dst[0, b, e], mid[b, e], dst[3, b, e])
                for a in range(3):
                    flipped[a, b, e] = taps[a].T
                g0, g1, g2 = (tap.astype(F32) * 0.5 for tap in taps)
                dst[1, b, e] = (g0 + g2 + g1).astype(BF16)
                dst[2, b, e] = (g0 + g2 - g1).astype(BF16)


def far_first(zs):
    return [0, 1] + list(range(zs - 1, 1, -1))


def attention_kernel(tok_n, zs, rows, own, *refs):
    order = far_first(zs)
    ours = [refs[order.index(d)] for d in range(zs)]
    theirs = [refs[zs + order.index(d)] for d in range(zs)]
    out_w, joint_w = refs[2 * zs : 2 + 2 * zs]
    part_refs = refs[2 + 2 * zs : -4]
    qq, kk, vv, part = refs[-4:]
    h, z, core, _ = place_of(tok_n)
    width = qq.shape[1]
    queries_n = qq.shape[0]
    labels = jnp.zeros((LABEL_ROWS, width), F32)
    for d in range(zs):
        qq[d * rows : (d + 1) * rows, :] = ours[d][0:rows, :]
        for ref, side in ((ours[d], core), (theirs[d], 1 - core)):
            at = pl.multiple_of((2 * (z ^ d) + side) * rows, rows)
            kk[pl.ds(at, rows), :] = ref[rows : 2 * rows, :]
            vv[pl.ds(at, rows), :] = ref[2 * rows : 3 * rows, :]
            labels = labels + ref[3 * rows + own :, :].astype(F32)
    heads_here = width // HD
    scale = HD ** (-0.5)
    query = qq[...]
    keys, values = kk[...], vv[...]
    lane_head = iota((queries_n, width), 1) // HD
    attended = jnp.zeros((queries_n, width), F32)
    for head in range(heads_here):
        mine = lane_head == head
        scores = dot_t(jnp.where(mine, query, jnp.zeros_like(query)), keys) * scale
        raw = jnp.exp(scores - jnp.max(scores, axis=1, keepdims=True))
        total = jnp.sum(raw, axis=1, keepdims=True)
        mixed = dot(raw.astype(BF16), values)
        attended = jnp.where(mine, mixed / total, attended)
    attended = attended.astype(BF16)
    part[...] = dot(attended, joint_w[...])
    for d in range(zs):
        at = pl.multiple_of(d * rows + h * own, own)
        part[pl.ds(at, own), :] += ours[d][3 * rows : 3 * rows + own, :].astype(F32)
    partial = part[...].astype(BF16)
    labels = labels.astype(BF16)
    first = dot(attended[0:rows, :], out_w[...])
    blocks = [first[i * own : (i + 1) * own, :] for i in range(rows // own)]
    for d, ref in enumerate(part_refs):
        ref[0:queries_n, :] = partial
        ref[queries_n : queries_n + LABEL_ROWS, :] = labels
        picked = blocks[0]
        for i in range(1, len(blocks)):
            picked = jnp.where((h ^ d) == i, blocks[i], picked)
        for i in range(picked.shape[1] // width):
            at = queries_n + LABEL_ROWS + i * own
            ref[at : at + own, :] = picked[:, i * width : (i + 1) * width].astype(BF16)


def decoder_kernel(sizes, *refs):
    nc, nt, ni, own_c, zs, tok_n, parts_n = sizes
    ours, theirs, r_ref, w1, w2, w1_t, w2_t, class_w, neck_w = refs[:9]
    parts = refs[9 : 9 + parts_n]
    encoded_ref, loss_ref, grad_ref, grid, cols, slope1, grad2, cols3, hid1, hid2, parts_out = refs[9 + parts_n :]
    channels = grid.shape[2]
    slab = nt * ni
    rows = nc * ni
    cells = nc * slab
    h, z, core, tslab = place_of(tok_n)
    taps = 9
    for d in range(zs):
        for ref, side in ((ours, core), (theirs, 1 - core)):
            block = ref[d * rows : (d + 1) * rows, :].astype(F32)
            at = pl.multiple_of((2 * (z ^ d) + side) * ni, ni)
            for c in range(nc):
                grid[c, pl.ds(at, ni), :] = block[c * ni : (c + 1) * ni, :]

    slope1[...] = jnp.zeros_like(slope1)
    grad2[...] = jnp.zeros_like(grad2)
    def spread(value, k, i):
        for e in range(3):
            moved = along_inline(value, e - 1, ni)
            for b in range(3):
                lane = (b * 3 + e) * channels
                cols[k, i * slab : (i + 1) * slab, lane : lane + channels] = along_rows(
                    moved, (b - 1) * ni
                ).astype(BF16)

    def spread_all(volume):
        empty = jnp.zeros((slab, channels), F32)
        for i in range(nc // 2):
            d0 = volume[2 * i - 1] if i > 0 else empty
            d1, d2 = volume[2 * i], volume[2 * i + 1]
            d3 = volume[2 * i + 2] if 2 * i + 2 < nc else empty
            for k, value in enumerate((d0 - d2, d1 + d2, d2 - d1, d1 - d3)):
                spread(value, k, i)

    half_cells = cells // 2

    def conv(weights, out):
        for k in range(4):
            matrix = weights[k].reshape(taps * channels, channels)
            for m in range(0, half_cells, TILE):
                parts_out[k, m : m + TILE, :] = dot(cols[k, m : m + TILE, :], matrix)
        for i in range(nc // 2):
            m0, m1, m2, m3 = (parts_out[k, i * slab : (i + 1) * slab, :] for k in range(4))
            out[2 * i * slab : (2 * i + 1) * slab, :] = m0 + m1 + m2
            out[(2 * i + 1) * slab : (2 * i + 2) * slab, :] = m1 - m2 - m3

    spread_all([grid[c] for c in range(nc)])
    conv(w1, hid1)
    for c in range(nc):
        v = hid1[c * slab : (c + 1) * slab, :]
        s = sigma_of(v)
        slope1[c + 1, ni : ni + slab, :] = s * (1.0 + v * (1.0 - s))
        grid[c] = (v * s).astype(BF16).astype(F32)
    spread_all([grid[c] for c in range(nc)])
    conv(w2, hid2)
    hidden_two = hid2[...]
    sigma_two = sigma_of(hidden_two)
    active_two = (hidden_two * sigma_two).astype(BF16)
    class_row = class_w[...].astype(F32).reshape(1, channels)
    logits = dot_t(active_two, jnp.broadcast_to(class_row, (128, channels)).astype(BF16))
    probability = sigma_of(logits)
    lab = ours[rows * zs : rows * zs + ni, 0:128].astype(F32)
    spread_lab = jnp.broadcast_to(lab[None], (cells // ni, ni, 128)).reshape(cells, 128)
    wanted = iota((cells, 128), 0) // ni
    picked = jnp.where(iota((cells, 128), 1) == wanted, spread_lab, 0.0).astype(BF16)
    mask = dot(picked, jnp.ones((128, 128), BF16))
    intersection = jnp.sum(probability * mask, axis=0, keepdims=True)
    total_prob = jnp.sum(probability, axis=0, keepdims=True)
    total_fault = jnp.sum(mask, axis=0, keepdims=True)
    denominator = total_prob + total_fault
    loss_ref[...] = 1.0 - 2.0 * intersection / denominator
    grad_logits = (
        LOSS_SCALE
        * float(cells)
        * -2.0
        * (mask * denominator - intersection)
        / (denominator * denominator)
        * probability
        * (1.0 - probability)
    )
    wide = jnp.concatenate([grad_logits] * (channels // 128), axis=1)
    slope_two = sigma_two * (1.0 + hidden_two * (1.0 - sigma_two))
    g2 = wide * class_row * slope_two
    for c in range(nc):
        grad2[c + 2, 2 * ni : 2 * ni + slab, :] = g2[c * slab : (c + 1) * slab, :]

    band = 4 * ni
    c0 = h * own_c
    t0 = pl.multiple_of(tslab * ni, ni)
    for i in range(own_c + 4):
        region = grad2[c0 + i, pl.ds(t0, band + 2 * ni), :]
        for e in range(3):
            moved = along_inline(region, 1 - e, ni)
            for b in range(3):
                lane = (b * 3 + e) * channels
                cols3[i * band : (i + 1) * band, lane : lane + channels] = moved[
                    (2 - b) * ni : (2 - b) * ni + band, :
                ].astype(BF16)
    out3 = (own_c + 2) * band
    total = jnp.zeros((out3, channels), F32)
    for a in range(3):
        for b in range(3):
            for e in range(3):
                lane = (b * 3 + e) * channels
                piece = cols3[(2 - a) * band : (2 - a) * band + out3, lane : lane + channels]
                total = total + dot(piece, w2_t[a, b, e])
    slopes = [slope1[c0 + i, pl.ds(t0, band), :] for i in range(own_c + 2)]
    g1 = (total * jnp.concatenate(slopes, axis=0)).astype(BF16).astype(F32)
    shifted = [along_inline(g1, 1 - e, ni) for e in range(3)]
    total = jnp.zeros((own_c * ni, channels), F32)
    for a in range(3):
        pieces = []
        for b in range(3):
            for e in range(3):
                cells_in = [
                    shifted[e][(i + 2 - a) * band + (2 - b) * ni : (i + 2 - a) * band + (3 - b) * ni, :]
                    for i in range(own_c)
                ]
                pieces.append(jnp.concatenate(cells_in, axis=0).astype(BF16))
        matrix = w1_t[a].reshape(taps * channels, channels)
        total = total + dot(jnp.concatenate(pieces, axis=1), matrix)
    grad = dot_t(total.astype(BF16), neck_w[...])
    grad_ref[...] = grad.reshape(grad_ref.shape).astype(BF16)

    own = own_c * ni
    width = parts[0].shape[1]
    base = rows * zs + LABEL_ROWS
    for i in range(r_ref.shape[3] // width):
        terms = [ref[base + i * own : base + (i + 1) * own, :].astype(F32) for ref in parts]
        total = pairwise(terms).reshape(own_c, 1, ni, width)
        lanes = slice(i * width, (i + 1) * width)
        encoded_ref[:, :, :, lanes] = (r_ref[:, :, :, lanes].astype(F32) + total).astype(BF16)


def pairwise(values):
    while len(values) > 1:
        values = [values[i] + values[i + 1] for i in range(0, len(values), 2)]
    return values[0]


def vmem():
    return pl.BlockSpec(memory_space=pltpu.VMEM)


def hbm():
    return pl.BlockSpec(memory_space=pltpu.HBM)


def whole_grid(
    queries, key_rows, value_rows, residual, w_out, w_neck, w_first, w_second, w_class, labels
):
    heads_n, tok_n = lax.axis_size("heads"), lax.axis_size("tok")
    zs = tok_n // 2
    _, nc, ni, width = queries.shape
    own_c = residual.shape[0]
    nt = labels.shape[1]
    channels = w_neck.shape[1]
    rows, own = nc * ni, own_c * ni

    def swap_tok(value, bits):
        return lax.ppermute(value, "tok", [(i, i ^ bits) for i in range(tok_n)])

    def swap_heads(value, bits):
        return lax.ppermute(value, "heads", [(i, i ^ bits) for i in range(heads_n)])

    packed = pl.pallas_call(
        functools.partial(pack_kernel, tok_n),
        out_shape=pltpu.VMEM((3 * rows + own + LABEL_ROWS, width), BF16),
        in_specs=[vmem()] * 6,
        out_specs=vmem(),
    )(queries, key_rows, value_rows, residual, w_neck, labels.transpose(0, 2, 1))
    ours = [packed] + [swap_tok(packed, 2 * d) for d in range(1, zs)]
    kept = [pltpu.with_memory_space_constraint(w, pltpu.HBM) for w in (w_first, w_second, w_out, w_neck)]
    first_in, second_in, first_t, second_t, joint, again, out_w, neck_w = pl.pallas_call(
        weights_kernel,
        out_shape=[pltpu.VMEM((4,) + w_first.shape[1:], BF16)] * 2
        + [pltpu.VMEM(w_first.shape, BF16)] * 2
        + [
            pltpu.VMEM((width, channels), BF16),
            pltpu.VMEM(packed.shape, BF16),
            pltpu.VMEM(w_out.shape, BF16),
            pltpu.VMEM(w_neck.shape, BF16),
        ],
        in_specs=[hbm()] * 4 + [vmem()],
        out_specs=[vmem()] * 8,
        scratch_shapes=[pltpu.VMEM(w_first.shape[1:], BF16)] * 2 + [pltpu.SemaphoreType.DMA((8,))],
        compiler_params=pltpu.CompilerParams(vmem_limit_bytes=24 * 2**20),
        cost_estimate=pl.CostEstimate(flops=0, bytes_accessed=28 * 2**20, transcendentals=0),
    )(*kept, packed)
    theirs = [swap_tok(value, 1) for value in [again] + ours[1:]]
    order = far_first(zs)
    queries_n, keys_n = rows * zs, rows * tok_n
    enc_rows = own * residual.shape[3] // width
    part_shape = pltpu.VMEM((queries_n + LABEL_ROWS + enc_rows, channels), BF16)
    sent = pl.pallas_call(
        functools.partial(attention_kernel, tok_n, zs, rows, own),
        out_shape=[part_shape] * heads_n,
        in_specs=[vmem()] * (2 * zs + 2),
        out_specs=[vmem()] * heads_n,
        scratch_shapes=[
            pltpu.VMEM((queries_n, width), BF16),
            pltpu.VMEM((keys_n, width), BF16),
            pltpu.VMEM((keys_n, width), BF16),
            pltpu.VMEM((queries_n, channels), F32),
        ],
        compiler_params=pltpu.CompilerParams(vmem_limit_bytes=16 * 2**20),
    )(*[ours[d] for d in order], *[theirs[d] for d in order], out_w, joint)
    parts = [swap_heads(sent[d], d) for d in range(heads_n - 1, 0, -1)] + [sent[0]]
    used = queries_n + LABEL_ROWS
    half = pairwise([part[:used].astype(F32) for part in parts]).astype(BF16)
    other = swap_tok(half, 1)
    slab = nt * ni
    return tuple(
        pl.pallas_call(
            functools.partial(decoder_kernel, (nc, nt, ni, own_c, zs, tok_n, heads_n)),
            out_shape=[
                jax.ShapeDtypeStruct(residual.shape, BF16),
                jax.ShapeDtypeStruct((1, 128), F32),
                jax.ShapeDtypeStruct(residual.shape, BF16),
            ],
            in_specs=[vmem()] * (9 + heads_n),
            out_specs=[vmem()] * 3,
            scratch_shapes=[
                pltpu.VMEM((nc, slab, channels), F32),
                pltpu.VMEM((4, nc // 2 * slab, 9 * channels), BF16),
                pltpu.VMEM((nc + 2, (nt + 4) * ni, channels), F32),
                pltpu.VMEM((nc + 4, (nt + 6) * ni, channels), F32),
                pltpu.VMEM(((own_c + 4) * 4 * ni, 9 * channels), BF16),
                pltpu.VMEM((nc * slab, channels), F32),
                pltpu.VMEM((nc * slab, channels), F32),
                pltpu.VMEM((4, nc // 2 * slab, channels), F32),
            ],
            compiler_params=pltpu.CompilerParams(vmem_limit_bytes=36 * 2**20),
        )(half, other, residual, first_in, second_in, first_t, second_t, w_class, neck_w, *parts)
    )


def power_of_two(n):
    return n > 0 and n & (n - 1) == 0


def fits_whole(queries, residual, w_neck, labels):
    heads_n, tok_n = lax.axis_size("heads"), lax.axis_size("tok")
    slabs, nc, ni, width = queries.shape
    nt = labels.shape[1]
    return (
        slabs == 1
        and nc * nt <= 128
        and labels.shape[2] == 1
        and ni == 8
        and nt == tok_n
        and tok_n >= 4
        and power_of_two(tok_n)
        and power_of_two(heads_n)
        and residual.shape[0] * heads_n == nc
        and nc * nt * ni <= 1024
        and (nc // 2 * nt * ni) % TILE == 0
        and nc % 2 == 0
        and width % 128 == 0
        and w_neck.shape[1] == width
        and (residual.shape[0] * ni) % 16 == 0
    )


def on_device(*arguments):
    queries, residual, w_neck, labels = (arguments[i] for i in (0, 3, 5, 9))
    if fits_whole(queries, residual, w_neck, labels):
        encoded, loss, grad = whole_grid(*arguments)
        return (encoded, loss[0, 0], grad)
    return on_tiles(*arguments)


def solution(mesh):
    placed = (
        P("tok", None, None, "heads"),
        P("tok", None, None, "heads"),
        P("tok", None, None, "heads"),
        P("heads", "tok", None, None),
        P("heads", None),
        P(),
        P(),
        P(),
        P(),
        P("heads", None, "tok"),
    )
    return jax.shard_map(
        on_device,
        mesh=mesh,
        in_specs=placed,
        out_specs=(P("heads", "tok", None, None), P(), P("heads", "tok", None, None)),
        check_vma=False,
    )
```

```python
import functools

import jax
import jax.numpy as jnp
from jax import lax
from jax.experimental import pallas as pl
from jax.experimental.pallas import tpu as pltpu
from jax.sharding import PartitionSpec as P

HD = 64
F32 = jnp.float32
BF16 = jnp.bfloat16
LABEL_ROWS = 8
TILE = 256


OFFSETS = [
    (along_c, along_t, along_x)
    for along_c in range(3)
    for along_t in range(3)
    for along_x in range(3)
]
LOSS_SCALE = 64.0
NEG_LARGE = -1e30


def padded_2(value, sides, width):
    for axis, dim in sides:
        size, length = (lax.axis_size(axis), value.shape[dim])
        up = [(i, (i + 1) % size) for i in range(size - 1)]
        down = [(j, i) for i, j in up]
        last = lax.slice_in_dim(value, length - width, length, axis=dim)
        first = lax.slice_in_dim(value, 0, width, axis=dim)
        before = lax.ppermute(last, axis, up)
        after = lax.ppermute(first, axis, down)
        value = jnp.concatenate([before, value, after], axis=dim)
    return value


def silu_slope(volume):
    sigma = jax.nn.sigmoid(volume)
    return sigma * (1.0 + volume * (1.0 - sigma))


def with_rims(volume):
    padded = padded_2(volume, (("heads", 0), ("tok", 2)), 1)
    return jnp.pad(padded, ((0, 0), (1, 1), (0, 0), (0, 0)))


def conv_apply(volume, weights, flipped):
    extent = volume.shape[:3]
    padded = with_rims(volume)
    pieces = []
    for along_c, along_t, along_x in OFFSETS:
        if flipped:
            anchor = (2 - along_c, 2 - along_t, 2 - along_x)
        else:
            anchor = (along_c, along_t, along_x)
        pieces.append(
            padded[
                anchor[0] : anchor[0] + extent[0],
                anchor[1] : anchor[1] + extent[1],
                anchor[2] : anchor[2] + extent[2],
            ]
        )
    stacked = jnp.stack(pieces, axis=3)
    columns = stacked.reshape(extent[0] * extent[1] * extent[2], 27, volume.shape[3])
    kernel = weights.reshape(27, weights.shape[3], weights.shape[4])
    if flipped:
        contraction = (((1, 2), (0, 2)), ((), ()))
    else:
        contraction = (((1, 2), (0, 1)), ((), ()))
    return lax.dot_general(columns, kernel, contraction, preferred_element_type=jnp.float32)


def online_step(carried, query_block, key_block, value_block, scale):
    row_peak, totals, weighted_sum = carried
    scores = (
        jnp.einsum("qhd,khd->qhk", query_block, key_block, preferred_element_type=jnp.float32)
        * scale
    )
    new_peak = jnp.maximum(row_peak, jnp.max(scores, axis=-1))
    factor = jnp.exp(row_peak - new_peak)
    raw_weights = jnp.exp(scores - new_peak[:, :, None])
    totals = totals * factor + jnp.sum(raw_weights, axis=-1)
    weighted_sum = weighted_sum * factor[:, :, None] + jnp.einsum(
        "qhk,khd->qhd",
        raw_weights.astype(jnp.bfloat16),
        value_block,
        preferred_element_type=jnp.float32,
    )
    return (new_peak, totals, weighted_sum)


def on_tiles(
    queries, key_rows, value_rows, residual, w_out, w_neck, w_first, w_second, w_class, labels
):
    width_here = queries.shape[-1]
    heads_here = width_here // HD
    scale = HD ** (-0.5)
    local_queries = queries.reshape(-1, heads_here, HD)
    query_total = local_queries.shape[0]
    start_state = (
        jnp.full((query_total, heads_here), NEG_LARGE, jnp.float32),
        jnp.zeros((query_total, heads_here), jnp.float32),
        jnp.zeros((query_total, heads_here, HD), jnp.float32),
    )

    def fold_keys(carried, key_piece):
        key_flat = key_piece[0].reshape(-1, heads_here, HD)
        value_flat = key_piece[1].reshape(-1, heads_here, HD)
        key_total = key_flat.shape[0]
        if key_total > 512 and key_total % 512 == 0:
            key_blocks = key_flat.reshape(key_total // 512, 512, heads_here, HD)
            value_blocks = value_flat.reshape(key_total // 512, 512, heads_here, HD)

            def scan_step(inner, paired):
                return (online_step(inner, local_queries, paired[0], paired[1], scale), None)

            return lax.scan(scan_step, carried, (key_blocks, value_blocks))[0]
        return online_step(carried, local_queries, key_flat, value_flat, scale)

    row_peak, totals, weighted_sum = fold_keys(
        start_state,
        (
            lax.all_gather(key_rows, "tok", axis=0, tiled=True),
            lax.all_gather(value_rows, "tok", axis=0, tiled=True),
        ),
    )
    attended = (weighted_sum / totals[:, :, None]).astype(jnp.bfloat16)
    attended_grid = attended.reshape(queries.shape)
    owned = lax.all_to_all(attended_grid, "heads", split_axis=1, concat_axis=3, tiled=True)
    attention_out = jnp.einsum(
        "tzxe,ed->ztxd",
        owned,
        lax.all_gather(w_out, "heads", axis=0, tiled=True),
        preferred_element_type=jnp.float32,
    )
    encoded = (residual.astype(jnp.float32) + attention_out).astype(jnp.bfloat16)
    tiled = lax.all_to_all(encoded, "tok", split_axis=2, concat_axis=1, tiled=True)
    neck_feats = jnp.einsum(
        "ztxd,dc->ztxc", tiled, w_neck, preferred_element_type=jnp.float32
    ).astype(jnp.bfloat16)
    extent = neck_feats.shape[:3]
    channels = w_neck.shape[1]
    cell_count = extent[0] * extent[1] * extent[2]
    hidden_one = conv_apply(neck_feats, w_first, False)
    active_one = jax.nn.silu(hidden_one).astype(jnp.bfloat16)
    hidden_two = conv_apply(active_one.reshape(extent + (channels,)), w_second, False)
    active_two = jax.nn.silu(hidden_two).astype(jnp.bfloat16)
    logits = jnp.dot(active_two, w_class, preferred_element_type=jnp.float32)
    probability = jax.nn.sigmoid(logits)
    fault_mask = labels.reshape(cell_count).astype(jnp.float32)
    intersection, total_prob, total_fault = lax.psum(
        (jnp.sum(probability * fault_mask), jnp.sum(probability), jnp.sum(fault_mask)),
        ("heads", "tok"),
    )
    dice_denominator = total_prob + total_fault
    dice_loss = 1.0 - 2.0 * intersection / dice_denominator
    cells_all = float(cell_count * lax.axis_size("heads") * lax.axis_size("tok"))
    grad_logits = (
        LOSS_SCALE
        * cells_all
        * -2.0
        * (fault_mask * dice_denominator - intersection)
        / (dice_denominator * dice_denominator)
        * probability
        * (1.0 - probability)
    )
    grad_hidden_two = (
        grad_logits[:, None] * w_class.astype(jnp.float32)[None, :] * silu_slope(hidden_two)
    ).astype(jnp.bfloat16)
    grad_active_one = conv_apply(grad_hidden_two.reshape(extent + (channels,)), w_second, True)
    grad_hidden_one = (grad_active_one * silu_slope(hidden_one)).astype(jnp.bfloat16)
    grad_neck = (
        conv_apply(grad_hidden_one.reshape(extent + (channels,)), w_first, True)
        .astype(jnp.bfloat16)
        .reshape(extent + (channels,))
    )
    grad_tiles = jnp.einsum(
        "ztxc,dc->ztxd", grad_neck, w_neck, preferred_element_type=jnp.float32
    ).astype(jnp.bfloat16)
    grad_encoded = lax.all_to_all(grad_tiles, "tok", split_axis=1, concat_axis=2, tiled=True)
    return (encoded, dice_loss, grad_encoded)


def dot(a, b):
    return jnp.dot(a, b, preferred_element_type=F32)


def dot_t(a, b):
    return lax.dot_general(a, b, (((1,), (1,)), ((), ())), preferred_element_type=F32)


def sigma_of(v):
    return 1.0 / (1.0 + jnp.exp(-v))


def slope_of(v):
    s = sigma_of(v)
    return s * (1.0 + v * (1.0 - s))


def iota(shape, dim):
    return lax.broadcasted_iota(jnp.int32, shape, dim)


def along_inline(value, step, inline):
    if step == 0:
        return value
    rows = value.shape[0]
    x = iota(value.shape, 0) % inline
    edge = inline - 1 if step > 0 else 0
    return jnp.where(x == edge, 0.0, pltpu.roll(value, (-step) % rows, axis=0))


def along_rows(value, step):
    if step == 0:
        return value
    zeros = jnp.zeros((abs(step), value.shape[1]), value.dtype)
    if step > 0:
        return jnp.concatenate([value[step:], zeros], axis=0)
    return jnp.concatenate([zeros, value[:step]], axis=0)


def place_of(tok_n):
    h, t = lax.axis_index("heads"), lax.axis_index("tok")
    return h, t // 2, t % 2, t


def pack_kernel(tok_n, q_ref, k_ref, v_ref, r_ref, neck_ref, lab_ref, out_ref):
    h, _, _, t = place_of(tok_n)
    rows = q_ref.shape[1] * q_ref.shape[2]
    width = q_ref.shape[3]
    for i, ref in enumerate((q_ref, k_ref, v_ref)):
        flat = ref[...].astype(F32).reshape(rows, width).astype(BF16)
        out_ref[i * rows : (i + 1) * rows, :] = flat
    own = r_ref.shape[0] * r_ref.shape[2]
    residual = r_ref[...].astype(F32).reshape(own, r_ref.shape[3]).astype(BF16)
    out_ref[3 * rows : 3 * rows + own, :] = dot(residual, neck_ref[...]).astype(BF16)
    own_c, _, nt = lab_ref.shape
    spread = jnp.zeros((LABEL_ROWS, width), F32)
    for c in range(own_c):
        row = jnp.broadcast_to(lab_ref[c].astype(F32), (LABEL_ROWS, nt)).astype(BF16)
        at = (h * own_c + c) * nt + iota((nt, width), 0)
        spread = spread + dot(row, (iota((nt, width), 1) == at).astype(F32).astype(BF16))
    out_ref[3 * rows + own :, :] = jnp.where(
        iota((LABEL_ROWS, width), 0) == t, spread, 0.0
    ).astype(BF16)


def weights_kernel(first_ref, second_ref, out_ref, neck_ref, packed_ref, *refs):
    first_in, second_in, first_t, second_t, joint, again, out_w, neck_w = refs[:8]
    first_mid, second_mid, sems = refs[8:]
    small = [
        pltpu.make_async_copy(out_ref, out_w, sems.at[6]),
        pltpu.make_async_copy(neck_ref, neck_w, sems.at[7]),
    ]
    for copy in small:
        copy.start()
    sets = (
        (first_ref, first_in, first_mid, first_t),
        (second_ref, second_in, second_mid, second_t),
    )
    copies = []
    for i, (src, dst, mid, _) in enumerate(sets):
        for a, place in enumerate((dst.at[0], mid, dst.at[3])):
            copies.append(pltpu.make_async_copy(src.at[a], place, sems.at[3 * i + a]))
            copies[-1].start()
    again[...] = packed_ref[...]
    for copy in small:
        copy.wait()
    joint[...] = dot(out_w[...], neck_w[...]).astype(BF16)
    for i, (_, dst, mid, flipped) in enumerate(sets):
        for a in range(3):
            copies[3 * i + a].wait()
        for b in range(3):
            for e in range(3):
                taps = (dst[0, b, e], mid[b, e], dst[3, b, e])
                for a in range(3):
                    flipped[a, b, e] = taps[a].T
                g0, g1, g2 = (tap.astype(F32) * 0.5 for tap in taps)
                dst[1, b, e] = (g0 + g2 + g1).astype(BF16)
                dst[2, b, e] = (g0 + g2 - g1).astype(BF16)


def far_first(zs):
    return [0, 1] + list(range(zs - 1, 1, -1))


def attention_kernel(tok_n, zs, rows, own, *refs):
    order = far_first(zs)
    ours = [refs[order.index(d)] for d in range(zs)]
    theirs = [refs[zs + order.index(d)] for d in range(zs)]
    out_w, joint_w = refs[2 * zs : 2 + 2 * zs]
    part_refs = refs[2 + 2 * zs : -4]
    qq, kk, vv, part = refs[-4:]
    h, z, core, _ = place_of(tok_n)
    width = qq.shape[1]
    queries_n = qq.shape[0]
    labels = jnp.zeros((LABEL_ROWS, width), F32)
    for d in range(zs):
        qq[d * rows : (d + 1) * rows, :] = ours[d][0:rows, :]
        for ref, side in ((ours[d], core), (theirs[d], 1 - core)):
            at = pl.multiple_of((2 * (z ^ d) + side) * rows, rows)
            kk[pl.ds(at, rows), :] = ref[rows : 2 * rows, :]
            vv[pl.ds(at, rows), :] = ref[2 * rows : 3 * rows, :]
            labels = labels + ref[3 * rows + own :, :].astype(F32)
    heads_here = width // HD
    scale = HD ** (-0.5)
    query = qq[...]
    keys, values = kk[...], vv[...]
    lane_head = iota((queries_n, width), 1) // HD
    attended = jnp.zeros((queries_n, width), F32)
    for head in range(heads_here):
        mine = lane_head == head
        scores = dot_t(jnp.where(mine, query, jnp.zeros_like(query)), keys) * scale
        raw = jnp.exp(scores - jnp.max(scores, axis=1, keepdims=True))
        total = jnp.sum(raw, axis=1, keepdims=True)
        mixed = dot(raw.astype(BF16), values)
        attended = jnp.where(mine, mixed / total, attended)
    attended = attended.astype(BF16)
    part[...] = dot(attended, joint_w[...])
    for d in range(zs):
        at = pl.multiple_of(d * rows + h * own, own)
        part[pl.ds(at, own), :] += ours[d][3 * rows : 3 * rows + own, :].astype(F32)
    partial = part[...].astype(BF16)
    labels = labels.astype(BF16)
    first = dot(attended[0:rows, :], out_w[...])
    blocks = [first[i * own : (i + 1) * own, :] for i in range(rows // own)]
    for d, ref in enumerate(part_refs):
        ref[0:queries_n, :] = partial
        picked = blocks[0]
        for i in range(1, len(blocks)):
            picked = jnp.where((h ^ d) == i, blocks[i], picked)
        for i in range(picked.shape[1] // width):
            at = queries_n + i * own
            ref[at : at + own, :] = picked[:, i * width : (i + 1) * width].astype(BF16)
        ref[ref.shape[0] - LABEL_ROWS :, :] = labels


def decoder_kernel(sizes, *refs):
    nc, nt, ni, own_c, zs, tok_n, parts_n = sizes
    ours, theirs, r_ref, w1, w2, w1_t, w2_t, class_w, neck_w = refs[:9]
    parts = refs[9 : 9 + parts_n]
    encoded_ref, loss_ref, grad_ref, grid, cols, slope1, grad2, cols3, hid1, hid2, parts_out = refs[9 + parts_n :]
    channels = grid.shape[2]
    slab = nt * ni
    rows = nc * ni
    cells = nc * slab
    h, z, core, tslab = place_of(tok_n)
    taps = 9
    for d in range(zs):
        for ref, side in ((ours, core), (theirs, 1 - core)):
            block = ref[d * rows : (d + 1) * rows, :].astype(F32)
            at = pl.multiple_of((2 * (z ^ d) + side) * ni, ni)
            for c in range(nc):
                grid[c, pl.ds(at, ni), :] = block[c * ni : (c + 1) * ni, :]

    slope1[...] = jnp.zeros_like(slope1)
    grad2[...] = jnp.zeros_like(grad2)
    def spread(value, k, i):
        for e in range(3):
            moved = along_inline(value, e - 1, ni)
            for b in range(3):
                lane = (b * 3 + e) * channels
                cols[k, i * slab : (i + 1) * slab, lane : lane + channels] = along_rows(
                    moved, (b - 1) * ni
                ).astype(BF16)

    def spread_all(volume):
        empty = jnp.zeros((slab, channels), F32)
        for i in range(nc // 2):
            d0 = volume[2 * i - 1] if i > 0 else empty
            d1, d2 = volume[2 * i], volume[2 * i + 1]
            d3 = volume[2 * i + 2] if 2 * i + 2 < nc else empty
            for k, value in enumerate((d0 - d2, d1 + d2, d2 - d1, d1 - d3)):
                spread(value, k, i)

    half_cells = cells // 2

    def conv(weights, out):
        for k in range(4):
            matrix = weights[k].reshape(taps * channels, channels)
            for m in range(0, half_cells, TILE):
                parts_out[k, m : m + TILE, :] = dot(cols[k, m : m + TILE, :], matrix)
        for i in range(nc // 2):
            m0, m1, m2, m3 = (parts_out[k, i * slab : (i + 1) * slab, :] for k in range(4))
            out[2 * i * slab : (2 * i + 1) * slab, :] = m0 + m1 + m2
            out[(2 * i + 1) * slab : (2 * i + 2) * slab, :] = m1 - m2 - m3

    spread_all([grid[c] for c in range(nc)])
    conv(w1, hid1)
    for c in range(nc):
        v = hid1[c * slab : (c + 1) * slab, :]
        s = sigma_of(v)
        slope1[c + 1, ni : ni + slab, :] = s * (1.0 + v * (1.0 - s))
        grid[c] = (v * s).astype(BF16).astype(F32)
    spread_all([grid[c] for c in range(nc)])
    conv(w2, hid2)
    hidden_two = hid2[...]
    sigma_two = sigma_of(hidden_two)
    active_two = (hidden_two * sigma_two).astype(BF16)
    class_row = class_w[...].astype(F32).reshape(1, channels)
    logits = dot_t(active_two, jnp.broadcast_to(class_row, (128, channels)).astype(BF16))
    probability = sigma_of(logits)
    last = parts[0].shape[0] - LABEL_ROWS
    lab = pairwise([ref[last : last + ni, 0:128].astype(F32) for ref in parts])
    spread_lab = jnp.broadcast_to(lab[None], (cells // ni, ni, 128)).reshape(cells, 128)
    wanted = iota((cells, 128), 0) // ni
    picked = jnp.where(iota((cells, 128), 1) == wanted, spread_lab, 0.0).astype(BF16)
    mask = dot(picked, jnp.ones((128, 128), BF16))
    intersection = jnp.sum(probability * mask, axis=0, keepdims=True)
    total_prob = jnp.sum(probability, axis=0, keepdims=True)
    total_fault = jnp.sum(mask, axis=0, keepdims=True)
    denominator = total_prob + total_fault
    loss_ref[...] = 1.0 - 2.0 * intersection / denominator
    grad_logits = (
        LOSS_SCALE
        * float(cells)
        * -2.0
        * (mask * denominator - intersection)
        / (denominator * denominator)
        * probability
        * (1.0 - probability)
    )
    wide = jnp.concatenate([grad_logits] * (channels // 128), axis=1)
    slope_two = sigma_two * (1.0 + hidden_two * (1.0 - sigma_two))
    g2 = wide * class_row * slope_two
    for c in range(nc):
        grad2[c + 2, 2 * ni : 2 * ni + slab, :] = g2[c * slab : (c + 1) * slab, :]

    band = 4 * ni
    c0 = h * own_c
    t0 = pl.multiple_of(tslab * ni, ni)
    for i in range(own_c + 4):
        region = grad2[c0 + i, pl.ds(t0, band + 2 * ni), :]
        for e in range(3):
            moved = along_inline(region, 1 - e, ni)
            for b in range(3):
                lane = (b * 3 + e) * channels
                cols3[i * band : (i + 1) * band, lane : lane + channels] = moved[
                    (2 - b) * ni : (2 - b) * ni + band, :
                ].astype(BF16)
    out3 = (own_c + 2) * band
    total = jnp.zeros((out3, channels), F32)
    for a in range(3):
        for b in range(3):
            for e in range(3):
                lane = (b * 3 + e) * channels
                piece = cols3[(2 - a) * band : (2 - a) * band + out3, lane : lane + channels]
                total = total + dot(piece, w2_t[a, b, e])
    slopes = [slope1[c0 + i, pl.ds(t0, band), :] for i in range(own_c + 2)]
    g1 = (total * jnp.concatenate(slopes, axis=0)).astype(BF16).astype(F32)
    shifted = [along_inline(g1, 1 - e, ni) for e in range(3)]
    total = jnp.zeros((own_c * ni, channels), F32)
    for a in range(3):
        pieces = []
        for b in range(3):
            for e in range(3):
                cells_in = [
                    shifted[e][(i + 2 - a) * band + (2 - b) * ni : (i + 2 - a) * band + (3 - b) * ni, :]
                    for i in range(own_c)
                ]
                pieces.append(jnp.concatenate(cells_in, axis=0).astype(BF16))
        matrix = w1_t[a].reshape(taps * channels, channels)
        total = total + dot(jnp.concatenate(pieces, axis=1), matrix)
    grad = dot_t(total.astype(BF16), neck_w[...])
    grad_ref[...] = grad.reshape(grad_ref.shape).astype(BF16)

    own = own_c * ni
    width = parts[0].shape[1]
    base = rows * zs
    for i in range(r_ref.shape[3] // width):
        terms = [ref[base + i * own : base + (i + 1) * own, :].astype(F32) for ref in parts]
        total = pairwise(terms).reshape(own_c, 1, ni, width)
        lanes = slice(i * width, (i + 1) * width)
        encoded_ref[:, :, :, lanes] = (r_ref[:, :, :, lanes].astype(F32) + total).astype(BF16)


def pairwise(values):
    while len(values) > 1:
        values = [values[i] + values[i + 1] for i in range(0, len(values), 2)]
    return values[0]


def vmem():
    return pl.BlockSpec(memory_space=pltpu.VMEM)


def hbm():
    return pl.BlockSpec(memory_space=pltpu.HBM)


def whole_grid(
    queries, key_rows, value_rows, residual, w_out, w_neck, w_first, w_second, w_class, labels
):
    heads_n, tok_n = lax.axis_size("heads"), lax.axis_size("tok")
    zs = tok_n // 2
    _, nc, ni, width = queries.shape
    own_c = residual.shape[0]
    nt = labels.shape[1]
    channels = w_neck.shape[1]
    rows, own = nc * ni, own_c * ni

    def swap_tok(value, bits):
        return lax.ppermute(value, "tok", [(i, i ^ bits) for i in range(tok_n)])

    def swap_heads(value, bits):
        return lax.ppermute(value, "heads", [(i, i ^ bits) for i in range(heads_n)])

    packed = pl.pallas_call(
        functools.partial(pack_kernel, tok_n),
        out_shape=pltpu.VMEM((3 * rows + own + LABEL_ROWS, width), BF16),
        in_specs=[vmem()] * 6,
        out_specs=vmem(),
    )(queries, key_rows, value_rows, residual, w_neck, labels.transpose(0, 2, 1))
    ours = [packed] + [swap_tok(packed, 2 * d) for d in range(1, zs)]
    kept = [pltpu.with_memory_space_constraint(w, pltpu.HBM) for w in (w_first, w_second, w_out, w_neck)]
    first_in, second_in, first_t, second_t, joint, again, out_w, neck_w = pl.pallas_call(
        weights_kernel,
        out_shape=[pltpu.VMEM((4,) + w_first.shape[1:], BF16)] * 2
        + [pltpu.VMEM(w_first.shape, BF16)] * 2
        + [
            pltpu.VMEM((width, channels), BF16),
            pltpu.VMEM(packed.shape, BF16),
            pltpu.VMEM(w_out.shape, BF16),
            pltpu.VMEM(w_neck.shape, BF16),
        ],
        in_specs=[hbm()] * 4 + [vmem()],
        out_specs=[vmem()] * 8,
        scratch_shapes=[pltpu.VMEM(w_first.shape[1:], BF16)] * 2 + [pltpu.SemaphoreType.DMA((8,))],
        compiler_params=pltpu.CompilerParams(vmem_limit_bytes=24 * 2**20),
        cost_estimate=pl.CostEstimate(flops=0, bytes_accessed=28 * 2**20, transcendentals=0),
    )(*kept, packed)
    theirs = [swap_tok(value, 1) for value in [again] + ours[1:]]
    order = far_first(zs)
    queries_n, keys_n = rows * zs, rows * tok_n
    enc_rows = own * residual.shape[3] // width
    part_shape = pltpu.VMEM((queries_n + LABEL_ROWS + enc_rows, channels), BF16)
    sent = pl.pallas_call(
        functools.partial(attention_kernel, tok_n, zs, rows, own),
        out_shape=[part_shape] * heads_n,
        in_specs=[vmem()] * (2 * zs + 2),
        out_specs=[vmem()] * heads_n,
        scratch_shapes=[
            pltpu.VMEM((queries_n, width), BF16),
            pltpu.VMEM((keys_n, width), BF16),
            pltpu.VMEM((keys_n, width), BF16),
            pltpu.VMEM((queries_n, channels), F32),
        ],
        compiler_params=pltpu.CompilerParams(vmem_limit_bytes=16 * 2**20),
    )(*[ours[d] for d in order], *[theirs[d] for d in order], out_w, joint)
    parts = [swap_heads(sent[d], d) for d in range(heads_n - 1, 0, -1)] + [sent[0]]
    half = pairwise([part[:queries_n].astype(F32) for part in parts]).astype(BF16)
    other = swap_tok(half, 1)
    slab = nt * ni
    return tuple(
        pl.pallas_call(
            functools.partial(decoder_kernel, (nc, nt, ni, own_c, zs, tok_n, heads_n)),
            out_shape=[
                jax.ShapeDtypeStruct(residual.shape, BF16),
                jax.ShapeDtypeStruct((1, 128), F32),
                jax.ShapeDtypeStruct(residual.shape, BF16),
            ],
            in_specs=[vmem()] * (9 + heads_n),
            out_specs=[vmem()] * 3,
            scratch_shapes=[
                pltpu.VMEM((nc, slab, channels), F32),
                pltpu.VMEM((4, nc // 2 * slab, 9 * channels), BF16),
                pltpu.VMEM((nc + 2, (nt + 4) * ni, channels), F32),
                pltpu.VMEM((nc + 4, (nt + 6) * ni, channels), F32),
                pltpu.VMEM(((own_c + 4) * 4 * ni, 9 * channels), BF16),
                pltpu.VMEM((nc * slab, channels), F32),
                pltpu.VMEM((nc * slab, channels), F32),
                pltpu.VMEM((4, nc // 2 * slab, channels), F32),
            ],
            compiler_params=pltpu.CompilerParams(vmem_limit_bytes=36 * 2**20),
        )(half, other, residual, first_in, second_in, first_t, second_t, w_class, neck_w, *parts)
    )


def power_of_two(n):
    return n > 0 and n & (n - 1) == 0


def fits_whole(queries, residual, w_neck, labels):
    heads_n, tok_n = lax.axis_size("heads"), lax.axis_size("tok")
    slabs, nc, ni, width = queries.shape
    nt = labels.shape[1]
    return (
        slabs == 1
        and nc * nt <= 128
        and labels.shape[2] == 1
        and ni == LABEL_ROWS
        and nt == tok_n
        and tok_n >= 4
        and power_of_two(tok_n)
        and power_of_two(heads_n)
        and residual.shape[0] * heads_n == nc
        and nc * nt * ni <= 1024
        and (nc // 2 * nt * ni) % TILE == 0
        and nc % 2 == 0
        and width % 128 == 0
        and w_neck.shape[1] == width
        and (residual.shape[0] * ni) % 16 == 0
    )


def on_device(*arguments):
    queries, residual, w_neck, labels = (arguments[i] for i in (0, 3, 5, 9))
    if fits_whole(queries, residual, w_neck, labels):
        encoded, loss, grad = whole_grid(*arguments)
        return (encoded, loss[0, 0], grad)
    return on_tiles(*arguments)


def solution(mesh):
    placed = (
        P("tok", None, None, "heads"),
        P("tok", None, None, "heads"),
        P("tok", None, None, "heads"),
        P("heads", "tok", None, None),
        P("heads", None),
        P(),
        P(),
        P(),
        P(),
        P("heads", None, "tok"),
    )
    return jax.shard_map(
        on_device,
        mesh=mesh,
        in_specs=placed,
        out_specs=(P("heads", "tok", None, None), P(), P("heads", "tok", None, None)),
        check_vma=False,
    )
```

```python
import functools

import jax
import jax.numpy as jnp
from jax import lax
from jax.experimental import pallas as pl
from jax.experimental.pallas import tpu as pltpu
from jax.sharding import PartitionSpec as P

HD = 64
F32 = jnp.float32
BF16 = jnp.bfloat16
LABEL_ROWS = 8
TILE = 128


OFFSETS = [
    (along_c, along_t, along_x)
    for along_c in range(3)
    for along_t in range(3)
    for along_x in range(3)
]
LOSS_SCALE = 64.0
NEG_LARGE = -1e30


def padded_2(value, sides, width):
    for axis, dim in sides:
        size, length = (lax.axis_size(axis), value.shape[dim])
        up = [(i, (i + 1) % size) for i in range(size - 1)]
        down = [(j, i) for i, j in up]
        last = lax.slice_in_dim(value, length - width, length, axis=dim)
        first = lax.slice_in_dim(value, 0, width, axis=dim)
        before = lax.ppermute(last, axis, up)
        after = lax.ppermute(first, axis, down)
        value = jnp.concatenate([before, value, after], axis=dim)
    return value


def silu_slope(volume):
    sigma = jax.nn.sigmoid(volume)
    return sigma * (1.0 + volume * (1.0 - sigma))


def with_rims(volume):
    padded = padded_2(volume, (("heads", 0), ("tok", 2)), 1)
    return jnp.pad(padded, ((0, 0), (1, 1), (0, 0), (0, 0)))


def conv_apply(volume, weights, flipped):
    extent = volume.shape[:3]
    padded = with_rims(volume)
    pieces = []
    for along_c, along_t, along_x in OFFSETS:
        if flipped:
            anchor = (2 - along_c, 2 - along_t, 2 - along_x)
        else:
            anchor = (along_c, along_t, along_x)
        pieces.append(
            padded[
                anchor[0] : anchor[0] + extent[0],
                anchor[1] : anchor[1] + extent[1],
                anchor[2] : anchor[2] + extent[2],
            ]
        )
    stacked = jnp.stack(pieces, axis=3)
    columns = stacked.reshape(extent[0] * extent[1] * extent[2], 27, volume.shape[3])
    kernel = weights.reshape(27, weights.shape[3], weights.shape[4])
    if flipped:
        contraction = (((1, 2), (0, 2)), ((), ()))
    else:
        contraction = (((1, 2), (0, 1)), ((), ()))
    return lax.dot_general(columns, kernel, contraction, preferred_element_type=jnp.float32)


def online_step(carried, query_block, key_block, value_block, scale):
    row_peak, totals, weighted_sum = carried
    scores = (
        jnp.einsum("qhd,khd->qhk", query_block, key_block, preferred_element_type=jnp.float32)
        * scale
    )
    new_peak = jnp.maximum(row_peak, jnp.max(scores, axis=-1))
    factor = jnp.exp(row_peak - new_peak)
    raw_weights = jnp.exp(scores - new_peak[:, :, None])
    totals = totals * factor + jnp.sum(raw_weights, axis=-1)
    weighted_sum = weighted_sum * factor[:, :, None] + jnp.einsum(
        "qhk,khd->qhd",
        raw_weights.astype(jnp.bfloat16),
        value_block,
        preferred_element_type=jnp.float32,
    )
    return (new_peak, totals, weighted_sum)


def on_tiles(
    queries, key_rows, value_rows, residual, w_out, w_neck, w_first, w_second, w_class, labels
):
    width_here = queries.shape[-1]
    heads_here = width_here // HD
    scale = HD ** (-0.5)
    local_queries = queries.reshape(-1, heads_here, HD)
    query_total = local_queries.shape[0]
    start_state = (
        jnp.full((query_total, heads_here), NEG_LARGE, jnp.float32),
        jnp.zeros((query_total, heads_here), jnp.float32),
        jnp.zeros((query_total, heads_here, HD), jnp.float32),
    )

    def fold_keys(carried, key_piece):
        key_flat = key_piece[0].reshape(-1, heads_here, HD)
        value_flat = key_piece[1].reshape(-1, heads_here, HD)
        key_total = key_flat.shape[0]
        if key_total > 512 and key_total % 512 == 0:
            key_blocks = key_flat.reshape(key_total // 512, 512, heads_here, HD)
            value_blocks = value_flat.reshape(key_total // 512, 512, heads_here, HD)

            def scan_step(inner, paired):
                return (online_step(inner, local_queries, paired[0], paired[1], scale), None)

            return lax.scan(scan_step, carried, (key_blocks, value_blocks))[0]
        return online_step(carried, local_queries, key_flat, value_flat, scale)

    row_peak, totals, weighted_sum = fold_keys(
        start_state,
        (
            lax.all_gather(key_rows, "tok", axis=0, tiled=True),
            lax.all_gather(value_rows, "tok", axis=0, tiled=True),
        ),
    )
    attended = (weighted_sum / totals[:, :, None]).astype(jnp.bfloat16)
    attended_grid = attended.reshape(queries.shape)
    owned = lax.all_to_all(attended_grid, "heads", split_axis=1, concat_axis=3, tiled=True)
    attention_out = jnp.einsum(
        "tzxe,ed->ztxd",
        owned,
        lax.all_gather(w_out, "heads", axis=0, tiled=True),
        preferred_element_type=jnp.float32,
    )
    encoded = (residual.astype(jnp.float32) + attention_out).astype(jnp.bfloat16)
    tiled = lax.all_to_all(encoded, "tok", split_axis=2, concat_axis=1, tiled=True)
    neck_feats = jnp.einsum(
        "ztxd,dc->ztxc", tiled, w_neck, preferred_element_type=jnp.float32
    ).astype(jnp.bfloat16)
    extent = neck_feats.shape[:3]
    channels = w_neck.shape[1]
    cell_count = extent[0] * extent[1] * extent[2]
    hidden_one = conv_apply(neck_feats, w_first, False)
    active_one = jax.nn.silu(hidden_one).astype(jnp.bfloat16)
    hidden_two = conv_apply(active_one.reshape(extent + (channels,)), w_second, False)
    active_two = jax.nn.silu(hidden_two).astype(jnp.bfloat16)
    logits = jnp.dot(active_two, w_class, preferred_element_type=jnp.float32)
    probability = jax.nn.sigmoid(logits)
    fault_mask = labels.reshape(cell_count).astype(jnp.float32)
    intersection, total_prob, total_fault = lax.psum(
        (jnp.sum(probability * fault_mask), jnp.sum(probability), jnp.sum(fault_mask)),
        ("heads", "tok"),
    )
    dice_denominator = total_prob + total_fault
    dice_loss = 1.0 - 2.0 * intersection / dice_denominator
    cells_all = float(cell_count * lax.axis_size("heads") * lax.axis_size("tok"))
    grad_logits = (
        LOSS_SCALE
        * cells_all
        * -2.0
        * (fault_mask * dice_denominator - intersection)
        / (dice_denominator * dice_denominator)
        * probability
        * (1.0 - probability)
    )
    grad_hidden_two = (
        grad_logits[:, None] * w_class.astype(jnp.float32)[None, :] * silu_slope(hidden_two)
    ).astype(jnp.bfloat16)
    grad_active_one = conv_apply(grad_hidden_two.reshape(extent + (channels,)), w_second, True)
    grad_hidden_one = (grad_active_one * silu_slope(hidden_one)).astype(jnp.bfloat16)
    grad_neck = (
        conv_apply(grad_hidden_one.reshape(extent + (channels,)), w_first, True)
        .astype(jnp.bfloat16)
        .reshape(extent + (channels,))
    )
    grad_tiles = jnp.einsum(
        "ztxc,dc->ztxd", grad_neck, w_neck, preferred_element_type=jnp.float32
    ).astype(jnp.bfloat16)
    grad_encoded = lax.all_to_all(grad_tiles, "tok", split_axis=1, concat_axis=2, tiled=True)
    return (encoded, dice_loss, grad_encoded)


def dot(a, b):
    return jnp.dot(a, b, preferred_element_type=F32)


def dot_t(a, b):
    return lax.dot_general(a, b, (((1,), (1,)), ((), ())), preferred_element_type=F32)


def sigma_of(v):
    return 1.0 / (1.0 + jnp.exp(-v))


def slope_of(v):
    s = sigma_of(v)
    return s * (1.0 + v * (1.0 - s))


def iota(shape, dim):
    return lax.broadcasted_iota(jnp.int32, shape, dim)


def along_inline(value, step, inline):
    if step == 0:
        return value
    rows = value.shape[0]
    x = iota(value.shape, 0) % inline
    edge = inline - 1 if step > 0 else 0
    return jnp.where(x == edge, 0.0, pltpu.roll(value, (-step) % rows, axis=0))


def along_rows(value, step):
    if step == 0:
        return value
    zeros = jnp.zeros((abs(step), value.shape[1]), value.dtype)
    if step > 0:
        return jnp.concatenate([value[step:], zeros], axis=0)
    return jnp.concatenate([zeros, value[:step]], axis=0)


def place_of(tok_n):
    h, t = lax.axis_index("heads"), lax.axis_index("tok")
    return h, t // 2, t % 2, t


def pack_kernel(tok_n, q_ref, k_ref, v_ref, r_ref, neck_ref, lab_ref, out_ref):
    h, _, _, t = place_of(tok_n)
    rows = q_ref.shape[1] * q_ref.shape[2]
    width = q_ref.shape[3]
    for i, ref in enumerate((q_ref, k_ref, v_ref)):
        flat = ref[...].astype(F32).reshape(rows, width).astype(BF16)
        out_ref[i * rows : (i + 1) * rows, :] = flat
    own = r_ref.shape[0] * r_ref.shape[2]
    residual = r_ref[...].astype(F32).reshape(own, r_ref.shape[3]).astype(BF16)
    out_ref[3 * rows : 3 * rows + own, :] = dot(residual, neck_ref[...]).astype(BF16)
    own_c, _, nt = lab_ref.shape
    spread = jnp.zeros((LABEL_ROWS, width), F32)
    for c in range(own_c):
        row = jnp.broadcast_to(lab_ref[c].astype(F32), (LABEL_ROWS, nt)).astype(BF16)
        at = (h * own_c + c) * nt + iota((nt, width), 0)
        spread = spread + dot(row, (iota((nt, width), 1) == at).astype(F32).astype(BF16))
    out_ref[3 * rows + own :, :] = jnp.where(
        iota((LABEL_ROWS, width), 0) == t, spread, 0.0
    ).astype(BF16)


def weights_kernel(first_ref, second_ref, out_ref, neck_ref, packed_ref, *refs):
    first_in, second_in, first_t, second_t, joint, again, out_w, neck_w = refs[:8]
    first_mid, second_mid, sems = refs[8:]
    small = [
        pltpu.make_async_copy(out_ref, out_w, sems.at[6]),
        pltpu.make_async_copy(neck_ref, neck_w, sems.at[7]),
    ]
    for copy in small:
        copy.start()
    sets = (
        (first_ref, first_in, first_mid, first_t),
        (second_ref, second_in, second_mid, second_t),
    )
    copies = []
    for i, (src, dst, mid, _) in enumerate(sets):
        for a, place in enumerate((dst.at[0], mid, dst.at[3])):
            copies.append(pltpu.make_async_copy(src.at[a], place, sems.at[3 * i + a]))
            copies[-1].start()
    again[...] = packed_ref[...]
    for copy in small:
        copy.wait()
    joint[...] = dot(out_w[...], neck_w[...]).astype(BF16)
    for i, (_, dst, mid, flipped) in enumerate(sets):
        for a in range(3):
            copies[3 * i + a].wait()
        for b in range(3):
            for e in range(3):
                taps = (dst[0, b, e], mid[b, e], dst[3, b, e])
                for a in range(3):
                    flipped[a, b, e] = taps[a].T
                g0, g1, g2 = (tap.astype(F32) * 0.5 for tap in taps)
                dst[1, b, e] = (g0 + g2 + g1).astype(BF16)
                dst[2, b, e] = (g0 + g2 - g1).astype(BF16)


def far_first(zs):
    return list(range(zs - 1, 2, -1)) + [1, 2, 0]


def attention_kernel(tok_n, zs, rows, own, *refs):
    order = far_first(zs)
    ours = [refs[order.index(d)] for d in range(zs)]
    theirs = [refs[zs + order.index(d)] for d in range(zs)]
    out_w, joint_w = refs[2 * zs : 2 + 2 * zs]
    part_refs = refs[2 + 2 * zs : -4]
    qq, kk, vv, part = refs[-4:]
    h, z, core, _ = place_of(tok_n)
    width = qq.shape[1]
    queries_n = qq.shape[0]
    labels = jnp.zeros((LABEL_ROWS, width), F32)
    for d in range(zs):
        qq[d * rows : (d + 1) * rows, :] = ours[d][0:rows, :]
        for ref, side in ((ours[d], core), (theirs[d], 1 - core)):
            at = pl.multiple_of((2 * (z ^ d) + side) * rows, rows)
            kk[pl.ds(at, rows), :] = ref[rows : 2 * rows, :]
            vv[pl.ds(at, rows), :] = ref[2 * rows : 3 * rows, :]
            labels = labels + ref[3 * rows + own :, :].astype(F32)
    heads_here = width // HD
    scale = HD ** (-0.5)
    query = qq[...]
    keys, values = kk[...], vv[...]
    lane_head = iota((queries_n, width), 1) // HD
    attended = jnp.zeros((queries_n, width), F32)
    for head in range(heads_here):
        mine = lane_head == head
        scores = dot_t(jnp.where(mine, query, jnp.zeros_like(query)), keys) * scale
        raw = jnp.exp(scores - jnp.max(scores, axis=1, keepdims=True))
        total = jnp.sum(raw, axis=1, keepdims=True)
        mixed = dot(raw.astype(BF16), values)
        attended = jnp.where(mine, mixed / total, attended)
    attended = attended.astype(BF16)
    part[...] = dot(attended, joint_w[...])
    for d in range(zs):
        at = pl.multiple_of(d * rows + h * own, own)
        part[pl.ds(at, own), :] += ours[d][3 * rows : 3 * rows + own, :].astype(F32)
    partial = part[...].astype(BF16)
    labels = labels.astype(BF16)
    first = dot(attended[0:rows, :], out_w[...])
    blocks = [first[i * own : (i + 1) * own, :] for i in range(rows // own)]
    for d, ref in enumerate(part_refs):
        ref[0:queries_n, :] = partial
        picked = blocks[0]
        for i in range(1, len(blocks)):
            picked = jnp.where((h ^ d) == i, blocks[i], picked)
        for i in range(picked.shape[1] // width):
            at = queries_n + i * own
            ref[at : at + own, :] = picked[:, i * width : (i + 1) * width].astype(BF16)
        ref[ref.shape[0] - LABEL_ROWS :, :] = labels


def decoder_kernel(sizes, *refs):
    nc, nt, ni, own_c, zs, tok_n, parts_n = sizes
    ours, theirs, r_ref, w1, w2, w1_t, w2_t, class_w, neck_w = refs[:9]
    parts = refs[9 : 9 + parts_n]
    encoded_ref, loss_ref, grad_ref, grid, cols, slope1, grad2, cols3, slope2, act, parts_out = refs[9 + parts_n :]
    channels = grid.shape[2]
    slab = nt * ni
    rows = nc * ni
    cells = nc * slab
    h, z, core, tslab = place_of(tok_n)
    taps = 9
    for d in range(zs):
        for ref, side in ((ours, core), (theirs, 1 - core)):
            block = ref[d * rows : (d + 1) * rows, :].astype(F32)
            at = pl.multiple_of((2 * (z ^ d) + side) * ni, ni)
            for c in range(nc):
                grid[c, pl.ds(at, ni), :] = block[c * ni : (c + 1) * ni, :]

    slope1[...] = jnp.zeros_like(slope1)
    grad2[...] = jnp.zeros_like(grad2)
    def spread(value, k, i):
        for e in range(3):
            moved = along_inline(value, e - 1, ni)
            for b in range(3):
                lane = (b * 3 + e) * channels
                cols[k, i * slab : (i + 1) * slab, lane : lane + channels] = along_rows(
                    moved, (b - 1) * ni
                ).astype(BF16)

    def spread_all(volume):
        empty = jnp.zeros((slab, channels), F32)
        for i in range(nc // 2):
            d0 = volume[2 * i - 1] if i > 0 else empty
            d1, d2 = volume[2 * i], volume[2 * i + 1]
            d3 = volume[2 * i + 2] if 2 * i + 2 < nc else empty
            for k, value in enumerate((d0 - d2, d1 + d2, d2 - d1, d1 - d3)):
                spread(value, k, i)

    half_cells = cells // 2

    def conv(weights, finish):
        for m in range(0, half_cells, TILE):
            for k in range(4):
                matrix = weights[k].reshape(taps * channels, channels)
                parts_out[k, m : m + TILE, :] = dot(cols[k, m : m + TILE, :], matrix)
            for i in range(m // slab, (m + TILE) // slab):
                m0, m1, m2, m3 = (parts_out[k, i * slab : (i + 1) * slab, :] for k in range(4))
                finish(2 * i, m0 + m1 + m2)
                finish(2 * i + 1, m1 - m2 - m3)

    class_row = class_w[...].astype(F32).reshape(1, channels)

    def finish_one(c, v):
        s = sigma_of(v)
        slope1[c + 1, ni : ni + slab, :] = s * (1.0 + v * (1.0 - s))
        grid[c] = (v * s).astype(BF16).astype(F32)

    def finish_two(c, v):
        s = sigma_of(v)
        slope2[c * slab : (c + 1) * slab, :] = s * (1.0 + v * (1.0 - s)) * class_row
        act[c * slab : (c + 1) * slab, :] = (v * s).astype(BF16)

    spread_all([grid[c] for c in range(nc)])
    conv(w1, finish_one)
    spread_all([grid[c] for c in range(nc)])
    conv(w2, finish_two)
    active_two = act[...]
    logits = dot_t(active_two, jnp.broadcast_to(class_row, (128, channels)).astype(BF16))
    probability = sigma_of(logits)
    last = parts[0].shape[0] - LABEL_ROWS
    lab = pairwise([ref[last : last + ni, 0:128].astype(F32) for ref in parts])
    spread_lab = jnp.broadcast_to(lab[None], (cells // ni, ni, 128)).reshape(cells, 128)
    wanted = iota((cells, 128), 0) // ni
    picked = jnp.where(iota((cells, 128), 1) == wanted, spread_lab, 0.0).astype(BF16)
    mask = dot(picked, jnp.ones((128, 128), BF16))
    intersection = jnp.sum(probability * mask, axis=0, keepdims=True)
    total_prob = jnp.sum(probability, axis=0, keepdims=True)
    total_fault = jnp.sum(mask, axis=0, keepdims=True)
    denominator = total_prob + total_fault
    loss_ref[...] = 1.0 - 2.0 * intersection / denominator
    grad_logits = (
        LOSS_SCALE
        * float(cells)
        * -2.0
        * (mask * denominator - intersection)
        / (denominator * denominator)
        * probability
        * (1.0 - probability)
    )
    for c in range(nc):
        rows_c = slice(c * slab, (c + 1) * slab)
        wide = jnp.concatenate([grad_logits[rows_c, :]] * (channels // 128), axis=1)
        grad2[c + 2, 2 * ni : 2 * ni + slab, :] = wide * slope2[rows_c, :]

    band = 4 * ni
    c0 = h * own_c
    t0 = pl.multiple_of(tslab * ni, ni)
    for i in range(own_c + 4):
        region = grad2[c0 + i, pl.ds(t0, band + 2 * ni), :]
        for e in range(3):
            moved = along_inline(region, 1 - e, ni)
            for b in range(3):
                lane = (b * 3 + e) * channels
                cols3[i * band : (i + 1) * band, lane : lane + channels] = moved[
                    (2 - b) * ni : (2 - b) * ni + band, :
                ].astype(BF16)
    out3 = (own_c + 2) * band
    total = jnp.zeros((out3, channels), F32)
    for a in range(3):
        for b in range(3):
            for e in range(3):
                lane = (b * 3 + e) * channels
                piece = cols3[(2 - a) * band : (2 - a) * band + out3, lane : lane + channels]
                total = total + dot(piece, w2_t[a, b, e])
    slopes = [slope1[c0 + i, pl.ds(t0, band), :] for i in range(own_c + 2)]
    g1 = (total * jnp.concatenate(slopes, axis=0)).astype(BF16).astype(F32)
    shifted = [along_inline(g1, 1 - e, ni) for e in range(3)]
    total = jnp.zeros((own_c * ni, channels), F32)
    for a in range(3):
        pieces = []
        for b in range(3):
            for e in range(3):
                cells_in = [
                    shifted[e][(i + 2 - a) * band + (2 - b) * ni : (i + 2 - a) * band + (3 - b) * ni, :]
                    for i in range(own_c)
                ]
                pieces.append(jnp.concatenate(cells_in, axis=0).astype(BF16))
        matrix = w1_t[a].reshape(taps * channels, channels)
        total = total + dot(jnp.concatenate(pieces, axis=1), matrix)
    grad = dot_t(total.astype(BF16), neck_w[...])
    grad_ref[...] = grad.reshape(grad_ref.shape).astype(BF16)

    own = own_c * ni
    width = parts[0].shape[1]
    base = rows * zs
    for i in range(r_ref.shape[3] // width):
        terms = [ref[base + i * own : base + (i + 1) * own, :].astype(F32) for ref in parts]
        total = pairwise(terms).reshape(own_c, 1, ni, width)
        lanes = slice(i * width, (i + 1) * width)
        encoded_ref[:, :, :, lanes] = (r_ref[:, :, :, lanes].astype(F32) + total).astype(BF16)


def pairwise(values):
    while len(values) > 1:
        values = [values[i] + values[i + 1] for i in range(0, len(values), 2)]
    return values[0]


def vmem():
    return pl.BlockSpec(memory_space=pltpu.VMEM)


def hbm():
    return pl.BlockSpec(memory_space=pltpu.HBM)


def whole_grid(
    queries, key_rows, value_rows, residual, w_out, w_neck, w_first, w_second, w_class, labels
):
    heads_n, tok_n = lax.axis_size("heads"), lax.axis_size("tok")
    zs = tok_n // 2
    _, nc, ni, width = queries.shape
    own_c = residual.shape[0]
    nt = labels.shape[1]
    channels = w_neck.shape[1]
    rows, own = nc * ni, own_c * ni

    def swap_tok(value, bits):
        return lax.ppermute(value, "tok", [(i, i ^ bits) for i in range(tok_n)])

    def swap_heads(value, bits):
        return lax.ppermute(value, "heads", [(i, i ^ bits) for i in range(heads_n)])

    packed = pl.pallas_call(
        functools.partial(pack_kernel, tok_n),
        out_shape=pltpu.VMEM((3 * rows + own + LABEL_ROWS, width), BF16),
        in_specs=[vmem()] * 6,
        out_specs=vmem(),
    )(queries, key_rows, value_rows, residual, w_neck, labels.transpose(0, 2, 1))
    ours = [packed] + [swap_tok(packed, 2 * d) for d in range(1, zs)]
    kept = [pltpu.with_memory_space_constraint(w, pltpu.HBM) for w in (w_first, w_second, w_out, w_neck)]
    first_in, second_in, first_t, second_t, joint, again, out_w, neck_w = pl.pallas_call(
        weights_kernel,
        out_shape=[pltpu.VMEM((4,) + w_first.shape[1:], BF16)] * 2
        + [pltpu.VMEM(w_first.shape, BF16)] * 2
        + [
            pltpu.VMEM((width, channels), BF16),
            pltpu.VMEM(packed.shape, BF16),
            pltpu.VMEM(w_out.shape, BF16),
            pltpu.VMEM(w_neck.shape, BF16),
        ],
        in_specs=[hbm()] * 4 + [vmem()],
        out_specs=[vmem()] * 8,
        scratch_shapes=[pltpu.VMEM(w_first.shape[1:], BF16)] * 2 + [pltpu.SemaphoreType.DMA((8,))],
        compiler_params=pltpu.CompilerParams(vmem_limit_bytes=24 * 2**20),
        cost_estimate=pl.CostEstimate(flops=0, bytes_accessed=28 * 2**20, transcendentals=0),
    )(*kept, packed)
    theirs = [swap_tok(value, 1) for value in [again] + ours[1:]]
    order = far_first(zs)
    queries_n, keys_n = rows * zs, rows * tok_n
    enc_rows = own * residual.shape[3] // width
    part_shape = pltpu.VMEM((queries_n + LABEL_ROWS + enc_rows, channels), BF16)
    sent = pl.pallas_call(
        functools.partial(attention_kernel, tok_n, zs, rows, own),
        out_shape=[part_shape] * heads_n,
        in_specs=[vmem()] * (2 * zs + 2),
        out_specs=[vmem()] * heads_n,
        scratch_shapes=[
            pltpu.VMEM((queries_n, width), BF16),
            pltpu.VMEM((keys_n, width), BF16),
            pltpu.VMEM((keys_n, width), BF16),
            pltpu.VMEM((queries_n, channels), F32),
        ],
        compiler_params=pltpu.CompilerParams(vmem_limit_bytes=16 * 2**20),
    )(*[ours[d] for d in order], *[theirs[d] for d in order], out_w, joint)
    parts = [swap_heads(sent[d], d) for d in range(heads_n - 1, 0, -1)] + [sent[0]]
    half = pairwise([part[:queries_n].astype(F32) for part in parts]).astype(BF16)
    other = swap_tok(half, 1)
    slab = nt * ni
    return tuple(
        pl.pallas_call(
            functools.partial(decoder_kernel, (nc, nt, ni, own_c, zs, tok_n, heads_n)),
            out_shape=[
                jax.ShapeDtypeStruct(residual.shape, BF16),
                jax.ShapeDtypeStruct((1, 128), F32),
                jax.ShapeDtypeStruct(residual.shape, BF16),
            ],
            in_specs=[vmem()] * (9 + heads_n),
            out_specs=[vmem()] * 3,
            scratch_shapes=[
                pltpu.VMEM((nc, slab, channels), F32),
                pltpu.VMEM((4, nc // 2 * slab, 9 * channels), BF16),
                pltpu.VMEM((nc + 2, (nt + 4) * ni, channels), F32),
                pltpu.VMEM((nc + 4, (nt + 6) * ni, channels), F32),
                pltpu.VMEM(((own_c + 4) * 4 * ni, 9 * channels), BF16),
                pltpu.VMEM((nc * slab, channels), F32),
                pltpu.VMEM((nc * slab, channels), BF16),
                pltpu.VMEM((4, nc // 2 * slab, channels), F32),
            ],
            compiler_params=pltpu.CompilerParams(vmem_limit_bytes=36 * 2**20),
        )(half, other, residual, first_in, second_in, first_t, second_t, w_class, neck_w, *parts)
    )


def power_of_two(n):
    return n > 0 and n & (n - 1) == 0


def fits_whole(queries, residual, w_neck, labels):
    heads_n, tok_n = lax.axis_size("heads"), lax.axis_size("tok")
    slabs, nc, ni, width = queries.shape
    nt = labels.shape[1]
    return (
        slabs == 1
        and nc * nt <= 128
        and labels.shape[2] == 1
        and ni == LABEL_ROWS
        and nt == tok_n
        and tok_n >= 8
        and power_of_two(tok_n)
        and power_of_two(heads_n)
        and residual.shape[0] * heads_n == nc
        and nc * nt * ni <= 1024
        and (nc // 2 * nt * ni) % TILE == 0
        and nc % 2 == 0
        and width % 128 == 0
        and w_neck.shape[1] == width
        and (residual.shape[0] * ni) % 16 == 0
    )


def on_device(*arguments):
    queries, residual, w_neck, labels = (arguments[i] for i in (0, 3, 5, 9))
    if fits_whole(queries, residual, w_neck, labels):
        encoded, loss, grad = whole_grid(*arguments)
        return (encoded, loss[0, 0], grad)
    return on_tiles(*arguments)


def solution(mesh):
    placed = (
        P("tok", None, None, "heads"),
        P("tok", None, None, "heads"),
        P("tok", None, None, "heads"),
        P("heads", "tok", None, None),
        P("heads", None),
        P(),
        P(),
        P(),
        P(),
        P("heads", None, "tok"),
    )
    return jax.shard_map(
        on_device,
        mesh=mesh,
        in_specs=placed,
        out_specs=(P("heads", "tok", None, None), P(), P("heads", "tok", None, None)),
        check_vma=False,
    )
```

```python
import functools

import jax
import jax.numpy as jnp
from jax import lax
from jax.experimental import pallas as pl
from jax.experimental.pallas import tpu as pltpu
from jax.sharding import PartitionSpec as P

HD = 64
F32 = jnp.float32
BF16 = jnp.bfloat16
LABEL_ROWS = 8
TILE = 128


OFFSETS = [
    (along_c, along_t, along_x)
    for along_c in range(3)
    for along_t in range(3)
    for along_x in range(3)
]
LOSS_SCALE = 64.0
NEG_LARGE = -1e30


def padded_2(value, sides, width):
    for axis, dim in sides:
        size, length = (lax.axis_size(axis), value.shape[dim])
        up = [(i, (i + 1) % size) for i in range(size - 1)]
        down = [(j, i) for i, j in up]
        last = lax.slice_in_dim(value, length - width, length, axis=dim)
        first = lax.slice_in_dim(value, 0, width, axis=dim)
        before = lax.ppermute(last, axis, up)
        after = lax.ppermute(first, axis, down)
        value = jnp.concatenate([before, value, after], axis=dim)
    return value


def silu_slope(volume):
    sigma = jax.nn.sigmoid(volume)
    return sigma * (1.0 + volume * (1.0 - sigma))


def with_rims(volume):
    padded = padded_2(volume, (("heads", 0), ("tok", 2)), 1)
    return jnp.pad(padded, ((0, 0), (1, 1), (0, 0), (0, 0)))


def conv_apply(volume, weights, flipped):
    extent = volume.shape[:3]
    padded = with_rims(volume)
    pieces = []
    for along_c, along_t, along_x in OFFSETS:
        if flipped:
            anchor = (2 - along_c, 2 - along_t, 2 - along_x)
        else:
            anchor = (along_c, along_t, along_x)
        pieces.append(
            padded[
                anchor[0] : anchor[0] + extent[0],
                anchor[1] : anchor[1] + extent[1],
                anchor[2] : anchor[2] + extent[2],
            ]
        )
    stacked = jnp.stack(pieces, axis=3)
    columns = stacked.reshape(extent[0] * extent[1] * extent[2], 27, volume.shape[3])
    kernel = weights.reshape(27, weights.shape[3], weights.shape[4])
    if flipped:
        contraction = (((1, 2), (0, 2)), ((), ()))
    else:
        contraction = (((1, 2), (0, 1)), ((), ()))
    return lax.dot_general(columns, kernel, contraction, preferred_element_type=jnp.float32)


def online_step(carried, query_block, key_block, value_block, scale):
    row_peak, totals, weighted_sum = carried
    scores = (
        jnp.einsum("qhd,khd->qhk", query_block, key_block, preferred_element_type=jnp.float32)
        * scale
    )
    new_peak = jnp.maximum(row_peak, jnp.max(scores, axis=-1))
    factor = jnp.exp(row_peak - new_peak)
    raw_weights = jnp.exp(scores - new_peak[:, :, None])
    totals = totals * factor + jnp.sum(raw_weights, axis=-1)
    weighted_sum = weighted_sum * factor[:, :, None] + jnp.einsum(
        "qhk,khd->qhd",
        raw_weights.astype(jnp.bfloat16),
        value_block,
        preferred_element_type=jnp.float32,
    )
    return (new_peak, totals, weighted_sum)


def on_tiles(
    queries, key_rows, value_rows, residual, w_out, w_neck, w_first, w_second, w_class, labels
):
    width_here = queries.shape[-1]
    heads_here = width_here // HD
    scale = HD ** (-0.5)
    local_queries = queries.reshape(-1, heads_here, HD)
    query_total = local_queries.shape[0]
    start_state = (
        jnp.full((query_total, heads_here), NEG_LARGE, jnp.float32),
        jnp.zeros((query_total, heads_here), jnp.float32),
        jnp.zeros((query_total, heads_here, HD), jnp.float32),
    )

    def fold_keys(carried, key_piece):
        key_flat = key_piece[0].reshape(-1, heads_here, HD)
        value_flat = key_piece[1].reshape(-1, heads_here, HD)
        key_total = key_flat.shape[0]
        if key_total > 512 and key_total % 512 == 0:
            key_blocks = key_flat.reshape(key_total // 512, 512, heads_here, HD)
            value_blocks = value_flat.reshape(key_total // 512, 512, heads_here, HD)

            def scan_step(inner, paired):
                return (online_step(inner, local_queries, paired[0], paired[1], scale), None)

            return lax.scan(scan_step, carried, (key_blocks, value_blocks))[0]
        return online_step(carried, local_queries, key_flat, value_flat, scale)

    row_peak, totals, weighted_sum = fold_keys(
        start_state,
        (
            lax.all_gather(key_rows, "tok", axis=0, tiled=True),
            lax.all_gather(value_rows, "tok", axis=0, tiled=True),
        ),
    )
    attended = (weighted_sum / totals[:, :, None]).astype(jnp.bfloat16)
    attended_grid = attended.reshape(queries.shape)
    owned = lax.all_to_all(attended_grid, "heads", split_axis=1, concat_axis=3, tiled=True)
    attention_out = jnp.einsum(
        "tzxe,ed->ztxd",
        owned,
        lax.all_gather(w_out, "heads", axis=0, tiled=True),
        preferred_element_type=jnp.float32,
    )
    encoded = (residual.astype(jnp.float32) + attention_out).astype(jnp.bfloat16)
    tiled = lax.all_to_all(encoded, "tok", split_axis=2, concat_axis=1, tiled=True)
    neck_feats = jnp.einsum(
        "ztxd,dc->ztxc", tiled, w_neck, preferred_element_type=jnp.float32
    ).astype(jnp.bfloat16)
    extent = neck_feats.shape[:3]
    channels = w_neck.shape[1]
    cell_count = extent[0] * extent[1] * extent[2]
    hidden_one = conv_apply(neck_feats, w_first, False)
    active_one = jax.nn.silu(hidden_one).astype(jnp.bfloat16)
    hidden_two = conv_apply(active_one.reshape(extent + (channels,)), w_second, False)
    active_two = jax.nn.silu(hidden_two).astype(jnp.bfloat16)
    logits = jnp.dot(active_two, w_class, preferred_element_type=jnp.float32)
    probability = jax.nn.sigmoid(logits)
    fault_mask = labels.reshape(cell_count).astype(jnp.float32)
    intersection, total_prob, total_fault = lax.psum(
        (jnp.sum(probability * fault_mask), jnp.sum(probability), jnp.sum(fault_mask)),
        ("heads", "tok"),
    )
    dice_denominator = total_prob + total_fault
    dice_loss = 1.0 - 2.0 * intersection / dice_denominator
    cells_all = float(cell_count * lax.axis_size("heads") * lax.axis_size("tok"))
    grad_logits = (
        LOSS_SCALE
        * cells_all
        * -2.0
        * (fault_mask * dice_denominator - intersection)
        / (dice_denominator * dice_denominator)
        * probability
        * (1.0 - probability)
    )
    grad_hidden_two = (
        grad_logits[:, None] * w_class.astype(jnp.float32)[None, :] * silu_slope(hidden_two)
    ).astype(jnp.bfloat16)
    grad_active_one = conv_apply(grad_hidden_two.reshape(extent + (channels,)), w_second, True)
    grad_hidden_one = (grad_active_one * silu_slope(hidden_one)).astype(jnp.bfloat16)
    grad_neck = (
        conv_apply(grad_hidden_one.reshape(extent + (channels,)), w_first, True)
        .astype(jnp.bfloat16)
        .reshape(extent + (channels,))
    )
    grad_tiles = jnp.einsum(
        "ztxc,dc->ztxd", grad_neck, w_neck, preferred_element_type=jnp.float32
    ).astype(jnp.bfloat16)
    grad_encoded = lax.all_to_all(grad_tiles, "tok", split_axis=1, concat_axis=2, tiled=True)
    return (encoded, dice_loss, grad_encoded)


def dot(a, b):
    return jnp.dot(a, b, preferred_element_type=F32)


def dot_t(a, b):
    return lax.dot_general(a, b, (((1,), (1,)), ((), ())), preferred_element_type=F32)


def sigma_of(v):
    return 1.0 / (1.0 + jnp.exp(-v))


def slope_of(v):
    s = sigma_of(v)
    return s * (1.0 + v * (1.0 - s))


def iota(shape, dim):
    return lax.broadcasted_iota(jnp.int32, shape, dim)


def along_inline(value, step, inline):
    if step == 0:
        return value
    rows = value.shape[0]
    x = iota(value.shape, 0) % inline
    edge = inline - 1 if step > 0 else 0
    return jnp.where(x == edge, 0.0, pltpu.roll(value, (-step) % rows, axis=0))


def along_rows(value, step):
    if step == 0:
        return value
    zeros = jnp.zeros((abs(step), value.shape[1]), value.dtype)
    if step > 0:
        return jnp.concatenate([value[step:], zeros], axis=0)
    return jnp.concatenate([zeros, value[:step]], axis=0)


def place_of(tok_n):
    h, t = lax.axis_index("heads"), lax.axis_index("tok")
    return h, t // 2, t % 2, t


def pack_kernel(tok_n, q_ref, k_ref, v_ref, r_ref, neck_ref, lab_ref, out_ref):
    h, _, _, t = place_of(tok_n)
    rows = q_ref.shape[1] * q_ref.shape[2]
    width = q_ref.shape[3]
    for i, ref in enumerate((q_ref, k_ref, v_ref)):
        flat = ref[...].astype(F32).reshape(rows, width).astype(BF16)
        out_ref[i * rows : (i + 1) * rows, :] = flat
    own = r_ref.shape[0] * r_ref.shape[2]
    residual = r_ref[...].astype(F32).reshape(own, r_ref.shape[3]).astype(BF16)
    out_ref[3 * rows : 3 * rows + own, :] = dot(residual, neck_ref[...]).astype(BF16)
    own_c, _, nt = lab_ref.shape
    spread = jnp.zeros((LABEL_ROWS, width), F32)
    for c in range(own_c):
        row = jnp.broadcast_to(lab_ref[c].astype(F32), (LABEL_ROWS, nt)).astype(BF16)
        at = (h * own_c + c) * nt + iota((nt, width), 0)
        spread = spread + dot(row, (iota((nt, width), 1) == at).astype(F32).astype(BF16))
    out_ref[3 * rows + own :, :] = jnp.where(
        iota((LABEL_ROWS, width), 0) == t, spread, 0.0
    ).astype(BF16)


def weights_kernel(first_ref, second_ref, out_ref, neck_ref, packed_ref, *refs):
    first_in, second_in, first_t, second_t, joint, again, out_w, neck_w = refs[:8]
    first_mid, second_mid, sems = refs[8:]
    small = [
        pltpu.make_async_copy(out_ref, out_w, sems.at[6]),
        pltpu.make_async_copy(neck_ref, neck_w, sems.at[7]),
    ]
    for copy in small:
        copy.start()
    sets = (
        (first_ref, first_in, first_mid, first_t),
        (second_ref, second_in, second_mid, second_t),
    )
    copies = []
    for i, (src, dst, mid, _) in enumerate(sets):
        for a, place in enumerate((dst.at[0], mid, dst.at[3])):
            copies.append(pltpu.make_async_copy(src.at[a], place, sems.at[3 * i + a]))
            copies[-1].start()
    again[...] = packed_ref[...]
    for copy in small:
        copy.wait()
    joint[...] = dot(out_w[...], neck_w[...]).astype(BF16)
    for i, (_, dst, mid, flipped) in enumerate(sets):
        for a in range(3):
            copies[3 * i + a].wait()
        for b in range(3):
            for e in range(3):
                taps = (dst[0, b, e], mid[b, e], dst[3, b, e])
                for a in range(3):
                    flipped[a, b, e] = taps[a].T
                g0, g1, g2 = (tap.astype(F32) * 0.5 for tap in taps)
                dst[1, b, e] = (g0 + g2 + g1).astype(BF16)
                dst[2, b, e] = (g0 + g2 - g1).astype(BF16)


def far_first(zs):
    return list(range(zs - 1, 2, -1)) + [1, 2, 0]


def attention_kernel(tok_n, zs, rows, own, *refs):
    order = far_first(zs)
    ours = [refs[order.index(d)] for d in range(zs)]
    theirs = [refs[zs + order.index(d)] for d in range(zs)]
    out_w, joint_w = refs[2 * zs : 2 + 2 * zs]
    part_refs = refs[2 + 2 * zs : -4]
    qq, kk, vv, part = refs[-4:]
    h, z, core, _ = place_of(tok_n)
    width = qq.shape[1]
    queries_n = qq.shape[0]
    labels = jnp.zeros((LABEL_ROWS, width), F32)
    for d in range(zs):
        qq[d * rows : (d + 1) * rows, :] = ours[d][0:rows, :]
        for ref, side in ((ours[d], core), (theirs[d], 1 - core)):
            at = pl.multiple_of((2 * (z ^ d) + side) * rows, rows)
            kk[pl.ds(at, rows), :] = ref[rows : 2 * rows, :]
            vv[pl.ds(at, rows), :] = ref[2 * rows : 3 * rows, :]
            labels = labels + ref[3 * rows + own :, :].astype(F32)
    heads_here = width // HD
    scale = HD ** (-0.5)
    query = qq[...]
    keys, values = kk[...], vv[...]
    lane_head = iota((queries_n, width), 1) // HD
    attended = jnp.zeros((queries_n, width), F32)
    for head in range(heads_here):
        mine = lane_head == head
        scores = dot_t(jnp.where(mine, query, jnp.zeros_like(query)), keys) * scale
        raw = jnp.exp(scores - jnp.max(scores, axis=1, keepdims=True))
        total = jnp.sum(raw, axis=1, keepdims=True)
        mixed = dot(raw.astype(BF16), values)
        attended = jnp.where(mine, mixed / total, attended)
    attended = attended.astype(BF16)
    part[...] = dot(attended, joint_w[...])
    for d in range(zs):
        at = pl.multiple_of(d * rows + h * own, own)
        part[pl.ds(at, own), :] += ours[d][3 * rows : 3 * rows + own, :].astype(F32)
    partial = part[...].astype(BF16)
    labels = labels.astype(BF16)
    first = dot(attended[0:rows, :], out_w[...])
    blocks = [first[i * own : (i + 1) * own, :] for i in range(rows // own)]
    sum_ref, enc_refs = part_refs[0], part_refs[1:]
    sum_ref[0:queries_n, :] = partial
    sum_ref[queries_n:, :] = labels
    for d, ref in enumerate(enc_refs):
        picked = blocks[0]
        for i in range(1, len(blocks)):
            picked = jnp.where((h ^ d) == i, blocks[i], picked)
        ref[...] = picked.astype(BF16)


def decoder_kernel(sizes, *refs):
    nc, nt, ni, own_c, zs, tok_n, parts_n = sizes
    ours, theirs, w1, w2, w1_t, w2_t, class_w, neck_w = refs[:8]
    parts = refs[8 : 8 + parts_n]
    loss_ref, grad_ref, grid, cols, slope1, grad2, cols3, slope2, act, parts_out = refs[8 + parts_n :]
    channels = grid.shape[2]
    slab = nt * ni
    rows = nc * ni
    cells = nc * slab
    h, z, core, tslab = place_of(tok_n)
    taps = 9
    for d in range(zs):
        for ref, side in ((ours, core), (theirs, 1 - core)):
            block = ref[d * rows : (d + 1) * rows, :].astype(F32)
            at = pl.multiple_of((2 * (z ^ d) + side) * ni, ni)
            for c in range(nc):
                grid[c, pl.ds(at, ni), :] = block[c * ni : (c + 1) * ni, :]

    slope1[...] = jnp.zeros_like(slope1)
    grad2[...] = jnp.zeros_like(grad2)
    def spread(value, k, i):
        for e in range(3):
            moved = along_inline(value, e - 1, ni)
            for b in range(3):
                lane = (b * 3 + e) * channels
                cols[k, i * slab : (i + 1) * slab, lane : lane + channels] = along_rows(
                    moved, (b - 1) * ni
                ).astype(BF16)

    def spread_all(volume):
        empty = jnp.zeros((slab, channels), F32)
        for i in range(nc // 2):
            d0 = volume[2 * i - 1] if i > 0 else empty
            d1, d2 = volume[2 * i], volume[2 * i + 1]
            d3 = volume[2 * i + 2] if 2 * i + 2 < nc else empty
            for k, value in enumerate((d0 - d2, d1 + d2, d2 - d1, d1 - d3)):
                spread(value, k, i)

    half_cells = cells // 2

    def conv(weights, finish):
        for m in range(0, half_cells, TILE):
            for k in range(4):
                matrix = weights[k].reshape(taps * channels, channels)
                parts_out[k, m : m + TILE, :] = dot(cols[k, m : m + TILE, :], matrix)
            for i in range(m // slab, (m + TILE) // slab):
                m0, m1, m2, m3 = (parts_out[k, i * slab : (i + 1) * slab, :] for k in range(4))
                finish(2 * i, m0 + m1 + m2)
                finish(2 * i + 1, m1 - m2 - m3)

    class_row = class_w[...].astype(F32).reshape(1, channels)

    def finish_one(c, v):
        s = sigma_of(v)
        slope1[c + 1, ni : ni + slab, :] = s * (1.0 + v * (1.0 - s))
        grid[c] = (v * s).astype(BF16).astype(F32)

    def finish_two(c, v):
        s = sigma_of(v)
        slope2[c * slab : (c + 1) * slab, :] = s * (1.0 + v * (1.0 - s)) * class_row
        act[c * slab : (c + 1) * slab, :] = (v * s).astype(BF16)

    spread_all([grid[c] for c in range(nc)])
    conv(w1, finish_one)
    spread_all([grid[c] for c in range(nc)])
    conv(w2, finish_two)
    active_two = act[...]
    logits = dot_t(active_two, jnp.broadcast_to(class_row, (128, channels)).astype(BF16))
    probability = sigma_of(logits)
    last = parts[0].shape[0] - LABEL_ROWS
    lab = pairwise([ref[last : last + ni, 0:128].astype(F32) for ref in parts])
    spread_lab = jnp.broadcast_to(lab[None], (cells // ni, ni, 128)).reshape(cells, 128)
    wanted = iota((cells, 128), 0) // ni
    picked = jnp.where(iota((cells, 128), 1) == wanted, spread_lab, 0.0).astype(BF16)
    mask = dot(picked, jnp.ones((128, 128), BF16))
    intersection = jnp.sum(probability * mask, axis=0, keepdims=True)
    total_prob = jnp.sum(probability, axis=0, keepdims=True)
    total_fault = jnp.sum(mask, axis=0, keepdims=True)
    denominator = total_prob + total_fault
    loss_ref[...] = 1.0 - 2.0 * intersection / denominator
    grad_logits = (
        LOSS_SCALE
        * float(cells)
        * -2.0
        * (mask * denominator - intersection)
        / (denominator * denominator)
        * probability
        * (1.0 - probability)
    )
    for c in range(nc):
        rows_c = slice(c * slab, (c + 1) * slab)
        wide = jnp.concatenate([grad_logits[rows_c, :]] * (channels // 128), axis=1)
        grad2[c + 2, 2 * ni : 2 * ni + slab, :] = wide * slope2[rows_c, :]

    band = 4 * ni
    c0 = h * own_c
    t0 = pl.multiple_of(tslab * ni, ni)
    for i in range(own_c + 4):
        region = grad2[c0 + i, pl.ds(t0, band + 2 * ni), :]
        for e in range(3):
            moved = along_inline(region, 1 - e, ni)
            for b in range(3):
                lane = (b * 3 + e) * channels
                cols3[i * band : (i + 1) * band, lane : lane + channels] = moved[
                    (2 - b) * ni : (2 - b) * ni + band, :
                ].astype(BF16)
    out3 = (own_c + 2) * band
    total = jnp.zeros((out3, channels), F32)
    for a in range(3):
        for b in range(3):
            for e in range(3):
                lane = (b * 3 + e) * channels
                piece = cols3[(2 - a) * band : (2 - a) * band + out3, lane : lane + channels]
                total = total + dot(piece, w2_t[a, b, e])
    slopes = [slope1[c0 + i, pl.ds(t0, band), :] for i in range(own_c + 2)]
    g1 = (total * jnp.concatenate(slopes, axis=0)).astype(BF16).astype(F32)
    shifted = [along_inline(g1, 1 - e, ni) for e in range(3)]
    total = jnp.zeros((own_c * ni, channels), F32)
    for a in range(3):
        pieces = []
        for b in range(3):
            for e in range(3):
                cells_in = [
                    shifted[e][(i + 2 - a) * band + (2 - b) * ni : (i + 2 - a) * band + (3 - b) * ni, :]
                    for i in range(own_c)
                ]
                pieces.append(jnp.concatenate(cells_in, axis=0).astype(BF16))
        matrix = w1_t[a].reshape(taps * channels, channels)
        total = total + dot(jnp.concatenate(pieces, axis=1), matrix)
    grad = dot_t(total.astype(BF16), neck_w[...])
    grad_ref[...] = grad.reshape(grad_ref.shape).astype(BF16)


def pairwise(values):
    while len(values) > 1:
        values = [values[i] + values[i + 1] for i in range(0, len(values), 2)]
    return values[0]


def vmem():
    return pl.BlockSpec(memory_space=pltpu.VMEM)


def hbm():
    return pl.BlockSpec(memory_space=pltpu.HBM)


def whole_grid(
    queries, key_rows, value_rows, residual, w_out, w_neck, w_first, w_second, w_class, labels
):
    heads_n, tok_n = lax.axis_size("heads"), lax.axis_size("tok")
    zs = tok_n // 2
    _, nc, ni, width = queries.shape
    own_c = residual.shape[0]
    nt = labels.shape[1]
    channels = w_neck.shape[1]
    rows, own = nc * ni, own_c * ni

    def swap_tok(value, bits):
        return lax.ppermute(value, "tok", [(i, i ^ bits) for i in range(tok_n)])

    def swap_heads(value, bits):
        return lax.ppermute(value, "heads", [(i, i ^ bits) for i in range(heads_n)])

    packed = pl.pallas_call(
        functools.partial(pack_kernel, tok_n),
        out_shape=pltpu.VMEM((3 * rows + own + LABEL_ROWS, width), BF16),
        in_specs=[vmem()] * 6,
        out_specs=vmem(),
    )(queries, key_rows, value_rows, residual, w_neck, labels.transpose(0, 2, 1))
    ours = [packed] + [swap_tok(packed, 2 * d) for d in range(1, zs)]
    kept = [pltpu.with_memory_space_constraint(w, pltpu.HBM) for w in (w_first, w_second, w_out, w_neck)]
    first_in, second_in, first_t, second_t, joint, again, out_w, neck_w = pl.pallas_call(
        weights_kernel,
        out_shape=[pltpu.VMEM((4,) + w_first.shape[1:], BF16)] * 2
        + [pltpu.VMEM(w_first.shape, BF16)] * 2
        + [
            pltpu.VMEM((width, channels), BF16),
            pltpu.VMEM(packed.shape, BF16),
            pltpu.VMEM(w_out.shape, BF16),
            pltpu.VMEM(w_neck.shape, BF16),
        ],
        in_specs=[hbm()] * 4 + [vmem()],
        out_specs=[vmem()] * 8,
        scratch_shapes=[pltpu.VMEM(w_first.shape[1:], BF16)] * 2 + [pltpu.SemaphoreType.DMA((8,))],
        compiler_params=pltpu.CompilerParams(vmem_limit_bytes=24 * 2**20),
        cost_estimate=pl.CostEstimate(flops=0, bytes_accessed=28 * 2**20, transcendentals=0),
    )(*kept, packed)
    theirs = [swap_tok(value, 1) for value in [again] + ours[1:]]
    order = far_first(zs)
    queries_n, keys_n = rows * zs, rows * tok_n
    part_shape = pltpu.VMEM((queries_n + LABEL_ROWS, channels), BF16)
    enc_shape = pltpu.VMEM((own, residual.shape[3]), BF16)
    sent = pl.pallas_call(
        functools.partial(attention_kernel, tok_n, zs, rows, own),
        out_shape=[part_shape] + [enc_shape] * heads_n,
        in_specs=[vmem()] * (2 * zs + 2),
        out_specs=[vmem()] * (1 + heads_n),
        scratch_shapes=[
            pltpu.VMEM((queries_n, width), BF16),
            pltpu.VMEM((keys_n, width), BF16),
            pltpu.VMEM((keys_n, width), BF16),
            pltpu.VMEM((queries_n, channels), F32),
        ],
        compiler_params=pltpu.CompilerParams(vmem_limit_bytes=16 * 2**20),
    )(*[ours[d] for d in order], *[theirs[d] for d in order], out_w, joint)
    parts = [swap_heads(sent[0], d) for d in range(heads_n - 1, 0, -1)] + [sent[0]]
    half = pairwise([part[:queries_n].astype(F32) for part in parts]).astype(BF16)
    other = swap_tok(half, 1)
    slab = nt * ni
    loss, grad = (
        pl.pallas_call(
            functools.partial(decoder_kernel, (nc, nt, ni, own_c, zs, tok_n, heads_n)),
            out_shape=[
                jax.ShapeDtypeStruct((1, 128), F32),
                jax.ShapeDtypeStruct(residual.shape, BF16),
            ],
            in_specs=[vmem()] * (8 + heads_n),
            out_specs=[vmem()] * 2,
            scratch_shapes=[
                pltpu.VMEM((nc, slab, channels), F32),
                pltpu.VMEM((4, nc // 2 * slab, 9 * channels), BF16),
                pltpu.VMEM((nc + 2, (nt + 4) * ni, channels), F32),
                pltpu.VMEM((nc + 4, (nt + 6) * ni, channels), F32),
                pltpu.VMEM(((own_c + 4) * 4 * ni, 9 * channels), BF16),
                pltpu.VMEM((nc * slab, channels), F32),
                pltpu.VMEM((nc * slab, channels), BF16),
                pltpu.VMEM((4, nc // 2 * slab, channels), F32),
            ],
            compiler_params=pltpu.CompilerParams(vmem_limit_bytes=36 * 2**20),
        )(half, other, first_in, second_in, first_t, second_t, w_class, neck_w, *parts)
    )
    pieces = [swap_heads(sent[1 + d], d) for d in range(heads_n - 1, 0, -1)] + [sent[1]]
    total = pairwise([piece.astype(F32) for piece in pieces]).reshape(residual.shape)
    encoded = (residual.astype(F32) + total).astype(BF16)
    return (encoded, loss, grad)


def power_of_two(n):
    return n > 0 and n & (n - 1) == 0


def fits_whole(queries, residual, w_neck, labels):
    heads_n, tok_n = lax.axis_size("heads"), lax.axis_size("tok")
    slabs, nc, ni, width = queries.shape
    nt = labels.shape[1]
    return (
        slabs == 1
        and nc * nt <= 128
        and labels.shape[2] == 1
        and ni == LABEL_ROWS
        and nt == tok_n
        and tok_n >= 8
        and power_of_two(tok_n)
        and power_of_two(heads_n)
        and residual.shape[0] * heads_n == nc
        and nc * nt * ni <= 1024
        and (nc // 2 * nt * ni) % TILE == 0
        and nc % 2 == 0
        and width % 128 == 0
        and w_neck.shape[1] == width
        and (residual.shape[0] * ni) % 16 == 0
    )


def on_device(*arguments):
    queries, residual, w_neck, labels = (arguments[i] for i in (0, 3, 5, 9))
    if fits_whole(queries, residual, w_neck, labels):
        encoded, loss, grad = whole_grid(*arguments)
        return (encoded, loss[0, 0], grad)
    return on_tiles(*arguments)


def solution(mesh):
    placed = (
        P("tok", None, None, "heads"),
        P("tok", None, None, "heads"),
        P("tok", None, None, "heads"),
        P("heads", "tok", None, None),
        P("heads", None),
        P(),
        P(),
        P(),
        P(),
        P("heads", None, "tok"),
    )
    return jax.shard_map(
        on_device,
        mesh=mesh,
        in_specs=placed,
        out_specs=(P("heads", "tok", None, None), P(), P("heads", "tok", None, None)),
        check_vma=False,
    )
```

```python
import functools

import jax
import jax.numpy as jnp
from jax import lax
from jax.experimental import pallas as pl
from jax.experimental.pallas import tpu as pltpu
from jax.sharding import PartitionSpec as P

HD = 64
F32 = jnp.float32
BF16 = jnp.bfloat16
LABEL_ROWS = 8
TILE = 128


OFFSETS = [
    (along_c, along_t, along_x)
    for along_c in range(3)
    for along_t in range(3)
    for along_x in range(3)
]
LOSS_SCALE = 64.0
NEG_LARGE = -1e30


def padded_2(value, sides, width):
    for axis, dim in sides:
        size, length = (lax.axis_size(axis), value.shape[dim])
        up = [(i, (i + 1) % size) for i in range(size - 1)]
        down = [(j, i) for i, j in up]
        last = lax.slice_in_dim(value, length - width, length, axis=dim)
        first = lax.slice_in_dim(value, 0, width, axis=dim)
        before = lax.ppermute(last, axis, up)
        after = lax.ppermute(first, axis, down)
        value = jnp.concatenate([before, value, after], axis=dim)
    return value


def silu_slope(volume):
    sigma = jax.nn.sigmoid(volume)
    return sigma * (1.0 + volume * (1.0 - sigma))


def with_rims(volume):
    padded = padded_2(volume, (("heads", 0), ("tok", 2)), 1)
    return jnp.pad(padded, ((0, 0), (1, 1), (0, 0), (0, 0)))


def conv_apply(volume, weights, flipped):
    extent = volume.shape[:3]
    padded = with_rims(volume)
    pieces = []
    for along_c, along_t, along_x in OFFSETS:
        if flipped:
            anchor = (2 - along_c, 2 - along_t, 2 - along_x)
        else:
            anchor = (along_c, along_t, along_x)
        pieces.append(
            padded[
                anchor[0] : anchor[0] + extent[0],
                anchor[1] : anchor[1] + extent[1],
                anchor[2] : anchor[2] + extent[2],
            ]
        )
    stacked = jnp.stack(pieces, axis=3)
    columns = stacked.reshape(extent[0] * extent[1] * extent[2], 27, volume.shape[3])
    kernel = weights.reshape(27, weights.shape[3], weights.shape[4])
    if flipped:
        contraction = (((1, 2), (0, 2)), ((), ()))
    else:
        contraction = (((1, 2), (0, 1)), ((), ()))
    return lax.dot_general(columns, kernel, contraction, preferred_element_type=jnp.float32)


def online_step(carried, query_block, key_block, value_block, scale):
    row_peak, totals, weighted_sum = carried
    scores = (
        jnp.einsum("qhd,khd->qhk", query_block, key_block, preferred_element_type=jnp.float32)
        * scale
    )
    new_peak = jnp.maximum(row_peak, jnp.max(scores, axis=-1))
    factor = jnp.exp(row_peak - new_peak)
    raw_weights = jnp.exp(scores - new_peak[:, :, None])
    totals = totals * factor + jnp.sum(raw_weights, axis=-1)
    weighted_sum = weighted_sum * factor[:, :, None] + jnp.einsum(
        "qhk,khd->qhd",
        raw_weights.astype(jnp.bfloat16),
        value_block,
        preferred_element_type=jnp.float32,
    )
    return (new_peak, totals, weighted_sum)


def on_tiles(
    queries, key_rows, value_rows, residual, w_out, w_neck, w_first, w_second, w_class, labels
):
    width_here = queries.shape[-1]
    heads_here = width_here // HD
    scale = HD ** (-0.5)
    local_queries = queries.reshape(-1, heads_here, HD)
    query_total = local_queries.shape[0]
    start_state = (
        jnp.full((query_total, heads_here), NEG_LARGE, jnp.float32),
        jnp.zeros((query_total, heads_here), jnp.float32),
        jnp.zeros((query_total, heads_here, HD), jnp.float32),
    )

    def fold_keys(carried, key_piece):
        key_flat = key_piece[0].reshape(-1, heads_here, HD)
        value_flat = key_piece[1].reshape(-1, heads_here, HD)
        key_total = key_flat.shape[0]
        if key_total > 512 and key_total % 512 == 0:
            key_blocks = key_flat.reshape(key_total // 512, 512, heads_here, HD)
            value_blocks = value_flat.reshape(key_total // 512, 512, heads_here, HD)

            def scan_step(inner, paired):
                return (online_step(inner, local_queries, paired[0], paired[1], scale), None)

            return lax.scan(scan_step, carried, (key_blocks, value_blocks))[0]
        return online_step(carried, local_queries, key_flat, value_flat, scale)

    row_peak, totals, weighted_sum = fold_keys(
        start_state,
        (
            lax.all_gather(key_rows, "tok", axis=0, tiled=True),
            lax.all_gather(value_rows, "tok", axis=0, tiled=True),
        ),
    )
    attended = (weighted_sum / totals[:, :, None]).astype(jnp.bfloat16)
    attended_grid = attended.reshape(queries.shape)
    owned = lax.all_to_all(attended_grid, "heads", split_axis=1, concat_axis=3, tiled=True)
    attention_out = jnp.einsum(
        "tzxe,ed->ztxd",
        owned,
        lax.all_gather(w_out, "heads", axis=0, tiled=True),
        preferred_element_type=jnp.float32,
    )
    encoded = (residual.astype(jnp.float32) + attention_out).astype(jnp.bfloat16)
    tiled = lax.all_to_all(encoded, "tok", split_axis=2, concat_axis=1, tiled=True)
    neck_feats = jnp.einsum(
        "ztxd,dc->ztxc", tiled, w_neck, preferred_element_type=jnp.float32
    ).astype(jnp.bfloat16)
    extent = neck_feats.shape[:3]
    channels = w_neck.shape[1]
    cell_count = extent[0] * extent[1] * extent[2]
    hidden_one = conv_apply(neck_feats, w_first, False)
    active_one = jax.nn.silu(hidden_one).astype(jnp.bfloat16)
    hidden_two = conv_apply(active_one.reshape(extent + (channels,)), w_second, False)
    active_two = jax.nn.silu(hidden_two).astype(jnp.bfloat16)
    logits = jnp.dot(active_two, w_class, preferred_element_type=jnp.float32)
    probability = jax.nn.sigmoid(logits)
    fault_mask = labels.reshape(cell_count).astype(jnp.float32)
    intersection, total_prob, total_fault = lax.psum(
        (jnp.sum(probability * fault_mask), jnp.sum(probability), jnp.sum(fault_mask)),
        ("heads", "tok"),
    )
    dice_denominator = total_prob + total_fault
    dice_loss = 1.0 - 2.0 * intersection / dice_denominator
    cells_all = float(cell_count * lax.axis_size("heads") * lax.axis_size("tok"))
    grad_logits = (
        LOSS_SCALE
        * cells_all
        * -2.0
        * (fault_mask * dice_denominator - intersection)
        / (dice_denominator * dice_denominator)
        * probability
        * (1.0 - probability)
    )
    grad_hidden_two = (
        grad_logits[:, None] * w_class.astype(jnp.float32)[None, :] * silu_slope(hidden_two)
    ).astype(jnp.bfloat16)
    grad_active_one = conv_apply(grad_hidden_two.reshape(extent + (channels,)), w_second, True)
    grad_hidden_one = (grad_active_one * silu_slope(hidden_one)).astype(jnp.bfloat16)
    grad_neck = (
        conv_apply(grad_hidden_one.reshape(extent + (channels,)), w_first, True)
        .astype(jnp.bfloat16)
        .reshape(extent + (channels,))
    )
    grad_tiles = jnp.einsum(
        "ztxc,dc->ztxd", grad_neck, w_neck, preferred_element_type=jnp.float32
    ).astype(jnp.bfloat16)
    grad_encoded = lax.all_to_all(grad_tiles, "tok", split_axis=1, concat_axis=2, tiled=True)
    return (encoded, dice_loss, grad_encoded)


def dot(a, b):
    return jnp.dot(a, b, preferred_element_type=F32)


def dot_t(a, b):
    return lax.dot_general(a, b, (((1,), (1,)), ((), ())), preferred_element_type=F32)


def sigma_of(v):
    return 1.0 / (1.0 + jnp.exp(-v))


def slope_of(v):
    s = sigma_of(v)
    return s * (1.0 + v * (1.0 - s))


def iota(shape, dim):
    return lax.broadcasted_iota(jnp.int32, shape, dim)


def along_inline(value, step, inline):
    if step == 0:
        return value
    rows = value.shape[0]
    x = iota(value.shape, 0) % inline
    edge = inline - 1 if step > 0 else 0
    return jnp.where(x == edge, 0.0, pltpu.roll(value, (-step) % rows, axis=0))


def along_rows(value, step):
    if step == 0:
        return value
    zeros = jnp.zeros((abs(step), value.shape[1]), value.dtype)
    if step > 0:
        return jnp.concatenate([value[step:], zeros], axis=0)
    return jnp.concatenate([zeros, value[:step]], axis=0)


def place_of(tok_n):
    h, t = lax.axis_index("heads"), lax.axis_index("tok")
    return h, t // 2, t % 2, t


def pack_kernel(tok_n, q_ref, k_ref, v_ref, r_ref, neck_ref, lab_ref, out_ref):
    h, _, _, t = place_of(tok_n)
    rows = q_ref.shape[1] * q_ref.shape[2]
    width = q_ref.shape[3]
    for i, ref in enumerate((q_ref, k_ref, v_ref)):
        flat = ref[...].astype(F32).reshape(rows, width).astype(BF16)
        out_ref[i * rows : (i + 1) * rows, :] = flat
    own = r_ref.shape[0] * r_ref.shape[2]
    residual = r_ref[...].astype(F32).reshape(own, r_ref.shape[3]).astype(BF16)
    out_ref[3 * rows : 3 * rows + own, :] = dot(residual, neck_ref[...]).astype(BF16)
    own_c, _, nt = lab_ref.shape
    spread = jnp.zeros((LABEL_ROWS, width), F32)
    for c in range(own_c):
        row = jnp.broadcast_to(lab_ref[c].astype(F32), (LABEL_ROWS, nt)).astype(BF16)
        at = (h * own_c + c) * nt + iota((nt, width), 0)
        spread = spread + dot(row, (iota((nt, width), 1) == at).astype(F32).astype(BF16))
    out_ref[3 * rows + own :, :] = jnp.where(
        iota((LABEL_ROWS, width), 0) == t, spread, 0.0
    ).astype(BF16)


def weights_kernel(first_ref, second_ref, out_ref, neck_ref, packed_ref, *refs):
    first_in, second_in, first_t, second_t, joint, again, out_w, neck_w = refs[:8]
    first_mid, second_mid, sems = refs[8:]
    small = [
        pltpu.make_async_copy(out_ref, out_w, sems.at[6]),
        pltpu.make_async_copy(neck_ref, neck_w, sems.at[7]),
    ]
    for copy in small:
        copy.start()
    sets = (
        (first_ref, first_in, first_mid, first_t),
        (second_ref, second_in, second_mid, second_t),
    )
    copies = []
    for i, (src, dst, mid, _) in enumerate(sets):
        for a, place in enumerate((dst.at[0], mid, dst.at[3])):
            copies.append(pltpu.make_async_copy(src.at[a], place, sems.at[3 * i + a]))
            copies[-1].start()
    again[...] = packed_ref[...]
    for copy in small:
        copy.wait()
    joint[...] = dot(out_w[...], neck_w[...]).astype(BF16)
    for i, (_, dst, mid, flipped) in enumerate(sets):
        for a in range(3):
            copies[3 * i + a].wait()
        for b in range(3):
            for e in range(3):
                taps = (dst[0, b, e], mid[b, e], dst[3, b, e])
                for a in range(3):
                    flipped[a, b, e] = taps[a].T
                g0, g1, g2 = (tap.astype(F32) * 0.5 for tap in taps)
                dst[1, b, e] = (g0 + g2 + g1).astype(BF16)
                dst[2, b, e] = (g0 + g2 - g1).astype(BF16)


def far_first(zs):
    return list(range(zs - 1, 2, -1)) + [1, 2, 0]


def attention_kernel(tok_n, zs, rows, own, *refs):
    order = far_first(zs)
    ours = [refs[order.index(d)] for d in range(zs)]
    theirs = [refs[zs + order.index(d)] for d in range(zs)]
    joint_w, sum_ref, own_ref = refs[2 * zs : 3 + 2 * zs]
    qq, kk, vv, part = refs[-4:]
    h, z, core, _ = place_of(tok_n)
    width = qq.shape[1]
    queries_n = qq.shape[0]
    labels = jnp.zeros((LABEL_ROWS, width), F32)
    for d in range(zs):
        qq[d * rows : (d + 1) * rows, :] = ours[d][0:rows, :]
        for ref, side in ((ours[d], core), (theirs[d], 1 - core)):
            at = pl.multiple_of((2 * (z ^ d) + side) * rows, rows)
            kk[pl.ds(at, rows), :] = ref[rows : 2 * rows, :]
            vv[pl.ds(at, rows), :] = ref[2 * rows : 3 * rows, :]
            labels = labels + ref[3 * rows + own :, :].astype(F32)
    heads_here = width // HD
    scale = HD ** (-0.5)
    query = qq[...]
    keys, values = kk[...], vv[...]
    lane_head = iota((queries_n, width), 1) // HD
    attended = jnp.zeros((queries_n, width), F32)
    for head in range(heads_here):
        mine = lane_head == head
        scores = dot_t(jnp.where(mine, query, jnp.zeros_like(query)), keys) * scale
        raw = jnp.exp(scores - jnp.max(scores, axis=1, keepdims=True))
        total = jnp.sum(raw, axis=1, keepdims=True)
        mixed = dot(raw.astype(BF16), values)
        attended = jnp.where(mine, mixed / total, attended)
    attended = attended.astype(BF16)
    part[...] = dot(attended, joint_w[...])
    for d in range(zs):
        at = pl.multiple_of(d * rows + h * own, own)
        part[pl.ds(at, own), :] += ours[d][3 * rows : 3 * rows + own, :].astype(F32)
    partial = part[...].astype(BF16)
    labels = labels.astype(BF16)
    own_ref[...] = attended[0:rows, :]
    sum_ref[0:queries_n, :] = partial
    sum_ref[queries_n:, :] = labels


def output_kernel(tok_n, attended, out_w, *enc_refs):
    h, _, _, _ = place_of(tok_n)
    first = dot(attended[...], out_w[...])
    own = enc_refs[0].shape[0]
    blocks = [first[i * own : (i + 1) * own, :] for i in range(first.shape[0] // own)]
    for d, ref in enumerate(enc_refs):
        picked = blocks[0]
        for i in range(1, len(blocks)):
            picked = jnp.where((h ^ d) == i, blocks[i], picked)
        ref[...] = picked.astype(BF16)


def decoder_kernel(sizes, *refs):
    nc, nt, ni, own_c, zs, tok_n, parts_n = sizes
    ours, theirs, w1, w2, w1_t, w2_t, class_w, neck_w = refs[:8]
    parts = refs[8 : 8 + parts_n]
    loss_ref, grad_ref, grid, cols, slope1, grad2, cols3, slope2, act, parts_out = refs[8 + parts_n :]
    channels = grid.shape[2]
    slab = nt * ni
    rows = nc * ni
    cells = nc * slab
    h, z, core, tslab = place_of(tok_n)
    taps = 9
    for d in range(zs):
        for ref, side in ((ours, core), (theirs, 1 - core)):
            block = ref[d * rows : (d + 1) * rows, :].astype(F32)
            at = pl.multiple_of((2 * (z ^ d) + side) * ni, ni)
            for c in range(nc):
                grid[c, pl.ds(at, ni), :] = block[c * ni : (c + 1) * ni, :]

    slope1[...] = jnp.zeros_like(slope1)
    grad2[...] = jnp.zeros_like(grad2)
    def spread(value, k, i):
        for e in range(3):
            moved = along_inline(value, e - 1, ni)
            for b in range(3):
                lane = (b * 3 + e) * channels
                cols[k, i * slab : (i + 1) * slab, lane : lane + channels] = along_rows(
                    moved, (b - 1) * ni
                ).astype(BF16)

    def spread_all(volume):
        empty = jnp.zeros((slab, channels), F32)
        for i in range(nc // 2):
            d0 = volume[2 * i - 1] if i > 0 else empty
            d1, d2 = volume[2 * i], volume[2 * i + 1]
            d3 = volume[2 * i + 2] if 2 * i + 2 < nc else empty
            for k, value in enumerate((d0 - d2, d1 + d2, d2 - d1, d1 - d3)):
                spread(value, k, i)

    half_cells = cells // 2

    def conv(weights, finish):
        for m in range(0, half_cells, TILE):
            for k in range(4):
                matrix = weights[k].reshape(taps * channels, channels)
                parts_out[k, m : m + TILE, :] = dot(cols[k, m : m + TILE, :], matrix)
            for i in range(m // slab, (m + TILE) // slab):
                m0, m1, m2, m3 = (parts_out[k, i * slab : (i + 1) * slab, :] for k in range(4))
                finish(2 * i, m0 + m1 + m2)
                finish(2 * i + 1, m1 - m2 - m3)

    class_row = class_w[...].astype(F32).reshape(1, channels)

    def finish_one(c, v):
        s = sigma_of(v)
        slope1[c + 1, ni : ni + slab, :] = s * (1.0 + v * (1.0 - s))
        grid[c] = (v * s).astype(BF16).astype(F32)

    def finish_two(c, v):
        s = sigma_of(v)
        slope2[c * slab : (c + 1) * slab, :] = s * (1.0 + v * (1.0 - s)) * class_row
        act[c * slab : (c + 1) * slab, :] = (v * s).astype(BF16)

    spread_all([grid[c] for c in range(nc)])
    conv(w1, finish_one)
    spread_all([grid[c] for c in range(nc)])
    conv(w2, finish_two)
    active_two = act[...]
    logits = dot_t(active_two, jnp.broadcast_to(class_row, (128, channels)).astype(BF16))
    probability = sigma_of(logits)
    last = parts[0].shape[0] - LABEL_ROWS
    lab = pairwise([ref[last : last + ni, 0:128].astype(F32) for ref in parts])
    spread_lab = jnp.broadcast_to(lab[None], (cells // ni, ni, 128)).reshape(cells, 128)
    wanted = iota((cells, 128), 0) // ni
    picked = jnp.where(iota((cells, 128), 1) == wanted, spread_lab, 0.0).astype(BF16)
    mask = dot(picked, jnp.ones((128, 128), BF16))
    intersection = jnp.sum(probability * mask, axis=0, keepdims=True)
    total_prob = jnp.sum(probability, axis=0, keepdims=True)
    total_fault = jnp.sum(mask, axis=0, keepdims=True)
    denominator = total_prob + total_fault
    loss_ref[...] = 1.0 - 2.0 * intersection / denominator
    grad_logits = (
        LOSS_SCALE
        * float(cells)
        * -2.0
        * (mask * denominator - intersection)
        / (denominator * denominator)
        * probability
        * (1.0 - probability)
    )
    for c in range(nc):
        rows_c = slice(c * slab, (c + 1) * slab)
        wide = jnp.concatenate([grad_logits[rows_c, :]] * (channels // 128), axis=1)
        grad2[c + 2, 2 * ni : 2 * ni + slab, :] = wide * slope2[rows_c, :]

    band = 4 * ni
    c0 = h * own_c
    t0 = pl.multiple_of(tslab * ni, ni)
    for i in range(own_c + 4):
        region = grad2[c0 + i, pl.ds(t0, band + 2 * ni), :]
        for e in range(3):
            moved = along_inline(region, 1 - e, ni)
            for b in range(3):
                lane = (b * 3 + e) * channels
                cols3[i * band : (i + 1) * band, lane : lane + channels] = moved[
                    (2 - b) * ni : (2 - b) * ni + band, :
                ].astype(BF16)
    out3 = (own_c + 2) * band
    total = jnp.zeros((out3, channels), F32)
    for a in range(3):
        for b in range(3):
            for e in range(3):
                lane = (b * 3 + e) * channels
                piece = cols3[(2 - a) * band : (2 - a) * band + out3, lane : lane + channels]
                total = total + dot(piece, w2_t[a, b, e])
    slopes = [slope1[c0 + i, pl.ds(t0, band), :] for i in range(own_c + 2)]
    g1 = (total * jnp.concatenate(slopes, axis=0)).astype(BF16).astype(F32)
    shifted = [along_inline(g1, 1 - e, ni) for e in range(3)]
    total = jnp.zeros((own_c * ni, channels), F32)
    for a in range(3):
        pieces = []
        for b in range(3):
            for e in range(3):
                cells_in = [
                    shifted[e][(i + 2 - a) * band + (2 - b) * ni : (i + 2 - a) * band + (3 - b) * ni, :]
                    for i in range(own_c)
                ]
                pieces.append(jnp.concatenate(cells_in, axis=0).astype(BF16))
        matrix = w1_t[a].reshape(taps * channels, channels)
        total = total + dot(jnp.concatenate(pieces, axis=1), matrix)
    grad = dot_t(total.astype(BF16), neck_w[...])
    grad_ref[...] = grad.reshape(grad_ref.shape).astype(BF16)


def pairwise(values):
    while len(values) > 1:
        values = [values[i] + values[i + 1] for i in range(0, len(values), 2)]
    return values[0]


def vmem():
    return pl.BlockSpec(memory_space=pltpu.VMEM)


def hbm():
    return pl.BlockSpec(memory_space=pltpu.HBM)


def whole_grid(
    queries, key_rows, value_rows, residual, w_out, w_neck, w_first, w_second, w_class, labels
):
    heads_n, tok_n = lax.axis_size("heads"), lax.axis_size("tok")
    zs = tok_n // 2
    _, nc, ni, width = queries.shape
    own_c = residual.shape[0]
    nt = labels.shape[1]
    channels = w_neck.shape[1]
    rows, own = nc * ni, own_c * ni

    def swap_tok(value, bits):
        return lax.ppermute(value, "tok", [(i, i ^ bits) for i in range(tok_n)])

    def swap_heads(value, bits):
        return lax.ppermute(value, "heads", [(i, i ^ bits) for i in range(heads_n)])

    packed = pl.pallas_call(
        functools.partial(pack_kernel, tok_n),
        out_shape=pltpu.VMEM((3 * rows + own + LABEL_ROWS, width), BF16),
        in_specs=[vmem()] * 6,
        out_specs=vmem(),
    )(queries, key_rows, value_rows, residual, w_neck, labels.transpose(0, 2, 1))
    ours = [packed] + [swap_tok(packed, 2 * d) for d in range(1, zs)]
    kept = [pltpu.with_memory_space_constraint(w, pltpu.HBM) for w in (w_first, w_second, w_out, w_neck)]
    first_in, second_in, first_t, second_t, joint, again, out_w, neck_w = pl.pallas_call(
        weights_kernel,
        out_shape=[pltpu.VMEM((4,) + w_first.shape[1:], BF16)] * 2
        + [pltpu.VMEM(w_first.shape, BF16)] * 2
        + [
            pltpu.VMEM((width, channels), BF16),
            pltpu.VMEM(packed.shape, BF16),
            pltpu.VMEM(w_out.shape, BF16),
            pltpu.VMEM(w_neck.shape, BF16),
        ],
        in_specs=[hbm()] * 4 + [vmem()],
        out_specs=[vmem()] * 8,
        scratch_shapes=[pltpu.VMEM(w_first.shape[1:], BF16)] * 2 + [pltpu.SemaphoreType.DMA((8,))],
        compiler_params=pltpu.CompilerParams(vmem_limit_bytes=24 * 2**20),
        cost_estimate=pl.CostEstimate(flops=0, bytes_accessed=28 * 2**20, transcendentals=0),
    )(*kept, packed)
    theirs = [swap_tok(value, 1) for value in [again] + ours[1:]]
    order = far_first(zs)
    queries_n, keys_n = rows * zs, rows * tok_n
    part_shape = pltpu.VMEM((queries_n + LABEL_ROWS, channels), BF16)
    enc_shape = pltpu.VMEM((own, residual.shape[3]), BF16)
    message, attended = pl.pallas_call(
        functools.partial(attention_kernel, tok_n, zs, rows, own),
        out_shape=[part_shape, pltpu.VMEM((rows, width), BF16)],
        in_specs=[vmem()] * (2 * zs + 1),
        out_specs=[vmem()] * 2,
        scratch_shapes=[
            pltpu.VMEM((queries_n, width), BF16),
            pltpu.VMEM((keys_n, width), BF16),
            pltpu.VMEM((keys_n, width), BF16),
            pltpu.VMEM((queries_n, channels), F32),
        ],
        compiler_params=pltpu.CompilerParams(vmem_limit_bytes=16 * 2**20),
    )(*[ours[d] for d in order], *[theirs[d] for d in order], joint)
    parts = [message] + [swap_heads(message, d) for d in range(1, heads_n)]
    sent = pl.pallas_call(
        functools.partial(output_kernel, tok_n),
        out_shape=[enc_shape] * heads_n,
        in_specs=[vmem()] * 2,
        out_specs=[vmem()] * heads_n,
        compiler_params=pltpu.CompilerParams(vmem_limit_bytes=16 * 2**20),
    )(attended, out_w)
    half = pairwise([part[:queries_n].astype(F32) for part in parts]).astype(BF16)
    other = swap_tok(half, 1)
    slab = nt * ni
    loss, grad = (
        pl.pallas_call(
            functools.partial(decoder_kernel, (nc, nt, ni, own_c, zs, tok_n, heads_n)),
            out_shape=[
                jax.ShapeDtypeStruct((1, 128), F32),
                jax.ShapeDtypeStruct(residual.shape, BF16),
            ],
            in_specs=[vmem()] * (8 + heads_n),
            out_specs=[vmem()] * 2,
            scratch_shapes=[
                pltpu.VMEM((nc, slab, channels), F32),
                pltpu.VMEM((4, nc // 2 * slab, 9 * channels), BF16),
                pltpu.VMEM((nc + 2, (nt + 4) * ni, channels), F32),
                pltpu.VMEM((nc + 4, (nt + 6) * ni, channels), F32),
                pltpu.VMEM(((own_c + 4) * 4 * ni, 9 * channels), BF16),
                pltpu.VMEM((nc * slab, channels), F32),
                pltpu.VMEM((nc * slab, channels), BF16),
                pltpu.VMEM((4, nc // 2 * slab, channels), F32),
            ],
            compiler_params=pltpu.CompilerParams(vmem_limit_bytes=36 * 2**20),
        )(half, other, first_in, second_in, first_t, second_t, w_class, neck_w, *parts)
    )
    pieces = [swap_heads(sent[d], d) for d in range(heads_n - 1, 0, -1)] + [sent[0]]
    total = pairwise([piece.astype(F32) for piece in pieces]).reshape(residual.shape)
    encoded = (residual.astype(F32) + total).astype(BF16)
    return (encoded, loss, grad)


def power_of_two(n):
    return n > 0 and n & (n - 1) == 0


def fits_whole(queries, residual, w_neck, labels):
    heads_n, tok_n = lax.axis_size("heads"), lax.axis_size("tok")
    slabs, nc, ni, width = queries.shape
    nt = labels.shape[1]
    return (
        slabs == 1
        and nc * nt <= 128
        and labels.shape[2] == 1
        and ni == LABEL_ROWS
        and nt == tok_n
        and tok_n >= 8
        and power_of_two(tok_n)
        and power_of_two(heads_n)
        and residual.shape[0] * heads_n == nc
        and nc * nt * ni <= 1024
        and (nc // 2 * nt * ni) % TILE == 0
        and nc % 2 == 0
        and width % 128 == 0
        and w_neck.shape[1] == width
        and (residual.shape[0] * ni) % 16 == 0
    )


def on_device(*arguments):
    queries, residual, w_neck, labels = (arguments[i] for i in (0, 3, 5, 9))
    if fits_whole(queries, residual, w_neck, labels):
        encoded, loss, grad = whole_grid(*arguments)
        return (encoded, loss[0, 0], grad)
    return on_tiles(*arguments)


def solution(mesh):
    placed = (
        P("tok", None, None, "heads"),
        P("tok", None, None, "heads"),
        P("tok", None, None, "heads"),
        P("heads", "tok", None, None),
        P("heads", None),
        P(),
        P(),
        P(),
        P(),
        P("heads", None, "tok"),
    )
    return jax.shard_map(
        on_device,
        mesh=mesh,
        in_specs=placed,
        out_specs=(P("heads", "tok", None, None), P(), P("heads", "tok", None, None)),
        check_vma=False,
    )
```

```python
import functools

import jax
import jax.numpy as jnp
from jax import lax
from jax.experimental import pallas as pl
from jax.experimental.pallas import tpu as pltpu
from jax.sharding import PartitionSpec as P

HD = 64
F32 = jnp.float32
BF16 = jnp.bfloat16
LABEL_ROWS = 8
TILE = 128


OFFSETS = [
    (along_c, along_t, along_x)
    for along_c in range(3)
    for along_t in range(3)
    for along_x in range(3)
]
LOSS_SCALE = 64.0
NEG_LARGE = -1e30


def padded_2(value, sides, width):
    for axis, dim in sides:
        size, length = (lax.axis_size(axis), value.shape[dim])
        up = [(i, (i + 1) % size) for i in range(size - 1)]
        down = [(j, i) for i, j in up]
        last = lax.slice_in_dim(value, length - width, length, axis=dim)
        first = lax.slice_in_dim(value, 0, width, axis=dim)
        before = lax.ppermute(last, axis, up)
        after = lax.ppermute(first, axis, down)
        value = jnp.concatenate([before, value, after], axis=dim)
    return value


def silu_slope(volume):
    sigma = jax.nn.sigmoid(volume)
    return sigma * (1.0 + volume * (1.0 - sigma))


def with_rims(volume):
    padded = padded_2(volume, (("heads", 0), ("tok", 2)), 1)
    return jnp.pad(padded, ((0, 0), (1, 1), (0, 0), (0, 0)))


def conv_apply(volume, weights, flipped):
    extent = volume.shape[:3]
    padded = with_rims(volume)
    pieces = []
    for along_c, along_t, along_x in OFFSETS:
        if flipped:
            anchor = (2 - along_c, 2 - along_t, 2 - along_x)
        else:
            anchor = (along_c, along_t, along_x)
        pieces.append(
            padded[
                anchor[0] : anchor[0] + extent[0],
                anchor[1] : anchor[1] + extent[1],
                anchor[2] : anchor[2] + extent[2],
            ]
        )
    stacked = jnp.stack(pieces, axis=3)
    columns = stacked.reshape(extent[0] * extent[1] * extent[2], 27, volume.shape[3])
    kernel = weights.reshape(27, weights.shape[3], weights.shape[4])
    if flipped:
        contraction = (((1, 2), (0, 2)), ((), ()))
    else:
        contraction = (((1, 2), (0, 1)), ((), ()))
    return lax.dot_general(columns, kernel, contraction, preferred_element_type=jnp.float32)


def online_step(carried, query_block, key_block, value_block, scale):
    row_peak, totals, weighted_sum = carried
    scores = (
        jnp.einsum("qhd,khd->qhk", query_block, key_block, preferred_element_type=jnp.float32)
        * scale
    )
    new_peak = jnp.maximum(row_peak, jnp.max(scores, axis=-1))
    factor = jnp.exp(row_peak - new_peak)
    raw_weights = jnp.exp(scores - new_peak[:, :, None])
    totals = totals * factor + jnp.sum(raw_weights, axis=-1)
    weighted_sum = weighted_sum * factor[:, :, None] + jnp.einsum(
        "qhk,khd->qhd",
        raw_weights.astype(jnp.bfloat16),
        value_block,
        preferred_element_type=jnp.float32,
    )
    return (new_peak, totals, weighted_sum)


def on_tiles(
    queries, key_rows, value_rows, residual, w_out, w_neck, w_first, w_second, w_class, labels
):
    width_here = queries.shape[-1]
    heads_here = width_here // HD
    scale = HD ** (-0.5)
    local_queries = queries.reshape(-1, heads_here, HD)
    query_total = local_queries.shape[0]
    start_state = (
        jnp.full((query_total, heads_here), NEG_LARGE, jnp.float32),
        jnp.zeros((query_total, heads_here), jnp.float32),
        jnp.zeros((query_total, heads_here, HD), jnp.float32),
    )

    def fold_keys(carried, key_piece):
        key_flat = key_piece[0].reshape(-1, heads_here, HD)
        value_flat = key_piece[1].reshape(-1, heads_here, HD)
        key_total = key_flat.shape[0]
        if key_total > 512 and key_total % 512 == 0:
            key_blocks = key_flat.reshape(key_total // 512, 512, heads_here, HD)
            value_blocks = value_flat.reshape(key_total // 512, 512, heads_here, HD)

            def scan_step(inner, paired):
                return (online_step(inner, local_queries, paired[0], paired[1], scale), None)

            return lax.scan(scan_step, carried, (key_blocks, value_blocks))[0]
        return online_step(carried, local_queries, key_flat, value_flat, scale)

    row_peak, totals, weighted_sum = fold_keys(
        start_state,
        (
            lax.all_gather(key_rows, "tok", axis=0, tiled=True),
            lax.all_gather(value_rows, "tok", axis=0, tiled=True),
        ),
    )
    attended = (weighted_sum / totals[:, :, None]).astype(jnp.bfloat16)
    attended_grid = attended.reshape(queries.shape)
    owned = lax.all_to_all(attended_grid, "heads", split_axis=1, concat_axis=3, tiled=True)
    attention_out = jnp.einsum(
        "tzxe,ed->ztxd",
        owned,
        lax.all_gather(w_out, "heads", axis=0, tiled=True),
        preferred_element_type=jnp.float32,
    )
    encoded = (residual.astype(jnp.float32) + attention_out).astype(jnp.bfloat16)
    tiled = lax.all_to_all(encoded, "tok", split_axis=2, concat_axis=1, tiled=True)
    neck_feats = jnp.einsum(
        "ztxd,dc->ztxc", tiled, w_neck, preferred_element_type=jnp.float32
    ).astype(jnp.bfloat16)
    extent = neck_feats.shape[:3]
    channels = w_neck.shape[1]
    cell_count = extent[0] * extent[1] * extent[2]
    hidden_one = conv_apply(neck_feats, w_first, False)
    active_one = jax.nn.silu(hidden_one).astype(jnp.bfloat16)
    hidden_two = conv_apply(active_one.reshape(extent + (channels,)), w_second, False)
    active_two = jax.nn.silu(hidden_two).astype(jnp.bfloat16)
    logits = jnp.dot(active_two, w_class, preferred_element_type=jnp.float32)
    probability = jax.nn.sigmoid(logits)
    fault_mask = labels.reshape(cell_count).astype(jnp.float32)
    intersection, total_prob, total_fault = lax.psum(
        (jnp.sum(probability * fault_mask), jnp.sum(probability), jnp.sum(fault_mask)),
        ("heads", "tok"),
    )
    dice_denominator = total_prob + total_fault
    dice_loss = 1.0 - 2.0 * intersection / dice_denominator
    cells_all = float(cell_count * lax.axis_size("heads") * lax.axis_size("tok"))
    grad_logits = (
        LOSS_SCALE
        * cells_all
        * -2.0
        * (fault_mask * dice_denominator - intersection)
        / (dice_denominator * dice_denominator)
        * probability
        * (1.0 - probability)
    )
    grad_hidden_two = (
        grad_logits[:, None] * w_class.astype(jnp.float32)[None, :] * silu_slope(hidden_two)
    ).astype(jnp.bfloat16)
    grad_active_one = conv_apply(grad_hidden_two.reshape(extent + (channels,)), w_second, True)
    grad_hidden_one = (grad_active_one * silu_slope(hidden_one)).astype(jnp.bfloat16)
    grad_neck = (
        conv_apply(grad_hidden_one.reshape(extent + (channels,)), w_first, True)
        .astype(jnp.bfloat16)
        .reshape(extent + (channels,))
    )
    grad_tiles = jnp.einsum(
        "ztxc,dc->ztxd", grad_neck, w_neck, preferred_element_type=jnp.float32
    ).astype(jnp.bfloat16)
    grad_encoded = lax.all_to_all(grad_tiles, "tok", split_axis=1, concat_axis=2, tiled=True)
    return (encoded, dice_loss, grad_encoded)


def dot(a, b):
    return jnp.dot(a, b, preferred_element_type=F32)


def dot_t(a, b):
    return lax.dot_general(a, b, (((1,), (1,)), ((), ())), preferred_element_type=F32)


def sigma_of(v):
    return 1.0 / (1.0 + jnp.exp(-v))


def slope_of(v):
    s = sigma_of(v)
    return s * (1.0 + v * (1.0 - s))


def iota(shape, dim):
    return lax.broadcasted_iota(jnp.int32, shape, dim)


def along_inline(value, step, inline):
    if step == 0:
        return value
    rows = value.shape[0]
    x = iota(value.shape, 0) % inline
    edge = inline - 1 if step > 0 else 0
    return jnp.where(x == edge, 0.0, pltpu.roll(value, (-step) % rows, axis=0))


def along_rows(value, step):
    if step == 0:
        return value
    zeros = jnp.zeros((abs(step), value.shape[1]), value.dtype)
    if step > 0:
        return jnp.concatenate([value[step:], zeros], axis=0)
    return jnp.concatenate([zeros, value[:step]], axis=0)


def place_of(tok_n):
    h, t = lax.axis_index("heads"), lax.axis_index("tok")
    return h, t // 2, t % 2, t


def pack_kernel(tok_n, q_ref, k_ref, v_ref, r_ref, neck_ref, lab_ref, out_ref):
    h, _, _, t = place_of(tok_n)
    rows = q_ref.shape[1] * q_ref.shape[2]
    width = q_ref.shape[3]
    for i, ref in enumerate((q_ref, k_ref, v_ref)):
        flat = ref[...].astype(F32).reshape(rows, width).astype(BF16)
        out_ref[i * rows : (i + 1) * rows, :] = flat
    own = r_ref.shape[0] * r_ref.shape[2]
    residual = r_ref[...].astype(F32).reshape(own, r_ref.shape[3]).astype(BF16)
    out_ref[3 * rows : 3 * rows + own, :] = dot(residual, neck_ref[...]).astype(BF16)
    own_c, _, nt = lab_ref.shape
    spread = jnp.zeros((LABEL_ROWS, width), F32)
    for c in range(own_c):
        row = jnp.broadcast_to(lab_ref[c].astype(F32), (LABEL_ROWS, nt)).astype(BF16)
        at = (h * own_c + c) * nt + iota((nt, width), 0)
        spread = spread + dot(row, (iota((nt, width), 1) == at).astype(F32).astype(BF16))
    out_ref[3 * rows + own :, :] = jnp.where(
        iota((LABEL_ROWS, width), 0) == t, spread, 0.0
    ).astype(BF16)


def weights_kernel(first_ref, second_ref, out_ref, neck_ref, packed_ref, *refs):
    first_in, second_in, first_t, second_t, joint, again, out_w, neck_w = refs[:8]
    first_mid, second_mid, sems = refs[8:]
    small = [
        pltpu.make_async_copy(out_ref, out_w, sems.at[6]),
        pltpu.make_async_copy(neck_ref, neck_w, sems.at[7]),
    ]
    for copy in small:
        copy.start()
    sets = (
        (first_ref, first_in, first_mid, first_t),
        (second_ref, second_in, second_mid, second_t),
    )
    copies = []
    for i, (src, dst, mid, _) in enumerate(sets):
        for a, place in enumerate((dst.at[0], mid, dst.at[3])):
            copies.append(pltpu.make_async_copy(src.at[a], place, sems.at[3 * i + a]))
            copies[-1].start()
    again[...] = packed_ref[...]
    for copy in small:
        copy.wait()
    joint[...] = dot(out_w[...], neck_w[...]).astype(BF16)
    for i, (_, dst, mid, flipped) in enumerate(sets):
        for a in range(3):
            copies[3 * i + a].wait()
        for b in range(3):
            for e in range(3):
                taps = (dst[0, b, e], mid[b, e], dst[3, b, e])
                for a in range(3):
                    flipped[a, b, e] = taps[a].T
                g0, g1, g2 = (tap.astype(F32) * 0.5 for tap in taps)
                dst[1, b, e] = (g0 + g2 + g1).astype(BF16)
                dst[2, b, e] = (g0 + g2 - g1).astype(BF16)


def far_first(zs):
    return list(range(zs - 1, 2, -1)) + [1, 2, 0]


def attention_kernel(tok_n, zs, rows, own, *refs):
    order = far_first(zs)
    ours = [refs[order.index(d)] for d in range(zs)]
    theirs = [refs[zs + order.index(d)] for d in range(zs)]
    joint_w, sum_ref, own_ref = refs[2 * zs : 3 + 2 * zs]
    qq, kk, vv, part = refs[-4:]
    h, z, core, _ = place_of(tok_n)
    width = qq.shape[1]
    queries_n = qq.shape[0]
    labels = jnp.zeros((LABEL_ROWS, width), F32)
    for d in range(zs):
        qq[d * rows : (d + 1) * rows, :] = ours[d][0:rows, :]
        for ref, side in ((ours[d], core), (theirs[d], 1 - core)):
            at = pl.multiple_of((2 * (z ^ d) + side) * rows, rows)
            kk[pl.ds(at, rows), :] = ref[rows : 2 * rows, :]
            vv[pl.ds(at, rows), :] = ref[2 * rows : 3 * rows, :]
            labels = labels + ref[3 * rows + own :, :].astype(F32)
    heads_here = width // HD
    scale = HD ** (-0.5)
    query = qq[...]
    keys, values = kk[...], vv[...]
    lane_head = iota((queries_n, width), 1) // HD
    attended = jnp.zeros((queries_n, width), F32)
    for head in range(heads_here):
        mine = lane_head == head
        scores = dot_t(jnp.where(mine, query, jnp.zeros_like(query)), keys) * scale
        raw = jnp.exp(scores - jnp.max(scores, axis=1, keepdims=True))
        total = jnp.sum(raw, axis=1, keepdims=True)
        mixed = dot(raw.astype(BF16), values)
        attended = jnp.where(mine, mixed / total, attended)
    attended = attended.astype(BF16)
    part[...] = dot(attended, joint_w[...])
    for d in range(zs):
        at = pl.multiple_of(d * rows + h * own, own)
        part[pl.ds(at, own), :] += ours[d][3 * rows : 3 * rows + own, :].astype(F32)
    partial = part[...].astype(BF16)
    labels = labels.astype(BF16)
    own_ref[...] = attended[0:rows, :]
    sum_ref[0:queries_n, :] = partial
    sum_ref[queries_n:, :] = labels


def output_kernel(tok_n, attended, out_w, *enc_refs):
    h, _, _, _ = place_of(tok_n)
    first = dot(attended[...], out_w[...])
    own = enc_refs[0].shape[0]
    blocks = [first[i * own : (i + 1) * own, :] for i in range(first.shape[0] // own)]
    for d, ref in enumerate(enc_refs):
        picked = blocks[0]
        for i in range(1, len(blocks)):
            picked = jnp.where((h ^ d) == i, blocks[i], picked)
        ref[...] = picked.astype(BF16)


def decoder_kernel(sizes, *refs):
    nc, nt, ni, own_c, zs, tok_n, parts_n = sizes
    ours, theirs, w1, w2, w1_t, w2_t, class_w, neck_w = refs[:8]
    parts = refs[8 : 8 + parts_n]
    loss_ref, grad_ref, grid, cols, slope1, grad2, cols3, slope2, act, parts_out = refs[8 + parts_n :]
    channels = grid.shape[2]
    slab = nt * ni
    rows = nc * ni
    cells = nc * slab
    h, z, core, tslab = place_of(tok_n)
    taps = 9
    for d in range(zs):
        for ref, side in ((ours, core), (theirs, 1 - core)):
            block = ref[d * rows : (d + 1) * rows, :].astype(F32)
            at = pl.multiple_of((2 * (z ^ d) + side) * ni, ni)
            for c in range(nc):
                grid[c, pl.ds(at, ni), :] = block[c * ni : (c + 1) * ni, :]

    slope1[...] = jnp.zeros_like(slope1)
    grad2[...] = jnp.zeros_like(grad2)
    def spread(value, k, i):
        for e in range(3):
            moved = along_inline(value, e - 1, ni)
            for b in range(3):
                lane = (b * 3 + e) * channels
                cols[k, i * slab : (i + 1) * slab, lane : lane + channels] = along_rows(
                    moved, (b - 1) * ni
                ).astype(BF16)

    def spread_all(volume):
        empty = jnp.zeros((slab, channels), F32)
        for i in range(nc // 2):
            d0 = volume[2 * i - 1] if i > 0 else empty
            d1, d2 = volume[2 * i], volume[2 * i + 1]
            d3 = volume[2 * i + 2] if 2 * i + 2 < nc else empty
            for k, value in enumerate((d0 - d2, d1 + d2, d2 - d1, d1 - d3)):
                spread(value, k, i)

    half_cells = cells // 2

    def conv(weights, finish):
        for m in range(0, half_cells, TILE):
            for k in range(4):
                matrix = weights[k].reshape(taps * channels, channels)
                parts_out[k, m : m + TILE, :] = dot(cols[k, m : m + TILE, :], matrix)
            for i in range(m // slab, (m + TILE) // slab):
                m0, m1, m2, m3 = (parts_out[k, i * slab : (i + 1) * slab, :] for k in range(4))
                finish(2 * i, m0 + m1 + m2)
                finish(2 * i + 1, m1 - m2 - m3)

    class_row = class_w[...].astype(F32).reshape(1, channels)

    def finish_one(c, v):
        s = sigma_of(v)
        slope1[c + 1, ni : ni + slab, :] = s * (1.0 + v * (1.0 - s))
        grid[c] = (v * s).astype(BF16).astype(F32)

    def finish_two(c, v):
        s = sigma_of(v)
        slope2[c * slab : (c + 1) * slab, :] = s * (1.0 + v * (1.0 - s)) * class_row
        act[c * slab : (c + 1) * slab, :] = (v * s).astype(BF16)

    spread_all([grid[c] for c in range(nc)])
    conv(w1, finish_one)
    spread_all([grid[c] for c in range(nc)])
    conv(w2, finish_two)
    active_two = act[...]
    logits = dot_t(active_two, jnp.broadcast_to(class_row, (128, channels)).astype(BF16))
    probability = sigma_of(logits)
    last = parts[0].shape[0] - LABEL_ROWS
    lab = pairwise([ref[last : last + ni, 0:128].astype(F32) for ref in parts])
    spread_lab = jnp.broadcast_to(lab[None], (cells // ni, ni, 128)).reshape(cells, 128)
    wanted = iota((cells, 128), 0) // ni
    picked = jnp.where(iota((cells, 128), 1) == wanted, spread_lab, 0.0).astype(BF16)
    mask = dot(picked, jnp.ones((128, 128), BF16))
    intersection = jnp.sum(probability * mask, axis=0, keepdims=True)
    total_prob = jnp.sum(probability, axis=0, keepdims=True)
    total_fault = jnp.sum(mask, axis=0, keepdims=True)
    denominator = total_prob + total_fault
    loss_ref[...] = 1.0 - 2.0 * intersection / denominator
    grad_logits = (
        LOSS_SCALE
        * float(cells)
        * -2.0
        * (mask * denominator - intersection)
        / (denominator * denominator)
        * probability
        * (1.0 - probability)
    )
    for c in range(nc):
        rows_c = slice(c * slab, (c + 1) * slab)
        wide = jnp.concatenate([grad_logits[rows_c, :]] * (channels // 128), axis=1)
        grad2[c + 2, 2 * ni : 2 * ni + slab, :] = wide * slope2[rows_c, :]

    band = 4 * ni
    c0 = h * own_c
    t0 = pl.multiple_of(tslab * ni, ni)
    for i in range(own_c + 4):
        region = grad2[c0 + i, pl.ds(t0, band + 2 * ni), :]
        for e in range(3):
            moved = along_inline(region, 1 - e, ni)
            for b in range(3):
                lane = (b * 3 + e) * channels
                cols3[i * band : (i + 1) * band, lane : lane + channels] = moved[
                    (2 - b) * ni : (2 - b) * ni + band, :
                ].astype(BF16)
    out3 = (own_c + 2) * band
    total = jnp.zeros((out3, channels), F32)
    for a in range(3):
        for b in range(3):
            for e in range(3):
                lane = (b * 3 + e) * channels
                piece = cols3[(2 - a) * band : (2 - a) * band + out3, lane : lane + channels]
                total = total + dot(piece, w2_t[a, b, e])
    slopes = [slope1[c0 + i, pl.ds(t0, band), :] for i in range(own_c + 2)]
    g1 = (total * jnp.concatenate(slopes, axis=0)).astype(BF16).astype(F32)
    shifted = [along_inline(g1, 1 - e, ni) for e in range(3)]
    total = jnp.zeros((own_c * ni, channels), F32)
    for a in range(3):
        pieces = []
        for b in range(3):
            for e in range(3):
                cells_in = [
                    shifted[e][(i + 2 - a) * band + (2 - b) * ni : (i + 2 - a) * band + (3 - b) * ni, :]
                    for i in range(own_c)
                ]
                pieces.append(jnp.concatenate(cells_in, axis=0).astype(BF16))
        matrix = w1_t[a].reshape(taps * channels, channels)
        total = total + dot(jnp.concatenate(pieces, axis=1), matrix)
    grad = dot_t(total.astype(BF16), neck_w[...])
    grad_ref[...] = grad.reshape(grad_ref.shape).astype(BF16)


def pairwise(values):
    while len(values) > 1:
        values = [values[i] + values[i + 1] for i in range(0, len(values), 2)]
    return values[0]


def vmem():
    return pl.BlockSpec(memory_space=pltpu.VMEM)


def hbm():
    return pl.BlockSpec(memory_space=pltpu.HBM)


def whole_grid(
    queries, key_rows, value_rows, residual, w_out, w_neck, w_first, w_second, w_class, labels
):
    heads_n, tok_n = lax.axis_size("heads"), lax.axis_size("tok")
    zs = tok_n // 2
    _, nc, ni, width = queries.shape
    own_c = residual.shape[0]
    nt = labels.shape[1]
    channels = w_neck.shape[1]
    rows, own = nc * ni, own_c * ni

    def swap_tok(value, bits):
        return lax.ppermute(value, "tok", [(i, i ^ bits) for i in range(tok_n)])

    def swap_heads(value, bits):
        return lax.ppermute(value, "heads", [(i, i ^ bits) for i in range(heads_n)])

    packed = pl.pallas_call(
        functools.partial(pack_kernel, tok_n),
        out_shape=pltpu.VMEM((3 * rows + own + LABEL_ROWS, width), BF16),
        in_specs=[vmem()] * 6,
        out_specs=vmem(),
    )(queries, key_rows, value_rows, residual, w_neck, labels.transpose(0, 2, 1))
    ours = [packed] + [swap_tok(packed, 2 * d) for d in range(1, zs)]
    kept = [pltpu.with_memory_space_constraint(w, pltpu.HBM) for w in (w_first, w_second, w_out, w_neck)]
    first_in, second_in, first_t, second_t, joint, again, out_w, neck_w = pl.pallas_call(
        weights_kernel,
        out_shape=[pltpu.VMEM((4,) + w_first.shape[1:], BF16)] * 2
        + [pltpu.VMEM(w_first.shape, BF16)] * 2
        + [
            pltpu.VMEM((width, channels), BF16),
            pltpu.VMEM(packed.shape, BF16),
            pltpu.VMEM(w_out.shape, BF16),
            pltpu.VMEM(w_neck.shape, BF16),
        ],
        in_specs=[hbm()] * 4 + [vmem()],
        out_specs=[vmem()] * 8,
        scratch_shapes=[pltpu.VMEM(w_first.shape[1:], BF16)] * 2 + [pltpu.SemaphoreType.DMA((8,))],
        compiler_params=pltpu.CompilerParams(vmem_limit_bytes=24 * 2**20),
        cost_estimate=pl.CostEstimate(flops=0, bytes_accessed=28 * 2**20, transcendentals=0),
    )(*kept, packed)
    theirs = [swap_tok(value, 1) for value in [again] + ours[1:]]
    order = far_first(zs)
    queries_n, keys_n = rows * zs, rows * tok_n
    part_shape = pltpu.VMEM((queries_n + LABEL_ROWS, channels), BF16)
    enc_shape = pltpu.VMEM((own, residual.shape[3]), BF16)
    message, attended = pl.pallas_call(
        functools.partial(attention_kernel, tok_n, zs, rows, own),
        out_shape=[part_shape, pltpu.VMEM((rows, width), BF16)],
        in_specs=[vmem()] * (2 * zs + 1),
        out_specs=[vmem()] * 2,
        scratch_shapes=[
            pltpu.VMEM((queries_n, width), BF16),
            pltpu.VMEM((keys_n, width), BF16),
            pltpu.VMEM((keys_n, width), BF16),
            pltpu.VMEM((queries_n, channels), F32),
        ],
        compiler_params=pltpu.CompilerParams(vmem_limit_bytes=16 * 2**20),
    )(*[ours[d] for d in order], *[theirs[d] for d in order], joint)
    parts = [message] + [swap_heads(message, d) for d in range(1, heads_n)]
    sent = pl.pallas_call(
        functools.partial(output_kernel, tok_n),
        out_shape=[enc_shape] * heads_n,
        in_specs=[vmem()] * 2,
        out_specs=[vmem()] * heads_n,
        compiler_params=pltpu.CompilerParams(vmem_limit_bytes=16 * 2**20),
    )(attended, out_w)
    half = pairwise([part[:queries_n].astype(F32) for part in parts]).astype(BF16)
    other = swap_tok(half, 1)
    slab = nt * ni
    loss, grad = (
        pl.pallas_call(
            functools.partial(decoder_kernel, (nc, nt, ni, own_c, zs, tok_n, heads_n)),
            out_shape=[
                jax.ShapeDtypeStruct((1, 128), F32),
                jax.ShapeDtypeStruct(residual.shape, BF16),
            ],
            in_specs=[vmem()] * (8 + heads_n),
            out_specs=[vmem()] * 2,
            scratch_shapes=[
                pltpu.VMEM((nc, slab, channels), F32),
                pltpu.VMEM((4, nc // 2 * slab, 9 * channels), BF16),
                pltpu.VMEM((nc + 2, (nt + 4) * ni, channels), F32),
                pltpu.VMEM((nc + 4, (nt + 6) * ni, channels), F32),
                pltpu.VMEM(((own_c + 4) * 4 * ni, 9 * channels), BF16),
                pltpu.VMEM((nc * slab, channels), F32),
                pltpu.VMEM((nc * slab, channels), BF16),
                pltpu.VMEM((4, nc // 2 * slab, channels), F32),
            ],
            compiler_params=pltpu.CompilerParams(vmem_limit_bytes=36 * 2**20),
        )(half, other, first_in, second_in, first_t, second_t, w_class, neck_w, *parts)
    )
    pieces = [sent[0]] + [swap_heads(sent[d], d) for d in range(1, heads_n)]
    total = pairwise([piece.astype(F32) for piece in pieces]).reshape(residual.shape)
    encoded = (residual.astype(F32) + total).astype(BF16)
    return (encoded, loss, grad)


def power_of_two(n):
    return n > 0 and n & (n - 1) == 0


def fits_whole(queries, residual, w_neck, labels):
    heads_n, tok_n = lax.axis_size("heads"), lax.axis_size("tok")
    slabs, nc, ni, width = queries.shape
    nt = labels.shape[1]
    return (
        slabs == 1
        and nc * nt <= 128
        and labels.shape[2] == 1
        and ni == LABEL_ROWS
        and nt == tok_n
        and tok_n >= 8
        and power_of_two(tok_n)
        and power_of_two(heads_n)
        and residual.shape[0] * heads_n == nc
        and nc * nt * ni <= 1024
        and (nc // 2 * nt * ni) % TILE == 0
        and nc % 2 == 0
        and width % 128 == 0
        and w_neck.shape[1] == width
        and (residual.shape[0] * ni) % 16 == 0
    )


def on_device(*arguments):
    queries, residual, w_neck, labels = (arguments[i] for i in (0, 3, 5, 9))
    if fits_whole(queries, residual, w_neck, labels):
        encoded, loss, grad = whole_grid(*arguments)
        return (encoded, loss[0, 0], grad)
    return on_tiles(*arguments)


def solution(mesh):
    placed = (
        P("tok", None, None, "heads"),
        P("tok", None, None, "heads"),
        P("tok", None, None, "heads"),
        P("heads", "tok", None, None),
        P("heads", None),
        P(),
        P(),
        P(),
        P(),
        P("heads", None, "tok"),
    )
    return jax.shard_map(
        on_device,
        mesh=mesh,
        in_specs=placed,
        out_specs=(P("heads", "tok", None, None), P(), P("heads", "tok", None, None)),
        check_vma=False,
    )
```
